32 devices in a mesh: dp: 2 (over x), tp: 4 (over z), sec: 4 (over y, core).
Axes of the slice: x: 2, y: 2, z: 4, core: 2. Of those that a mesh axis runs over, the one named last changes fastest.
Arguments:
- hidden_states: bfloat16 [4, 128, 8192], P(None, ('dp', 'sec')), may hold values from -6 to 6
- w_query: bfloat16 [8192, 8192], P(('dp', 'sec'), 'tp'), may hold values from -0.0625 to 0.0625
- w_keyval: bfloat16 [8192, 2048], P(('dp', 'sec'), 'tp'), may hold values from -0.0625 to 0.0625
- key_cache: bfloat16 [128, 16, 256, 128], P(('dp', 'sec'), 'tp'), may hold values from -200 to 200, as said below
- value_cache: bfloat16 [128, 16, 256, 128], P(('dp', 'sec'), 'tp'), may hold values from -6 to 6
- cache_begin: int32 [128], P(('dp', 'sec')), may hold values from 0 to 128
- cache_end: int32 [128], P(('dp', 'sec')), may hold values from 256 to 512
Outputs:
- handoff: bfloat16 [4, 128, 8192], P(None, 'dp', ('tp', 'sec'))
The draws below stay inside these ranges and needn't reach their ends.
Inputs may be any that keep to these rules, and one draw needn't show every extreme that they name: `key_cache`: cached keys; largest magnitudes differ between draws.
All inputs are finite; a program needn't handle non-finite values.
Results may differ from the reference program's by a relative error of at most 0.04.
Values may be sent and summed in bfloat16 or wider, within the bound.
A program may use at most 64 MiB of HBM per device.

```python
import jax
import jax.numpy as jnp
from jax import lax

D = 8192
H = 64
KVH = 8
HD = 128
STEPS = 4
CACHE = 512
ROLLOUTS = 128


def draw_key_cache(key, part):
    base = jax.random.normal(key, (ROLLOUTS, 2 * KVH, CACHE // 2, HD), jnp.float32)
    return jnp.clip(base, -200.0, 200.0).astype(jnp.bfloat16)


def cache_bounds(key):
    begin = jax.random.randint(jax.random.fold_in(key, 11), (ROLLOUTS,), 0, CACHE // 4 + 1)
    finish = jax.random.randint(jax.random.fold_in(key, 12), (ROLLOUTS,), CACHE // 2, CACHE + 1)
    begin = begin.at[0].set(0).at[1].set(CACHE // 4)
    finish = finish.at[0].set(CACHE).at[1].set(CACHE // 2)
    return (begin.astype(jnp.int32), finish.astype(jnp.int32))


def draw_cache_begin(key, part):
    return cache_bounds(key)[0]


def draw_cache_end(key, part):
    return cache_bounds(key)[1]


def shard_levels(own_key, dims, shards, low, largest):
    def one(dim, blocks):
        steps = jax.random.uniform(jax.random.fold_in(jax.random.fold_in(own_key, 6), dim), (blocks,), jnp.float32, low / len(shards), largest / len(shards))
        return jnp.repeat(jnp.exp(steps), dims[dim] // blocks).reshape((-1,) + (1,) * (len(dims) - dim - 1))

    gain = one(*shards[0])
    for cut in shards[1:]:
        gain = gain * one(*cut)
    return gain


def noise(own_key, shape, deviation, most, cuts=(), held_as=jnp.bfloat16):
    drawn = jax.random.normal(own_key, shape, jnp.float32) * deviation
    if len(cuts) > 0:
        drawn = shard_levels(own_key, shape, cuts, -0.22, 0.18) * drawn
    return jnp.clip(drawn, min=-most, max=most).astype(held_as)


def setup_inputs(seed: int = 0) -> dict:
    key_list = jax.random.split(jax.random.key(seed), 8)
    return {
        "hidden_states": noise(key_list[0], (STEPS, ROLLOUTS, D), 1.0, 6.0, ((1, 8),)),
        "w_query": noise(key_list[1], (D, H * HD), D ** -0.5, 0.0625, ((0, 8), (1, 4))),
        "w_keyval": noise(key_list[2], (D, 2 * KVH * HD), D ** -0.5, 0.0625, ((0, 8), (1, 4))),
        "key_cache": draw_key_cache(jax.random.fold_in(key_list[7], 71), 0),
        "value_cache": noise(key_list[4], (ROLLOUTS, 2 * KVH, CACHE // 2, HD), 1.0, 6.0, ((0, 8), (1, 4))),
        "cache_begin": draw_cache_begin(jax.random.fold_in(key_list[7], 71), 0),
        "cache_end": draw_cache_end(jax.random.fold_in(key_list[7], 71), 0),
    }


THETA = 500000.0


def rotate(vector, positions):
    half = vector.shape[-1] // 2
    freq = THETA ** (-(jnp.arange(half, dtype=jnp.float32) * 2.0 / vector.shape[-1]))
    angle = positions[..., None] * freq
    angle = angle.reshape(positions.shape + (1,) * (vector.ndim - positions.ndim - 1) + (half,))
    cosine = jnp.cos(angle)
    sine = jnp.sin(angle)
    first = vector[..., :half]
    second = vector[..., half:]
    return jnp.concatenate([first * cosine - second * sine, second * cosine + first * sine], axis=-1)


def reference(hidden_states, w_query, w_keyval, key_cache, value_cache, cache_begin, cache_end):
    token_rows = hidden_states.reshape(STEPS * ROLLOUTS, D)
    positions = cache_end.astype(jnp.float32)[None, :] + jnp.arange(STEPS, dtype=jnp.float32)[:, None]
    query = jnp.dot(token_rows, w_query, preferred_element_type=jnp.float32).reshape(STEPS, ROLLOUTS, H, HD)
    query = rotate(query, positions).astype(jnp.bfloat16)
    keyval = jnp.dot(token_rows, w_keyval, preferred_element_type=jnp.float32).reshape(STEPS, ROLLOUTS, KVH, 2, HD)
    new_keys = rotate(keyval[:, :, :, 0], positions).astype(jnp.bfloat16)
    new_values = keyval[:, :, :, 1].astype(jnp.bfloat16)
    all_keys = key_cache.reshape(ROLLOUTS, KVH, CACHE, HD)
    all_values = value_cache.reshape(ROLLOUTS, KVH, CACHE, HD)
    group_size = H // KVH
    score_scale = HD ** -0.5
    cache_pos = jnp.arange(CACHE, dtype=jnp.int32)
    step_ids = jnp.arange(STEPS, dtype=jnp.int32)
    causal = step_ids[None, :] <= step_ids[:, None]

    def one_rollout(inputs):
        q_roll, k_roll, v_roll, nk_roll, nv_roll, begin, end = inputs
        q_float = q_roll.astype(jnp.float32).reshape(STEPS, KVH, group_size, HD)
        cache_scores = jnp.einsum('skgd,kpd->skgp', q_float, k_roll.astype(jnp.float32)) * score_scale
        new_scores = jnp.einsum('skgd,tkd->skgt', q_float, nk_roll.astype(jnp.float32)) * score_scale
        cache_live = (cache_pos >= begin) & (cache_pos < end)
        live = jnp.concatenate([
            jnp.broadcast_to(cache_live[None, None, None, :], cache_scores.shape),
            jnp.broadcast_to(causal[:, None, None, :], new_scores.shape)], axis=-1)
        scores = jnp.concatenate([cache_scores, new_scores], axis=-1)
        masked = jnp.where(live, scores, jnp.float32(-1e30))
        peak = jnp.max(masked, axis=-1, keepdims=True)
        expo = jnp.where(live, jnp.exp(masked - peak), jnp.float32(0.0))
        totals = jnp.sum(expo, axis=-1)
        probs = lax.optimization_barrier(expo.astype(jnp.bfloat16)).astype(jnp.float32)
        values = jnp.concatenate([v_roll.astype(jnp.float32), jnp.transpose(nv_roll.astype(jnp.float32), (1, 0, 2))], axis=1)
        weighted = jnp.einsum('skgp,kpd->skgd', probs, values) / totals[..., None]
        return weighted.astype(jnp.bfloat16).reshape(STEPS, H * HD)

    result = lax.map(one_rollout, (
        jnp.transpose(query, (1, 0, 2, 3)), all_keys, all_values,
        jnp.transpose(new_keys, (1, 0, 2, 3)), jnp.transpose(new_values, (1, 0, 2, 3)),
        cache_begin, cache_end))
    return jnp.transpose(result, (1, 0, 2))
```

```python
import functools

import jax
import jax.numpy as jnp
import numpy as np
from jax import lax
from jax.experimental import pallas as pl
from jax.experimental.pallas import tpu as pltpu
from jax.sharding import PartitionSpec as P

THETA = 500000.0


def swapped(value, axis, stride):
    mask = 2**stride
    pairs = [(source, source ^ mask) for source in range(lax.axis_size(axis))]
    return lax.ppermute(value, axis, pairs)


def rotate(vector, positions):
    half = vector.shape[-1] // 2
    freq = THETA ** (-(jnp.arange(half, dtype=jnp.float32) * 2.0 / vector.shape[-1]))
    angle = positions[..., None] * freq
    angle = angle.reshape(positions.shape + (1,) * (vector.ndim - positions.ndim - 1) + (half,))
    cosine = jnp.cos(angle)
    sine = jnp.sin(angle)
    first = vector[..., :half]
    second = vector[..., half:]
    return jnp.concatenate(
        [first * cosine - second * sine, second * cosine + first * sine], axis=-1
    )


def make_accumulate(token_rows, pieces):
    return (
        jnp.dot(token_rows, pieces[0], preferred_element_type=jnp.float32),
        jnp.dot(token_rows, pieces[1], preferred_element_type=jnp.float32),
    )


def partial_attention(query, keys, values, live, score_scale):
    scores = (
        jnp.einsum("sbkgd,bkpd->sbkgp", query, keys, preferred_element_type=jnp.float32)
        * score_scale
    )
    live = jnp.broadcast_to(live, scores.shape)
    masked = jnp.where(live, scores, jnp.float32(-1e30))
    maxima = jnp.max(masked, axis=-1)
    expo = jnp.where(live, jnp.exp(masked - maxima[..., None]), jnp.float32(0.0))
    totals = jnp.sum(expo, axis=-1)
    weighted = jnp.einsum(
        "sbkgp,bkpd->sbkgd", expo.astype(jnp.bfloat16), values, preferred_element_type=jnp.float32
    )
    return (maxima, totals, weighted)


def merge_parts(parts):
    overall = parts[0][0]
    for entry in parts[1:]:
        overall = jnp.maximum(overall, entry[0])
    weighted = jnp.zeros_like(parts[0][2])
    totals = jnp.zeros_like(parts[0][1])
    for entry in parts:
        factor = jnp.exp(entry[0] - overall)
        weighted = weighted + entry[2] * factor[..., None]
        totals = totals + entry[1] * factor
    return weighted / totals[..., None]


def general_body(hidden_states, w_query, w_keyval, key_cache, value_cache, cache_begin, cache_end):
    num_steps, batch_rows, width = hidden_states.shape
    head_size = key_cache.shape[-1]
    query_cols = w_query.shape[1]
    keyval_cols = w_keyval.shape[1]
    local_heads = query_cols // head_size
    slot_count = key_cache.shape[1]
    half_len = key_cache.shape[2]
    score_scale = head_size ** (-0.5)
    sec_count = lax.axis_size("sec")
    sec_index = lax.axis_index("sec")
    sec_group = lax.all_gather(hidden_states, "sec", axis=1, tiled=True)
    shard_rows = w_query.shape[0]
    dp_count = width // (sec_count * shard_rows)
    group_rows = num_steps * batch_rows * sec_count
    grouped = sec_group.reshape(group_rows, dp_count, sec_count, shard_rows)
    chosen = lax.dynamic_slice_in_dim(grouped, sec_index, 1, 2).reshape(
        group_rows, dp_count * shard_rows
    )
    query_all, keyval_all = make_accumulate(
        chosen,
        (
            lax.all_gather(w_query, "dp", axis=0, tiled=True),
            lax.all_gather(w_keyval, "dp", axis=0, tiled=True),
        ),
    )
    query_acc, keyval_acc = (
        lax.psum_scatter(
            query_all.reshape(num_steps, sec_count * batch_rows, query_cols),
            "sec",
            scatter_dimension=1,
            tiled=True,
        ),
        lax.psum_scatter(
            keyval_all.reshape(num_steps, sec_count * batch_rows, keyval_cols),
            "sec",
            scatter_dimension=1,
            tiled=True,
        ),
    )
    query_acc = query_acc.reshape(num_steps * batch_rows, query_cols)
    keyval_acc = keyval_acc.reshape(num_steps * batch_rows, keyval_cols)
    positions = (
        cache_end.astype(jnp.float32)[None, :] + jnp.arange(num_steps, dtype=jnp.float32)[:, None]
    )
    query = rotate(
        query_acc.reshape(num_steps, batch_rows, local_heads, head_size), positions
    ).astype(jnp.bfloat16)
    step_ids = jnp.arange(num_steps, dtype=jnp.int32)
    causal = step_ids[None, :] <= step_ids[:, None]
    if slot_count == 1:
        parity = lax.axis_index("tp") % 2
        own_proj = keyval_acc.reshape(num_steps, batch_rows, head_size)
        own_proj = jnp.where(parity == 0, rotate(own_proj, positions), own_proj).astype(
            jnp.bfloat16
        )
        partner_query, partner_proj = swapped((query, own_proj), "tp", 0)
        new_keys = jnp.where(parity == 0, own_proj, partner_proj)
        new_values = jnp.where(parity == 0, partner_proj, own_proj)
        lower_heads = jnp.where(parity == 0, query, partner_query)
        upper_heads = jnp.where(parity == 0, partner_query, query)
        both_heads = jnp.concatenate([lower_heads, upper_heads], axis=2)[:, :, None]
        cache_pos = parity * half_len + jnp.arange(half_len, dtype=jnp.int32)
        cache_live = (cache_pos[None, :] >= cache_begin[:, None]) & (
            cache_pos[None, :] < cache_end[:, None]
        )
        cache_part = partial_attention(
            both_heads, key_cache, value_cache, cache_live[None, :, None, None, :], score_scale
        )
        mine_start = parity * local_heads
        theirs_start = (1 - parity) * local_heads

        def select_heads(array, start):
            return lax.dynamic_slice_in_dim(array, start, local_heads, 3)

        returned = (
            swapped(select_heads(cache_part[0], theirs_start).astype(jnp.bfloat16), "tp", 0).astype(
                jnp.float32
            ),
            swapped(select_heads(cache_part[1], theirs_start).astype(jnp.bfloat16), "tp", 0).astype(
                jnp.float32
            ),
            swapped(select_heads(cache_part[2], theirs_start).astype(jnp.bfloat16), "tp", 0).astype(
                jnp.float32
            ),
        )
        own_part = (
            select_heads(cache_part[0], mine_start),
            select_heads(cache_part[1], mine_start),
            select_heads(cache_part[2], mine_start),
        )
        fresh_part = partial_attention(
            query[:, :, None],
            jnp.transpose(new_keys, (1, 0, 2))[:, None],
            jnp.transpose(new_values, (1, 0, 2))[:, None],
            causal[:, None, None, None, :],
            score_scale,
        )
        parts = [own_part, returned, fresh_part]
    else:
        local_kv = keyval_cols // (2 * head_size)
        keyval = keyval_acc.reshape(num_steps, batch_rows, local_kv, 2, head_size)
        new_keys = rotate(keyval[:, :, :, 0], positions).astype(jnp.bfloat16)
        new_values = keyval[:, :, :, 1].astype(jnp.bfloat16)
        whole_keys = key_cache.reshape(batch_rows, local_kv, 2 * half_len, head_size)
        whole_values = value_cache.reshape(batch_rows, local_kv, 2 * half_len, head_size)
        grouped_query = query.reshape(
            num_steps, batch_rows, local_kv, local_heads // local_kv, head_size
        )
        cache_pos = jnp.arange(2 * half_len, dtype=jnp.int32)
        cache_live = (cache_pos[None, :] >= cache_begin[:, None]) & (
            cache_pos[None, :] < cache_end[:, None]
        )
        cache_part = partial_attention(
            grouped_query, whole_keys, whole_values, cache_live[None, :, None, None, :], score_scale
        )
        fresh_part = partial_attention(
            grouped_query,
            jnp.transpose(new_keys, (1, 2, 0, 3)),
            jnp.transpose(new_values, (1, 2, 0, 3)),
            causal[:, None, None, None, :],
            score_scale,
        )
        parts = [cache_part, fresh_part]
    attended = (
        merge_parts(parts)
        .astype(jnp.bfloat16)
        .reshape(num_steps, batch_rows, local_heads * head_size)
    )
    return lax.all_to_all(attended, "sec", split_axis=2, concat_axis=1, tiled=True)


def fused_kernel(
    group, freq_ref, begin_ref, end_ref, hidden_ref, wq_ref, wkv_ref, key_ref, value_ref, out_ref,
    xbuf, wbuf, pbuf, rbuf, kbuf, vbuf, cosine, sine, qbuf, fresh, obuf, abuf,
    x_local, x_send, x_recv, w_local, w_send, w_recv, kv_sem, r_send, r_recv, o_local, o_send, o_recv,
):
    chunks = wkv_ref.shape[1] // (2 * key_ref.shape[3])
    steps, batch, _ = hidden_ref.shape
    size = key_ref.shape[3]
    depth = wq_ref.shape[0]
    span = 2 * depth
    rows = steps * batch
    half_len = key_ref.shape[2]
    blocks = (group + 2) // 2
    wide = blocks * size
    dp, sec = lax.axis_index("dp"), lax.axis_index("sec")
    core = sec % 2
    dp_other = 1 - dp
    sec_far = (sec + 2) % 4
    sec_pair = sec + 1 - 2 * core
    near = ({"dp": dp, "sec": sec}, {"dp": dp_other, "sec": sec}, {"dp": dp, "sec": sec_far}, {"dp": dp_other, "sec": sec_far})
    pair = {"dp": dp, "sec": sec_pair}
    cross = {"dp": dp, "sec": (sec_pair + 2) % 4}
    chips = (dp * 2 + sec // 2, dp_other * 2 + sec // 2, dp * 2 + sec_far // 2, dp_other * 2 + sec_far // 2)

    def weight_parts(chunk):
        first = chunk * group * size
        return (
            (2 * chunk, 0, wide, wq_ref, first),
            (2 * chunk + 1, 0, group * size - wide, wq_ref, first + wide),
            (2 * chunk + 1, group * size - wide, 2 * size, wkv_ref, chunk * 2 * size),
        )

    own_rows = pl.ds(pl.multiple_of(core * depth, depth), depth)

    def weight_refs(part):
        piece, start, width, source, column = part
        return (
            source.at[:, pl.ds(column, width)],
            wbuf.at[piece, own_rows, pl.ds(start, width)],
        )

    def hidden_slice(relation):
        return hidden_ref.at[:, :, pl.ds(pl.multiple_of(chips[relation] * span, span), span)]

    local_copies = {}
    x_own = pltpu.make_async_copy(hidden_slice(0), xbuf.at[0], x_local)
    x_own.start()
    for chunk in range(chunks):
        for index, part in enumerate(weight_parts(chunk)):
            source, target = weight_refs(part)
            copy = pltpu.make_async_copy(source, target, w_local.at[chunk, index])
            copy.start()
            local_copies[chunk, index] = copy

    barrier = pltpu.get_barrier_semaphore()
    for peer in near[1:] + (pair, cross):
        pl.semaphore_signal(barrier, inc=1, device_id=peer, device_id_type=pl.DeviceIdType.MESH)
    pl.semaphore_wait(barrier, 5)

    x_copies = []
    for relation in (3, 1, 2):
        copy = pltpu.make_async_remote_copy(
            src_ref=hidden_slice(relation), dst_ref=xbuf.at[relation],
            send_sem=x_send.at[relation - 1], recv_sem=x_recv.at[relation - 1],
            device_id=near[relation], device_id_type=pl.DeviceIdType.MESH,
        )
        copy.start()
        x_copies.append(copy)
    w_copies = {}
    for chunk in range(chunks):
        for index, part in enumerate(weight_parts(chunk)):
            source, target = weight_refs(part)
            copy = pltpu.make_async_remote_copy(
                src_ref=source, dst_ref=target,
                send_sem=w_send.at[chunk, index], recv_sem=w_recv.at[chunk, index],
                device_id=pair, device_id_type=pl.DeviceIdType.MESH,
            )
            copy.start()
            w_copies[chunk, index] = copy
    kv_copies = []
    for chunk in range(chunks):
        slots = pl.ds(2 * chunk, 2)
        for index, (source, target) in enumerate(((key_ref, kbuf), (value_ref, vbuf))):
            copy = pltpu.make_async_copy(source.at[:, slots], target.at[chunk], kv_sem.at[chunk, index])
            copy.start()
            kv_copies.append(copy)

    row = lax.broadcasted_iota(jnp.int32, (rows, size), 0)
    lane = lax.broadcasted_iota(jnp.int32, (rows, size), 1)
    place = row // batch
    for index in range(batch):
        place = place + jnp.where(row % batch == index, end_ref[index], 0)
    angle = place.astype(jnp.float32) * freq_ref[...]
    cosine[...] = jnp.cos(angle)
    sine[...] = jnp.where(lane < size // 2, -jnp.sin(angle), jnp.sin(angle))

    def rotated(vector):
        return vector * cosine[...] + pltpu.roll(vector, size // 2, 1) * sine[...]

    def send(piece, message, source, target):
        copy = pltpu.make_async_remote_copy(
            src_ref=source, dst_ref=rbuf.at[piece, message],
            send_sem=r_send.at[piece, message], recv_sem=r_recv.at[piece, message],
            device_id=target, device_id_type=pl.DeviceIdType.MESH,
        )
        copy.start()
        return copy

    tile = 512 if span % 512 == 0 else span

    def multiply(piece):
        for step in range(span // tile):
            deep = pl.ds(step * tile, tile)
            part = jnp.dot(
                xbuf[:, :, :, deep].reshape(4 * rows, tile), wbuf[piece, deep, :],
                preferred_element_type=jnp.float32,
            ).reshape(4, rows, wide)
            if step == 0:
                pbuf[piece] = part
            else:
                pbuf[piece] += part

    messages = {}

    def first_hop(piece):
        one = 1 if piece % 2 == 0 else 2
        messages[piece, 0] = send(piece, 0, pbuf.at[piece, 3], near[one])
        messages[piece, 1] = send(piece, 1, pbuf.at[piece, one], near[one])

    def second_hop(piece):
        two = 2 if piece % 2 == 0 else 1
        messages[piece, 0].wait_recv()
        pbuf[piece, two] += rbuf[piece, 0]
        messages[piece, 2] = send(piece, 2, pbuf.at[piece, two], near[two])

    x_own.wait()
    for copy in x_copies:
        copy.wait_recv()
    for chunk in range(chunks):
        for half in range(2):
            for index in ((0,), (1, 2))[half]:
                local_copies[chunk, index].wait()
                w_copies[chunk, index].wait_recv()
            multiply(2 * chunk + half)
            if chunk == 0:
                first_hop(half)

    def attend(chunk):
        new = [None, None]
        for half in range(2):
            piece = 2 * chunk + half
            messages[piece, 1].wait_recv()
            messages[piece, 2].wait_recv()
            for block in range(blocks):
                cols = pl.ds(block * size, size)
                total = pbuf[piece, 0, :, cols] + rbuf[piece, 1, :, cols] + rbuf[piece, 2, :, cols]
                head = half * blocks + block
                if head == group + 1:
                    new[1] = total.astype(jnp.bfloat16)
                elif head == group:
                    new[0] = rotated(total).astype(jnp.bfloat16)
                else:
                    turned = rotated(total).astype(jnp.bfloat16).astype(jnp.float32)
                    for step in range(steps):
                        qbuf[pl.ds(head * steps + step, batch, stride=group * steps), :] = turned[
                            step * batch : (step + 1) * batch
                        ]
        new_keys, new_values = new
        lines = group * steps
        scale = size ** (-0.5)
        query = qbuf[...].astype(jnp.bfloat16)
        contract = (((1,), (1,)), ((), ()))
        scores = lax.dot_general(query, new_keys, contract, preferred_element_type=jnp.float32) * scale
        line = lax.broadcasted_iota(jnp.int32, scores.shape, 0)
        other = lax.broadcasted_iota(jnp.int32, scores.shape, 1)
        live = (line // lines == other % batch) & (other // batch <= line % steps)
        fresh[...] = jnp.where(live, scores, jnp.float32(-1e30))
        kv_copies[2 * chunk].wait()
        kv_copies[2 * chunk + 1].wait()
        cache_len = 2 * half_len

        def one(index):
            here = pl.ds(pl.multiple_of(index * lines, lines), lines)
            keys = kbuf[chunk, index].reshape(cache_len, size)
            values = vbuf[chunk, index].reshape(cache_len, size)
            position = lax.broadcasted_iota(jnp.int32, (lines, cache_len), 1)
            cached = lax.dot_general(
                qbuf[here, :].astype(jnp.bfloat16), keys, contract, preferred_element_type=jnp.float32
            ) * scale
            cached = jnp.where(
                (position >= begin_ref[index]) & (position < end_ref[index]), cached, jnp.float32(-1e30)
            )
            extra = fresh[here, :]
            peak = jnp.maximum(
                jnp.max(cached, axis=1, keepdims=True), jnp.max(extra, axis=1, keepdims=True)
            )
            cached = jnp.exp(cached - peak)
            extra = jnp.exp(extra - peak)
            total = jnp.sum(cached, axis=1, keepdims=True) + jnp.sum(extra, axis=1, keepdims=True)
            weighted = jnp.dot(
                cached.astype(jnp.bfloat16), values, preferred_element_type=jnp.float32
            ) + jnp.dot(extra.astype(jnp.bfloat16), new_values, preferred_element_type=jnp.float32)
            obuf[here, :] = weighted / total

        unroll = 4 if batch % 4 == 0 else 1

        def several(outer, carry):
            for inner in range(unroll):
                one(outer * unroll + inner)
            return carry

        lax.fori_loop(0, batch // unroll, several, 0)
        for head in range(group):
            for step in range(steps):
                abuf[chunk, step, :, pl.ds(head * size, size)] = obuf[
                    pl.ds(head * steps + step, batch, stride=lines), :
                ].astype(jnp.bfloat16)

    share = out_ref.shape[2]
    per = 4 // chunks
    out_rows = pl.ds(pl.multiple_of(sec * batch, batch), batch)

    def handoff(target):
        chunk, place = target // per, target % per
        source = abuf.at[chunk, :, :, pl.ds(place * share, share)]
        keep = pltpu.make_async_copy(source, out_ref.at[:, out_rows, :], o_local)
        copy = pltpu.make_async_remote_copy(
            src_ref=source, dst_ref=out_ref.at[:, out_rows, :],
            send_sem=o_send.at[target], recv_sem=o_recv.at[sec],
            device_id={"dp": dp, "sec": target}, device_id_type=pl.DeviceIdType.MESH,
        )
        return keep, copy

    for chunk in range(chunks):
        second_hop(2 * chunk)
        second_hop(2 * chunk + 1)
        if chunk + 1 < chunks:
            first_hop(2 * chunk + 2)
            first_hop(2 * chunk + 3)
        attend(chunk)
        for target in range(chunk * per, (chunk + 1) * per):
            keep, copy = handoff(target)
            pl.when(sec == target)(keep.start)
            pl.when(sec != target)(copy.start)

    for target in range(4):
        keep, copy = handoff(target)
        pl.when(sec == target)(keep.wait)
        pl.when(sec != target)(copy.wait_send)
        arrived = pltpu.make_async_remote_copy(
            src_ref=abuf.at[0, :, :, pl.ds(0, share)],
            dst_ref=out_ref.at[:, pl.ds(target * batch, batch), :],
            send_sem=o_send.at[target], recv_sem=o_recv.at[target],
            device_id={"dp": dp, "sec": target}, device_id_type=pl.DeviceIdType.MESH,
        )
        pl.when(sec != target)(arrived.wait_recv)
    for copy in x_copies + list(w_copies.values()) + list(messages.values()):
        copy.wait_send()


def fused_body(hidden_states, w_query, w_keyval, key_cache, value_cache, cache_begin, cache_end):
    steps, batch, _ = hidden_states.shape
    slots, half_len, size = key_cache.shape[1:]
    depth = w_query.shape[0]
    chunks = slots // 2
    group = w_query.shape[1] // size // chunks
    rows = steps * batch
    wide = (group + 2) // 2 * size
    pieces = 2 * chunks
    share = w_query.shape[1] // 4
    lanes = np.arange(size, dtype=np.float32) % (size // 2)
    freq = np.float32(THETA) ** (-(lanes * np.float32(2.0) / np.float32(size)))
    anywhere = pl.BlockSpec(memory_space=pl.ANY)
    scalars = pl.BlockSpec(memory_space=pltpu.SMEM)
    dma = pltpu.SemaphoreType.DMA
    return pl.pallas_call(
        functools.partial(fused_kernel, group),
        out_shape=jax.ShapeDtypeStruct((steps, 4 * batch, share), jnp.bfloat16),
        in_specs=[pl.BlockSpec(memory_space=pltpu.VMEM), scalars, scalars] + [anywhere] * 5,
        out_specs=anywhere,
        scratch_shapes=[
            pltpu.VMEM((4, steps, batch, 2 * depth), jnp.bfloat16),
            pltpu.VMEM((pieces, 2 * depth, wide), jnp.bfloat16),
            pltpu.VMEM((pieces, 4, rows, wide), jnp.float32),
            pltpu.VMEM((pieces, 3, rows, wide), jnp.float32),
            pltpu.VMEM((chunks, batch, 2, half_len, size), jnp.bfloat16),
            pltpu.VMEM((chunks, batch, 2, half_len, size), jnp.bfloat16),
            pltpu.VMEM((rows, size), jnp.float32),
            pltpu.VMEM((rows, size), jnp.float32),
            pltpu.VMEM((group * rows, size), jnp.float32),
            pltpu.VMEM((group * rows, rows), jnp.float32),
            pltpu.VMEM((group * rows, size), jnp.float32),
            pltpu.VMEM((chunks, steps, batch, group * size), jnp.bfloat16),
            dma, dma((3,)), dma((3,)),
            dma((chunks, 3)), dma((chunks, 3)), dma((chunks, 3)),
            dma((chunks, 2)),
            dma((pieces, 3)), dma((pieces, 3)),
            dma, dma((4,)), dma((4,)),
        ],
        compiler_params=pltpu.CompilerParams(
            collective_id=0, has_side_effects=True, vmem_limit_bytes=56 * 1024 * 1024
        ),
        cost_estimate=pl.CostEstimate(
            flops=2 * 4 * rows * 2 * depth * pieces * wide,
            bytes_accessed=2 * (w_query.size + w_keyval.size + 2 * key_cache.size),
            transcendentals=0,
        ),
    )(freq[None, :], cache_begin, cache_end, hidden_states, w_query, w_keyval, key_cache, value_cache)


def body(sizes, hidden_states, w_query, w_keyval, key_cache, value_cache, cache_begin, cache_end):
    arrays = (hidden_states, w_query, w_keyval, key_cache, value_cache, cache_begin, cache_end)
    slots = key_cache.shape[1]
    if sizes["dp"] == 2 and sizes["sec"] == 4 and slots in (2, 4, 8):
        return fused_body(*arrays)
    return general_body(*arrays)


def solution(mesh):
    return jax.shard_map(
        functools.partial(body, mesh.shape),
        mesh=mesh,
        in_specs=(
            P(None, ("dp", "sec"), None),
            P(("dp", "sec"), "tp"),
            P(("dp", "sec"), "tp"),
            P(("dp", "sec"), "tp", None, None),
            P(("dp", "sec"), "tp", None, None),
            P(("dp", "sec")),
            P(("dp", "sec")),
        ),
        out_specs=P(None, "dp", ("tp", "sec")),
        check_vma=False,
    )
```

```python
import functools

import jax
import jax.numpy as jnp
import numpy as np
from jax import lax
from jax.experimental import pallas as pl
from jax.experimental.pallas import tpu as pltpu
from jax.sharding import PartitionSpec as P

THETA = 500000.0


def swapped(value, axis, stride):
    mask = 2**stride
    pairs = [(source, source ^ mask) for source in range(lax.axis_size(axis))]
    return lax.ppermute(value, axis, pairs)


def rotate(vector, positions):
    half = vector.shape[-1] // 2
    freq = THETA ** (-(jnp.arange(half, dtype=jnp.float32) * 2.0 / vector.shape[-1]))
    angle = positions[..., None] * freq
    angle = angle.reshape(positions.shape + (1,) * (vector.ndim - positions.ndim - 1) + (half,))
    cosine = jnp.cos(angle)
    sine = jnp.sin(angle)
    first = vector[..., :half]
    second = vector[..., half:]
    return jnp.concatenate(
        [first * cosine - second * sine, second * cosine + first * sine], axis=-1
    )


def make_accumulate(token_rows, pieces):
    return (
        jnp.dot(token_rows, pieces[0], preferred_element_type=jnp.float32),
        jnp.dot(token_rows, pieces[1], preferred_element_type=jnp.float32),
    )


def partial_attention(query, keys, values, live, score_scale):
    scores = (
        jnp.einsum("sbkgd,bkpd->sbkgp", query, keys, preferred_element_type=jnp.float32)
        * score_scale
    )
    live = jnp.broadcast_to(live, scores.shape)
    masked = jnp.where(live, scores, jnp.float32(-1e30))
    maxima = jnp.max(masked, axis=-1)
    expo = jnp.where(live, jnp.exp(masked - maxima[..., None]), jnp.float32(0.0))
    totals = jnp.sum(expo, axis=-1)
    weighted = jnp.einsum(
        "sbkgp,bkpd->sbkgd", expo.astype(jnp.bfloat16), values, preferred_element_type=jnp.float32
    )
    return (maxima, totals, weighted)


def merge_parts(parts):
    overall = parts[0][0]
    for entry in parts[1:]:
        overall = jnp.maximum(overall, entry[0])
    weighted = jnp.zeros_like(parts[0][2])
    totals = jnp.zeros_like(parts[0][1])
    for entry in parts:
        factor = jnp.exp(entry[0] - overall)
        weighted = weighted + entry[2] * factor[..., None]
        totals = totals + entry[1] * factor
    return weighted / totals[..., None]


def general_body(hidden_states, w_query, w_keyval, key_cache, value_cache, cache_begin, cache_end):
    num_steps, batch_rows, width = hidden_states.shape
    head_size = key_cache.shape[-1]
    query_cols = w_query.shape[1]
    keyval_cols = w_keyval.shape[1]
    local_heads = query_cols // head_size
    slot_count = key_cache.shape[1]
    half_len = key_cache.shape[2]
    score_scale = head_size ** (-0.5)
    sec_count = lax.axis_size("sec")
    sec_index = lax.axis_index("sec")
    sec_group = lax.all_gather(hidden_states, "sec", axis=1, tiled=True)
    shard_rows = w_query.shape[0]
    dp_count = width // (sec_count * shard_rows)
    group_rows = num_steps * batch_rows * sec_count
    grouped = sec_group.reshape(group_rows, dp_count, sec_count, shard_rows)
    chosen = lax.dynamic_slice_in_dim(grouped, sec_index, 1, 2).reshape(
        group_rows, dp_count * shard_rows
    )
    query_all, keyval_all = make_accumulate(
        chosen,
        (
            lax.all_gather(w_query, "dp", axis=0, tiled=True),
            lax.all_gather(w_keyval, "dp", axis=0, tiled=True),
        ),
    )
    query_acc, keyval_acc = (
        lax.psum_scatter(
            query_all.reshape(num_steps, sec_count * batch_rows, query_cols),
            "sec",
            scatter_dimension=1,
            tiled=True,
        ),
        lax.psum_scatter(
            keyval_all.reshape(num_steps, sec_count * batch_rows, keyval_cols),
            "sec",
            scatter_dimension=1,
            tiled=True,
        ),
    )
    query_acc = query_acc.reshape(num_steps * batch_rows, query_cols)
    keyval_acc = keyval_acc.reshape(num_steps * batch_rows, keyval_cols)
    positions = (
        cache_end.astype(jnp.float32)[None, :] + jnp.arange(num_steps, dtype=jnp.float32)[:, None]
    )
    query = rotate(
        query_acc.reshape(num_steps, batch_rows, local_heads, head_size), positions
    ).astype(jnp.bfloat16)
    step_ids = jnp.arange(num_steps, dtype=jnp.int32)
    causal = step_ids[None, :] <= step_ids[:, None]
    if slot_count == 1:
        parity = lax.axis_index("tp") % 2
        own_proj = keyval_acc.reshape(num_steps, batch_rows, head_size)
        own_proj = jnp.where(parity == 0, rotate(own_proj, positions), own_proj).astype(
            jnp.bfloat16
        )
        partner_query, partner_proj = swapped((query, own_proj), "tp", 0)
        new_keys = jnp.where(parity == 0, own_proj, partner_proj)
        new_values = jnp.where(parity == 0, partner_proj, own_proj)
        lower_heads = jnp.where(parity == 0, query, partner_query)
        upper_heads = jnp.where(parity == 0, partner_query, query)
        both_heads = jnp.concatenate([lower_heads, upper_heads], axis=2)[:, :, None]
        cache_pos = parity * half_len + jnp.arange(half_len, dtype=jnp.int32)
        cache_live = (cache_pos[None, :] >= cache_begin[:, None]) & (
            cache_pos[None, :] < cache_end[:, None]
        )
        cache_part = partial_attention(
            both_heads, key_cache, value_cache, cache_live[None, :, None, None, :], score_scale
        )
        mine_start = parity * local_heads
        theirs_start = (1 - parity) * local_heads

        def select_heads(array, start):
            return lax.dynamic_slice_in_dim(array, start, local_heads, 3)

        returned = (
            swapped(select_heads(cache_part[0], theirs_start).astype(jnp.bfloat16), "tp", 0).astype(
                jnp.float32
            ),
            swapped(select_heads(cache_part[1], theirs_start).astype(jnp.bfloat16), "tp", 0).astype(
                jnp.float32
            ),
            swapped(select_heads(cache_part[2], theirs_start).astype(jnp.bfloat16), "tp", 0).astype(
                jnp.float32
            ),
        )
        own_part = (
            select_heads(cache_part[0], mine_start),
            select_heads(cache_part[1], mine_start),
            select_heads(cache_part[2], mine_start),
        )
        fresh_part = partial_attention(
            query[:, :, None],
            jnp.transpose(new_keys, (1, 0, 2))[:, None],
            jnp.transpose(new_values, (1, 0, 2))[:, None],
            causal[:, None, None, None, :],
            score_scale,
        )
        parts = [own_part, returned, fresh_part]
    else:
        local_kv = keyval_cols // (2 * head_size)
        keyval = keyval_acc.reshape(num_steps, batch_rows, local_kv, 2, head_size)
        new_keys = rotate(keyval[:, :, :, 0], positions).astype(jnp.bfloat16)
        new_values = keyval[:, :, :, 1].astype(jnp.bfloat16)
        whole_keys = key_cache.reshape(batch_rows, local_kv, 2 * half_len, head_size)
        whole_values = value_cache.reshape(batch_rows, local_kv, 2 * half_len, head_size)
        grouped_query = query.reshape(
            num_steps, batch_rows, local_kv, local_heads // local_kv, head_size
        )
        cache_pos = jnp.arange(2 * half_len, dtype=jnp.int32)
        cache_live = (cache_pos[None, :] >= cache_begin[:, None]) & (
            cache_pos[None, :] < cache_end[:, None]
        )
        cache_part = partial_attention(
            grouped_query, whole_keys, whole_values, cache_live[None, :, None, None, :], score_scale
        )
        fresh_part = partial_attention(
            grouped_query,
            jnp.transpose(new_keys, (1, 2, 0, 3)),
            jnp.transpose(new_values, (1, 2, 0, 3)),
            causal[:, None, None, None, :],
            score_scale,
        )
        parts = [cache_part, fresh_part]
    attended = (
        merge_parts(parts)
        .astype(jnp.bfloat16)
        .reshape(num_steps, batch_rows, local_heads * head_size)
    )
    return lax.all_to_all(attended, "sec", split_axis=2, concat_axis=1, tiled=True)


def fused_kernel(
    group, freq_ref, begin_ref, end_ref, hidden_ref, wq_ref, wkv_ref, key_ref, value_ref, out_ref,
    xbuf, wbuf, pbuf, rbuf, kbuf, vbuf, cosine, sine, qbuf, fresh, obuf, abuf,
    x_local, x_send, x_recv, w_local, w_send, w_recv, kv_sem, r_send, r_recv, o_local, o_send, o_recv,
):
    chunks = wkv_ref.shape[1] // (2 * key_ref.shape[3])
    steps, batch, _ = hidden_ref.shape
    size = key_ref.shape[3]
    depth = wq_ref.shape[0]
    span = 2 * depth
    rows = steps * batch
    half_len = key_ref.shape[2]
    blocks = (group + 2) // 2
    wide = blocks * size
    dp, sec = lax.axis_index("dp"), lax.axis_index("sec")
    core = sec % 2
    dp_other = 1 - dp
    sec_far = (sec + 2) % 4
    sec_pair = sec + 1 - 2 * core
    near = ({"dp": dp, "sec": sec}, {"dp": dp_other, "sec": sec}, {"dp": dp, "sec": sec_far}, {"dp": dp_other, "sec": sec_far})
    pair = {"dp": dp, "sec": sec_pair}
    cross = {"dp": dp, "sec": (sec_pair + 2) % 4}
    odd = lax.axis_index("tp") % 2
    above = {"tp": lax.axis_index("tp") + 1 - 2 * odd}
    chips = (dp * 2 + sec // 2, dp_other * 2 + sec // 2, dp * 2 + sec_far // 2, dp_other * 2 + sec_far // 2)

    def weight_parts(chunk):
        first = chunk * group * size
        return (
            (2 * chunk, 0, wide, wq_ref, first),
            (2 * chunk + 1, 0, group * size - wide, wq_ref, first + wide),
            (2 * chunk + 1, group * size - wide, 2 * size, wkv_ref, chunk * 2 * size),
        )

    own_rows = pl.ds(pl.multiple_of(core * depth, depth), depth)

    def weight_refs(part):
        piece, start, width, source, column = part
        return (
            source.at[:, pl.ds(column, width)],
            wbuf.at[piece, own_rows, pl.ds(start, width)],
        )

    def hidden_slice(relation):
        return hidden_ref.at[:, :, pl.ds(pl.multiple_of(chips[relation] * span, span), span)]

    local_copies = {}
    x_own = pltpu.make_async_copy(hidden_slice(0), xbuf.at[0], x_local)
    x_own.start()
    for chunk in range(chunks):
        for index, part in enumerate(weight_parts(chunk)):
            source, target = weight_refs(part)
            copy = pltpu.make_async_copy(source, target, w_local.at[chunk, index])
            copy.start()
            local_copies[chunk, index] = copy

    barrier = pltpu.get_barrier_semaphore()
    for peer in near[1:] + (pair, cross, above):
        pl.semaphore_signal(barrier, inc=1, device_id=peer, device_id_type=pl.DeviceIdType.MESH)
    pl.semaphore_wait(barrier, 6)

    half_steps = steps // 2
    mine = pl.ds(odd * half_steps, half_steps)
    theirs = pl.ds((1 - odd) * half_steps, half_steps)
    x_copies = []
    for relation in (3, 1, 2):
        source, target = hidden_slice(relation), xbuf.at[relation]
        if relation == 3:
            source, target = source.at[mine], target.at[mine]
        copy = pltpu.make_async_remote_copy(
            src_ref=source, dst_ref=target,
            send_sem=x_send.at[relation], recv_sem=x_recv.at[relation],
            device_id=near[relation], device_id_type=pl.DeviceIdType.MESH,
        )
        copy.start()
        x_copies.append(copy)
    w_copies = {}
    for chunk in range(chunks):
        for index, part in enumerate(weight_parts(chunk)):
            source, target = weight_refs(part)
            copy = pltpu.make_async_remote_copy(
                src_ref=source, dst_ref=target,
                send_sem=w_send.at[chunk, index], recv_sem=w_recv.at[chunk, index],
                device_id=pair, device_id_type=pl.DeviceIdType.MESH,
            )
            copy.start()
            w_copies[chunk, index] = copy
    kv_copies = []
    for chunk in range(chunks):
        slots = pl.ds(2 * chunk, 2)
        for index, (source, target) in enumerate(((key_ref, kbuf), (value_ref, vbuf))):
            copy = pltpu.make_async_copy(source.at[:, slots], target.at[chunk], kv_sem.at[chunk, index])
            copy.start()
            kv_copies.append(copy)

    row = lax.broadcasted_iota(jnp.int32, (rows, size), 0)
    lane = lax.broadcasted_iota(jnp.int32, (rows, size), 1)
    place = row // batch
    for index in range(batch):
        place = place + jnp.where(row % batch == index, end_ref[index], 0)
    angle = place.astype(jnp.float32) * freq_ref[...]
    cosine[...] = jnp.cos(angle)
    sine[...] = jnp.where(lane < size // 2, -jnp.sin(angle), jnp.sin(angle))

    def rotated(vector):
        return vector * cosine[...] + pltpu.roll(vector, size // 2, 1) * sine[...]

    def send(piece, message, source, target):
        copy = pltpu.make_async_remote_copy(
            src_ref=source, dst_ref=rbuf.at[piece, message],
            send_sem=r_send.at[piece, message], recv_sem=r_recv.at[piece, message],
            device_id=target, device_id_type=pl.DeviceIdType.MESH,
        )
        copy.start()
        return copy

    tile = 512 if span % 512 == 0 else span

    def multiply(piece, first, count):
        group_rows = pl.ds(first, count)
        for step in range(span // tile):
            deep = pl.ds(step * tile, tile)
            part = jnp.dot(
                xbuf[group_rows, :, :, deep].reshape(count * rows, tile), wbuf[piece, deep, :],
                preferred_element_type=jnp.float32,
            ).reshape(count, rows, wide)
            if step == 0:
                pbuf[piece, group_rows] = part
            else:
                pbuf[piece, group_rows] += part

    messages = {}

    def first_hop(piece, message):
        one = 1 if piece % 2 == 0 else 2
        source = pbuf.at[piece, 3 if message == 0 else one]
        messages[piece, message] = send(piece, message, source, near[one])

    def second_hop(piece):
        two = 2 if piece % 2 == 0 else 1
        messages[piece, 0].wait_recv()
        pbuf[piece, two] += rbuf[piece, 0]
        messages[piece, 2] = send(piece, 2, pbuf.at[piece, two], near[two])

    def await_weights(piece):
        for index in ((0,), (1, 2))[piece % 2]:
            local_copies[piece // 2, index].wait()
            w_copies[piece // 2, index].wait_recv()

    x_copies[0].wait_recv()
    passed = pltpu.make_async_remote_copy(
        src_ref=xbuf.at[3, mine], dst_ref=xbuf.at[3, mine],
        send_sem=x_send.at[0], recv_sem=x_recv.at[0],
        device_id=above, device_id_type=pl.DeviceIdType.MESH,
    )
    passed.start()
    pltpu.make_async_remote_copy(
        src_ref=xbuf.at[3, theirs], dst_ref=xbuf.at[3, theirs],
        send_sem=x_send.at[0], recv_sem=x_recv.at[0],
        device_id=above, device_id_type=pl.DeviceIdType.MESH,
    ).wait_recv()
    for piece in range(2):
        await_weights(piece)
        multiply(piece, 3, 1)
        first_hop(piece, 0)
    x_own.wait()
    x_copies[1].wait_recv()
    x_copies[2].wait_recv()
    for piece in range(2):
        multiply(piece, 0, 3)
        first_hop(piece, 1)
    for piece in range(2, 2 * chunks):
        await_weights(piece)
        multiply(piece, 0, 4)

    def attend(chunk):
        new = [None, None]
        for half in range(2):
            piece = 2 * chunk + half
            messages[piece, 1].wait_recv()
            messages[piece, 2].wait_recv()
            for block in range(blocks):
                cols = pl.ds(block * size, size)
                total = pbuf[piece, 0, :, cols] + rbuf[piece, 1, :, cols] + rbuf[piece, 2, :, cols]
                head = half * blocks + block
                if head == group + 1:
                    new[1] = total.astype(jnp.bfloat16)
                elif head == group:
                    new[0] = rotated(total).astype(jnp.bfloat16)
                else:
                    turned = rotated(total).astype(jnp.bfloat16).astype(jnp.float32)
                    for step in range(steps):
                        qbuf[pl.ds(head * steps + step, batch, stride=group * steps), :] = turned[
                            step * batch : (step + 1) * batch
                        ]
        new_keys, new_values = new
        lines = group * steps
        scale = size ** (-0.5)
        query = qbuf[...].astype(jnp.bfloat16)
        contract = (((1,), (1,)), ((), ()))
        scores = lax.dot_general(query, new_keys, contract, preferred_element_type=jnp.float32) * scale
        line = lax.broadcasted_iota(jnp.int32, scores.shape, 0)
        other = lax.broadcasted_iota(jnp.int32, scores.shape, 1)
        live = (line // lines == other % batch) & (other // batch <= line % steps)
        fresh[...] = jnp.where(live, scores, jnp.float32(-1e30))
        kv_copies[2 * chunk].wait()
        kv_copies[2 * chunk + 1].wait()
        cache_len = 2 * half_len

        def one(index):
            here = pl.ds(pl.multiple_of(index * lines, lines), lines)
            keys = kbuf[chunk, index].reshape(cache_len, size)
            values = vbuf[chunk, index].reshape(cache_len, size)
            position = lax.broadcasted_iota(jnp.int32, (lines, cache_len), 1)
            cached = lax.dot_general(
                qbuf[here, :].astype(jnp.bfloat16), keys, contract, preferred_element_type=jnp.float32
            ) * scale
            cached = jnp.where(
                (position >= begin_ref[index]) & (position < end_ref[index]), cached, jnp.float32(-1e30)
            )
            extra = fresh[here, :]
            peak = jnp.maximum(
                jnp.max(cached, axis=1, keepdims=True), jnp.max(extra, axis=1, keepdims=True)
            )
            cached = jnp.exp(cached - peak)
            extra = jnp.exp(extra - peak)
            total = jnp.sum(cached, axis=1, keepdims=True) + jnp.sum(extra, axis=1, keepdims=True)
            weighted = jnp.dot(
                cached.astype(jnp.bfloat16), values, preferred_element_type=jnp.float32
            ) + jnp.dot(extra.astype(jnp.bfloat16), new_values, preferred_element_type=jnp.float32)
            obuf[here, :] = weighted / total

        unroll = 8 if batch % 8 == 0 else 1

        def several(outer, carry):
            for inner in range(unroll):
                one(outer * unroll + inner)
            return carry

        lax.fori_loop(0, batch // unroll, several, 0)
        for head in range(group):
            for step in range(steps):
                abuf[chunk, step, :, pl.ds(head * size, size)] = obuf[
                    pl.ds(head * steps + step, batch, stride=lines), :
                ].astype(jnp.bfloat16)

    share = out_ref.shape[2]
    per = 4 // chunks
    out_rows = pl.ds(pl.multiple_of(sec * batch, batch), batch)

    def handoff(target):
        chunk, place = target // per, target % per
        source = abuf.at[chunk, :, :, pl.ds(place * share, share)]
        keep = pltpu.make_async_copy(source, out_ref.at[:, out_rows, :], o_local)
        copy = pltpu.make_async_remote_copy(
            src_ref=source, dst_ref=out_ref.at[:, out_rows, :],
            send_sem=o_send.at[target], recv_sem=o_recv.at[sec],
            device_id={"dp": dp, "sec": target}, device_id_type=pl.DeviceIdType.MESH,
        )
        return keep, copy

    for piece in range(2):
        second_hop(piece)
    for chunk in range(chunks):
        if chunk + 1 < chunks:
            for message in range(2):
                first_hop(2 * chunk + 2, message)
                first_hop(2 * chunk + 3, message)
            second_hop(2 * chunk + 2)
            second_hop(2 * chunk + 3)
        attend(chunk)
        for target in range(chunk * per, (chunk + 1) * per):
            keep, copy = handoff(target)
            pl.when(sec == target)(keep.start)
            pl.when(sec != target)(copy.start)

    for target in range(4):
        keep, copy = handoff(target)
        pl.when(sec == target)(keep.wait)
        pl.when(sec != target)(copy.wait_send)
        arrived = pltpu.make_async_remote_copy(
            src_ref=abuf.at[0, :, :, pl.ds(0, share)],
            dst_ref=out_ref.at[:, pl.ds(target * batch, batch), :],
            send_sem=o_send.at[target], recv_sem=o_recv.at[target],
            device_id={"dp": dp, "sec": target}, device_id_type=pl.DeviceIdType.MESH,
        )
        pl.when(sec != target)(arrived.wait_recv)
    for copy in x_copies + [passed] + list(w_copies.values()) + list(messages.values()):
        copy.wait_send()


def fused_body(hidden_states, w_query, w_keyval, key_cache, value_cache, cache_begin, cache_end):
    steps, batch, _ = hidden_states.shape
    slots, half_len, size = key_cache.shape[1:]
    depth = w_query.shape[0]
    chunks = slots // 2
    group = w_query.shape[1] // size // chunks
    rows = steps * batch
    wide = (group + 2) // 2 * size
    pieces = 2 * chunks
    share = w_query.shape[1] // 4
    lanes = np.arange(size, dtype=np.float32) % (size // 2)
    freq = np.float32(THETA) ** (-(lanes * np.float32(2.0) / np.float32(size)))
    anywhere = pl.BlockSpec(memory_space=pl.ANY)
    scalars = pl.BlockSpec(memory_space=pltpu.SMEM)
    dma = pltpu.SemaphoreType.DMA
    return pl.pallas_call(
        functools.partial(fused_kernel, group),
        out_shape=jax.ShapeDtypeStruct((steps, 4 * batch, share), jnp.bfloat16),
        in_specs=[pl.BlockSpec(memory_space=pltpu.VMEM), scalars, scalars] + [anywhere] * 5,
        out_specs=anywhere,
        scratch_shapes=[
            pltpu.VMEM((4, steps, batch, 2 * depth), jnp.bfloat16),
            pltpu.VMEM((pieces, 2 * depth, wide), jnp.bfloat16),
            pltpu.VMEM((pieces, 4, rows, wide), jnp.float32),
            pltpu.VMEM((pieces, 3, rows, wide), jnp.float32),
            pltpu.VMEM((chunks, batch, 2, half_len, size), jnp.bfloat16),
            pltpu.VMEM((chunks, batch, 2, half_len, size), jnp.bfloat16),
            pltpu.VMEM((rows, size), jnp.float32),
            pltpu.VMEM((rows, size), jnp.float32),
            pltpu.VMEM((group * rows, size), jnp.float32),
            pltpu.VMEM((group * rows, rows), jnp.float32),
            pltpu.VMEM((group * rows, size), jnp.float32),
            pltpu.VMEM((chunks, steps, batch, group * size), jnp.bfloat16),
            dma, dma((4,)), dma((4,)),
            dma((chunks, 3)), dma((chunks, 3)), dma((chunks, 3)),
            dma((chunks, 2)),
            dma((pieces, 3)), dma((pieces, 3)),
            dma, dma((4,)), dma((4,)),
        ],
        compiler_params=pltpu.CompilerParams(
            collective_id=0, has_side_effects=True, vmem_limit_bytes=56 * 1024 * 1024
        ),
        cost_estimate=pl.CostEstimate(
            flops=2 * 4 * rows * 2 * depth * pieces * wide,
            bytes_accessed=2 * (w_query.size + w_keyval.size + 2 * key_cache.size),
            transcendentals=0,
        ),
    )(freq[None, :], cache_begin, cache_end, hidden_states, w_query, w_keyval, key_cache, value_cache)


def body(sizes, hidden_states, w_query, w_keyval, key_cache, value_cache, cache_begin, cache_end):
    arrays = (hidden_states, w_query, w_keyval, key_cache, value_cache, cache_begin, cache_end)
    slots = key_cache.shape[1]
    if sizes["dp"] == 2 and sizes["sec"] == 4 and sizes["tp"] % 2 == 0 and slots in (2, 4, 8):
        return fused_body(*arrays)
    return general_body(*arrays)


def solution(mesh):
    return jax.shard_map(
        functools.partial(body, mesh.shape),
        mesh=mesh,
        in_specs=(
            P(None, ("dp", "sec"), None),
            P(("dp", "sec"), "tp"),
            P(("dp", "sec"), "tp"),
            P(("dp", "sec"), "tp", None, None),
            P(("dp", "sec"), "tp", None, None),
            P(("dp", "sec")),
            P(("dp", "sec")),
        ),
        out_specs=P(None, "dp", ("tp", "sec")),
        check_vma=False,
    )
```

```python
import functools

import jax
import jax.numpy as jnp
import numpy as np
from jax import lax
from jax.experimental import pallas as pl
from jax.experimental.pallas import tpu as pltpu
from jax.sharding import PartitionSpec as P

THETA = 500000.0


def swapped(value, axis, stride):
    mask = 2**stride
    pairs = [(source, source ^ mask) for source in range(lax.axis_size(axis))]
    return lax.ppermute(value, axis, pairs)


def rotate(vector, positions):
    half = vector.shape[-1] // 2
    freq = THETA ** (-(jnp.arange(half, dtype=jnp.float32) * 2.0 / vector.shape[-1]))
    angle = positions[..., None] * freq
    angle = angle.reshape(positions.shape + (1,) * (vector.ndim - positions.ndim - 1) + (half,))
    cosine = jnp.cos(angle)
    sine = jnp.sin(angle)
    first = vector[..., :half]
    second = vector[..., half:]
    return jnp.concatenate(
        [first * cosine - second * sine, second * cosine + first * sine], axis=-1
    )


def make_accumulate(token_rows, pieces):
    return (
        jnp.dot(token_rows, pieces[0], preferred_element_type=jnp.float32),
        jnp.dot(token_rows, pieces[1], preferred_element_type=jnp.float32),
    )


def partial_attention(query, keys, values, live, score_scale):
    scores = (
        jnp.einsum("sbkgd,bkpd->sbkgp", query, keys, preferred_element_type=jnp.float32)
        * score_scale
    )
    live = jnp.broadcast_to(live, scores.shape)
    masked = jnp.where(live, scores, jnp.float32(-1e30))
    maxima = jnp.max(masked, axis=-1)
    expo = jnp.where(live, jnp.exp(masked - maxima[..., None]), jnp.float32(0.0))
    totals = jnp.sum(expo, axis=-1)
    weighted = jnp.einsum(
        "sbkgp,bkpd->sbkgd", expo.astype(jnp.bfloat16), values, preferred_element_type=jnp.float32
    )
    return (maxima, totals, weighted)


def merge_parts(parts):
    overall = parts[0][0]
    for entry in parts[1:]:
        overall = jnp.maximum(overall, entry[0])
    weighted = jnp.zeros_like(parts[0][2])
    totals = jnp.zeros_like(parts[0][1])
    for entry in parts:
        factor = jnp.exp(entry[0] - overall)
        weighted = weighted + entry[2] * factor[..., None]
        totals = totals + entry[1] * factor
    return weighted / totals[..., None]


def general_body(hidden_states, w_query, w_keyval, key_cache, value_cache, cache_begin, cache_end):
    num_steps, batch_rows, width = hidden_states.shape
    head_size = key_cache.shape[-1]
    query_cols = w_query.shape[1]
    keyval_cols = w_keyval.shape[1]
    local_heads = query_cols // head_size
    slot_count = key_cache.shape[1]
    half_len = key_cache.shape[2]
    score_scale = head_size ** (-0.5)
    sec_count = lax.axis_size("sec")
    sec_index = lax.axis_index("sec")
    sec_group = lax.all_gather(hidden_states, "sec", axis=1, tiled=True)
    shard_rows = w_query.shape[0]
    dp_count = width // (sec_count * shard_rows)
    group_rows = num_steps * batch_rows * sec_count
    grouped = sec_group.reshape(group_rows, dp_count, sec_count, shard_rows)
    chosen = lax.dynamic_slice_in_dim(grouped, sec_index, 1, 2).reshape(
        group_rows, dp_count * shard_rows
    )
    query_all, keyval_all = make_accumulate(
        chosen,
        (
            lax.all_gather(w_query, "dp", axis=0, tiled=True),
            lax.all_gather(w_keyval, "dp", axis=0, tiled=True),
        ),
    )
    query_acc, keyval_acc = (
        lax.psum_scatter(
            query_all.reshape(num_steps, sec_count * batch_rows, query_cols),
            "sec",
            scatter_dimension=1,
            tiled=True,
        ),
        lax.psum_scatter(
            keyval_all.reshape(num_steps, sec_count * batch_rows, keyval_cols),
            "sec",
            scatter_dimension=1,
            tiled=True,
        ),
    )
    query_acc = query_acc.reshape(num_steps * batch_rows, query_cols)
    keyval_acc = keyval_acc.reshape(num_steps * batch_rows, keyval_cols)
    positions = (
        cache_end.astype(jnp.float32)[None, :] + jnp.arange(num_steps, dtype=jnp.float32)[:, None]
    )
    query = rotate(
        query_acc.reshape(num_steps, batch_rows, local_heads, head_size), positions
    ).astype(jnp.bfloat16)
    step_ids = jnp.arange(num_steps, dtype=jnp.int32)
    causal = step_ids[None, :] <= step_ids[:, None]
    if slot_count == 1:
        parity = lax.axis_index("tp") % 2
        own_proj = keyval_acc.reshape(num_steps, batch_rows, head_size)
        own_proj = jnp.where(parity == 0, rotate(own_proj, positions), own_proj).astype(
            jnp.bfloat16
        )
        partner_query, partner_proj = swapped((query, own_proj), "tp", 0)
        new_keys = jnp.where(parity == 0, own_proj, partner_proj)
        new_values = jnp.where(parity == 0, partner_proj, own_proj)
        lower_heads = jnp.where(parity == 0, query, partner_query)
        upper_heads = jnp.where(parity == 0, partner_query, query)
        both_heads = jnp.concatenate([lower_heads, upper_heads], axis=2)[:, :, None]
        cache_pos = parity * half_len + jnp.arange(half_len, dtype=jnp.int32)
        cache_live = (cache_pos[None, :] >= cache_begin[:, None]) & (
            cache_pos[None, :] < cache_end[:, None]
        )
        cache_part = partial_attention(
            both_heads, key_cache, value_cache, cache_live[None, :, None, None, :], score_scale
        )
        mine_start = parity * local_heads
        theirs_start = (1 - parity) * local_heads

        def select_heads(array, start):
            return lax.dynamic_slice_in_dim(array, start, local_heads, 3)

        returned = (
            swapped(select_heads(cache_part[0], theirs_start).astype(jnp.bfloat16), "tp", 0).astype(
                jnp.float32
            ),
            swapped(select_heads(cache_part[1], theirs_start).astype(jnp.bfloat16), "tp", 0).astype(
                jnp.float32
            ),
            swapped(select_heads(cache_part[2], theirs_start).astype(jnp.bfloat16), "tp", 0).astype(
                jnp.float32
            ),
        )
        own_part = (
            select_heads(cache_part[0], mine_start),
            select_heads(cache_part[1], mine_start),
            select_heads(cache_part[2], mine_start),
        )
        fresh_part = partial_attention(
            query[:, :, None],
            jnp.transpose(new_keys, (1, 0, 2))[:, None],
            jnp.transpose(new_values, (1, 0, 2))[:, None],
            causal[:, None, None, None, :],
            score_scale,
        )
        parts = [own_part, returned, fresh_part]
    else:
        local_kv = keyval_cols // (2 * head_size)
        keyval = keyval_acc.reshape(num_steps, batch_rows, local_kv, 2, head_size)
        new_keys = rotate(keyval[:, :, :, 0], positions).astype(jnp.bfloat16)
        new_values = keyval[:, :, :, 1].astype(jnp.bfloat16)
        whole_keys = key_cache.reshape(batch_rows, local_kv, 2 * half_len, head_size)
        whole_values = value_cache.reshape(batch_rows, local_kv, 2 * half_len, head_size)
        grouped_query = query.reshape(
            num_steps, batch_rows, local_kv, local_heads // local_kv, head_size
        )
        cache_pos = jnp.arange(2 * half_len, dtype=jnp.int32)
        cache_live = (cache_pos[None, :] >= cache_begin[:, None]) & (
            cache_pos[None, :] < cache_end[:, None]
        )
        cache_part = partial_attention(
            grouped_query, whole_keys, whole_values, cache_live[None, :, None, None, :], score_scale
        )
        fresh_part = partial_attention(
            grouped_query,
            jnp.transpose(new_keys, (1, 2, 0, 3)),
            jnp.transpose(new_values, (1, 2, 0, 3)),
            causal[:, None, None, None, :],
            score_scale,
        )
        parts = [cache_part, fresh_part]
    attended = (
        merge_parts(parts)
        .astype(jnp.bfloat16)
        .reshape(num_steps, batch_rows, local_heads * head_size)
    )
    return lax.all_to_all(attended, "sec", split_axis=2, concat_axis=1, tiled=True)


def fused_kernel(
    group, freq_ref, begin_ref, end_ref, hidden_ref, wq_ref, wkv_ref, key_ref, value_ref, out_ref,
    xbuf, wbuf, pbuf, rbuf, kbuf, vbuf, cosine, sine, qbuf, fresh, obuf, abuf,
    x_local, x_send, x_recv, w_local, w_send, w_recv, kv_sem, r_send, r_recv, o_local, o_send, o_recv,
):
    chunks = wkv_ref.shape[1] // (2 * key_ref.shape[3])
    steps, batch, _ = hidden_ref.shape
    size = key_ref.shape[3]
    depth = wq_ref.shape[0]
    span = 2 * depth
    rows = steps * batch
    half_len = key_ref.shape[2]
    blocks = (group + 2) // 2
    wide = blocks * size
    dp, sec = lax.axis_index("dp"), lax.axis_index("sec")
    core = sec % 2
    dp_other = 1 - dp
    sec_far = (sec + 2) % 4
    sec_pair = sec + 1 - 2 * core
    near = ({"dp": dp, "sec": sec}, {"dp": dp_other, "sec": sec}, {"dp": dp, "sec": sec_far}, {"dp": dp_other, "sec": sec_far})
    pair = {"dp": dp, "sec": sec_pair}
    cross = {"dp": dp, "sec": (sec_pair + 2) % 4}
    odd = lax.axis_index("tp") % 2
    above = {"tp": lax.axis_index("tp") + 1 - 2 * odd}
    chips = (dp * 2 + sec // 2, dp_other * 2 + sec // 2, dp * 2 + sec_far // 2, dp_other * 2 + sec_far // 2)

    def weight_parts(chunk):
        first = chunk * group * size
        return (
            (2 * chunk, 0, wide, wq_ref, first),
            (2 * chunk + 1, 0, group * size - wide, wq_ref, first + wide),
            (2 * chunk + 1, group * size - wide, 2 * size, wkv_ref, chunk * 2 * size),
        )

    own_rows = pl.ds(pl.multiple_of(core * depth, depth), depth)

    def weight_refs(part):
        piece, start, width, source, column = part
        return (
            source.at[:, pl.ds(column, width)],
            wbuf.at[piece, own_rows, pl.ds(start, width)],
        )

    def hidden_slice(relation):
        return hidden_ref.at[:, :, pl.ds(pl.multiple_of(chips[relation] * span, span), span)]

    local_copies, messages = {}, {}
    x_own = pltpu.make_async_copy(hidden_slice(0), xbuf.at[0], x_local)
    x_own.start()
    for chunk in range(chunks):
        for index, part in enumerate(weight_parts(chunk)):
            source, target = weight_refs(part)
            copy = pltpu.make_async_copy(source, target, w_local.at[chunk, index])
            copy.start()
            local_copies[chunk, index] = copy

    barrier = pltpu.get_barrier_semaphore()
    for peer in near[1:] + (pair, cross, above):
        pl.semaphore_signal(barrier, inc=1, device_id=peer, device_id_type=pl.DeviceIdType.MESH)
    pl.semaphore_wait(barrier, 6)

    def deliver(source, target, index, device):
        copy = pltpu.make_async_remote_copy(
            src_ref=source, dst_ref=target, send_sem=x_send.at[index], recv_sem=x_recv.at[index],
            device_id=device, device_id_type=pl.DeviceIdType.MESH,
        )
        return copy

    half_steps = steps // 2
    x_copies = {}
    for step in range(half_steps):
        where = odd * half_steps + step
        x_copies[step] = deliver(hidden_slice(3).at[where], xbuf.at[3, where], step, near[3])
    most = pl.ds(odd, steps - 1)
    for relation in (1, 2):
        x_copies[half_steps + relation - 1] = deliver(
            hidden_slice(relation).at[most], xbuf.at[relation, most], half_steps + relation - 1, near[relation]
        )
    for copy in x_copies.values():
        copy.start()
    w_copies = {}

    def swap_weights(chunk):
        for index, part in enumerate(weight_parts(chunk)):
            source, target = weight_refs(part)
            copy = pltpu.make_async_remote_copy(
                src_ref=source, dst_ref=target,
                send_sem=w_send.at[chunk, index], recv_sem=w_recv.at[chunk, index],
                device_id=pair, device_id_type=pl.DeviceIdType.MESH,
            )
            copy.start()
            w_copies[chunk, index] = copy

    swap_weights(0)
    kv_copies = []

    def load_cache(chunk):
        slots = pl.ds(2 * chunk, 2)
        for index, (source, target) in enumerate(((key_ref, kbuf), (value_ref, vbuf))):
            copy = pltpu.make_async_copy(source.at[:, slots], target.at[chunk], kv_sem.at[chunk, index])
            copy.start()
            kv_copies.append(copy)

    row = lax.broadcasted_iota(jnp.int32, (rows, size), 0)
    lane = lax.broadcasted_iota(jnp.int32, (rows, size), 1)
    place = row // batch
    for index in range(batch):
        place = place + jnp.where(row % batch == index, end_ref[index], 0)
    angle = place.astype(jnp.float32) * freq_ref[...]
    cosine[...] = jnp.cos(angle).reshape(steps, batch, size)
    turned_sine = jnp.sin(angle)
    sine[...] = jnp.where(lane < size // 2, -turned_sine, turned_sine).reshape(steps, batch, size)

    def send(piece, message, source, landing, target):
        copy = pltpu.make_async_remote_copy(
            src_ref=source, dst_ref=landing,
            send_sem=r_send.at[piece, message], recv_sem=r_recv.at[piece, message],
            device_id=target, device_id_type=pl.DeviceIdType.MESH,
        )
        copy.start()
        messages[piece, message] = copy

    tile = 512 if span % 512 == 0 else span

    def multiply(piece, first, count):
        group_rows = pl.ds(first, count)
        for step in range(span // tile):
            deep = pl.ds(step * tile, tile)
            part = jnp.dot(
                xbuf[group_rows, :, :, deep].reshape(count * rows, tile), wbuf[piece, deep, :],
                preferred_element_type=jnp.float32,
            ).reshape(count, steps, batch, wide)
            if step == 0:
                pbuf[piece, group_rows] = part
            else:
                pbuf[piece, group_rows] += part

    def first_hop(piece, message):
        one = 1 if piece % 2 == 0 else 2
        source = pbuf.at[piece, 3 if message == 0 else one]
        send(piece, message, source, rbuf.at[piece, message], near[one])

    lot = batch // 2

    def second_hop(piece):
        two = 2 if piece % 2 == 0 else 1
        messages[piece, 0].wait_recv()
        pbuf[piece, two] += rbuf[piece, 0]
        for part in range(2):
            some = pl.ds(part * lot, lot)
            send(piece, 2 + part, pbuf.at[piece, two, :, some], rbuf.at[piece, 2, :, some], near[two])

    def await_weights(piece):
        for index in ((0,), (1, 2))[piece % 2]:
            local_copies[piece // 2, index].wait()
            w_copies[piece // 2, index].wait_recv()

    passed = []
    for step in range(half_steps):
        x_copies[step].wait_recv()
        here = xbuf.at[3, odd * half_steps + step]
        passed.append(deliver(here, here, half_steps + 2 + step, above))
        passed[-1].start()
    for step in range(half_steps):
        there = xbuf.at[3, (1 - odd) * half_steps + step]
        deliver(there, there, half_steps + 2 + step, above).wait_recv()
    for piece in range(2):
        await_weights(piece)
    for chunk in range(1, chunks):
        swap_weights(chunk)
    for piece in range(2):
        multiply(piece, 3, 1)
        first_hop(piece, 0)
    for chunk in range(chunks):
        load_cache(chunk)
    x_own.wait()
    for relation in (1, 2):
        x_copies[half_steps + relation - 1].wait_recv()
        here = xbuf.at[relation, odd * (steps - 1)]
        passed.append(deliver(here, here, 2 * half_steps + 1 + relation, above))
        passed[-1].start()
    for relation in (1, 2):
        there = xbuf.at[relation, (1 - odd) * (steps - 1)]
        deliver(there, there, 2 * half_steps + 1 + relation, above).wait_recv()
    for piece in range(2):
        multiply(piece, 0, 3)
        first_hop(piece, 1)
    for piece in range(2, 2 * chunks):
        await_weights(piece)
        multiply(piece, 0, 4)

    def attend(chunk, lot_index):
        lines = group * steps
        some = pl.ds(lot_index * lot, lot)
        those = pl.ds(lot_index * lot * lines, lot * lines)
        turn = (cosine[:, some].reshape(steps * lot, size), sine[:, some].reshape(steps * lot, size))

        def rotated(vector):
            return vector * turn[0] + pltpu.roll(vector, size // 2, 1) * turn[1]

        new = [None, None]
        for half in range(2):
            piece = 2 * chunk + half
            if lot_index == 0:
                messages[piece, 1].wait_recv()
            messages[piece, 2 + lot_index].wait_recv()
            for block in range(blocks):
                cols = pl.ds(block * size, size)
                total = (
                    pbuf[piece, 0, :, some, cols] + rbuf[piece, 1, :, some, cols] + rbuf[piece, 2, :, some, cols]
                ).reshape(steps * lot, size)
                head = half * blocks + block
                if head == group + 1:
                    new[1] = total.astype(jnp.bfloat16)
                elif head == group:
                    new[0] = rotated(total).astype(jnp.bfloat16)
                else:
                    turned = rotated(total).astype(jnp.bfloat16).astype(jnp.float32)
                    for step in range(steps):
                        qbuf[pl.ds(lot_index * lot * lines + head * steps + step, lot, stride=lines), :] = turned[
                            step * lot : (step + 1) * lot
                        ]
        new_keys, new_values = new
        scale = size ** (-0.5)
        query = qbuf[those, :].astype(jnp.bfloat16)
        contract = (((1,), (1,)), ((), ()))
        scores = lax.dot_general(query, new_keys, contract, preferred_element_type=jnp.float32) * scale
        line = lax.broadcasted_iota(jnp.int32, scores.shape, 0)
        other = lax.broadcasted_iota(jnp.int32, scores.shape, 1)
        live = (line // lines == other % lot) & (other // lot <= line % steps)
        fresh[those, :] = jnp.where(live, scores, jnp.float32(-1e30))
        if lot_index == 0:
            kv_copies[2 * chunk].wait()
            kv_copies[2 * chunk + 1].wait()
        cache_len = 2 * half_len

        def one(index):
            here = pl.ds(pl.multiple_of(index * lines, lines), lines)
            keys = kbuf[chunk, index].reshape(cache_len, size)
            values = vbuf[chunk, index].reshape(cache_len, size)
            position = lax.broadcasted_iota(jnp.int32, (lines, cache_len), 1)
            cached = lax.dot_general(
                qbuf[here, :].astype(jnp.bfloat16), keys, contract, preferred_element_type=jnp.float32
            ) * scale
            cached = jnp.where(
                (position >= begin_ref[index]) & (position < end_ref[index]), cached, jnp.float32(-1e30)
            )
            extra = fresh[here, :]
            peak = jnp.maximum(
                jnp.max(cached, axis=1, keepdims=True), jnp.max(extra, axis=1, keepdims=True)
            )
            cached = jnp.exp(cached - peak)
            extra = jnp.exp(extra - peak)
            total = jnp.sum(cached, axis=1, keepdims=True) + jnp.sum(extra, axis=1, keepdims=True)
            weighted = jnp.dot(
                cached.astype(jnp.bfloat16), values, preferred_element_type=jnp.float32
            ) + jnp.dot(extra.astype(jnp.bfloat16), new_values, preferred_element_type=jnp.float32)
            obuf[here, :] = weighted / total

        def several(outer, carry):
            for inner in range(4):
                one(lot_index * lot + outer * 4 + inner)
            return carry

        lax.fori_loop(0, lot // 4, several, 0)

    def collect(chunk):
        lines = group * steps
        for head in range(group):
            for step in range(steps):
                abuf[chunk, step, :, pl.ds(head * size, size)] = obuf[
                    pl.ds(head * steps + step, batch, stride=lines), :
                ].astype(jnp.bfloat16)

    share = out_ref.shape[2]
    per = 4 // chunks
    out_rows = pl.ds(pl.multiple_of(sec * batch, batch), batch)

    def handoff(target):
        chunk, place = target // per, target % per
        source = abuf.at[chunk, :, :, pl.ds(place * share, share)]
        keep = pltpu.make_async_copy(source, out_ref.at[:, out_rows, :], o_local)
        copy = pltpu.make_async_remote_copy(
            src_ref=source, dst_ref=out_ref.at[:, out_rows, :],
            send_sem=o_send.at[target], recv_sem=o_recv.at[sec],
            device_id={"dp": dp, "sec": target}, device_id_type=pl.DeviceIdType.MESH,
        )
        return keep, copy

    for piece in range(2):
        second_hop(piece)
    for chunk in range(chunks):
        if chunk + 1 < chunks:
            for message in range(2):
                first_hop(2 * chunk + 2, message)
                first_hop(2 * chunk + 3, message)
            second_hop(2 * chunk + 2)
            second_hop(2 * chunk + 3)
        attend(chunk, 0)
        attend(chunk, 1)
        collect(chunk)
        for target in range(chunk * per, (chunk + 1) * per):
            keep, copy = handoff(target)
            pl.when(sec == target)(keep.start)
            pl.when(sec != target)(copy.start)

    for target in range(4):
        keep, copy = handoff(target)
        pl.when(sec == target)(keep.wait)
        pl.when(sec != target)(copy.wait_send)
        arrived = pltpu.make_async_remote_copy(
            src_ref=abuf.at[0, :, :, pl.ds(0, share)],
            dst_ref=out_ref.at[:, pl.ds(target * batch, batch), :],
            send_sem=o_send.at[target], recv_sem=o_recv.at[target],
            device_id={"dp": dp, "sec": target}, device_id_type=pl.DeviceIdType.MESH,
        )
        pl.when(sec != target)(arrived.wait_recv)
    for copy in list(x_copies.values()) + passed + list(w_copies.values()) + list(messages.values()):
        copy.wait_send()


def fused_body(hidden_states, w_query, w_keyval, key_cache, value_cache, cache_begin, cache_end):
    steps, batch, _ = hidden_states.shape
    slots, half_len, size = key_cache.shape[1:]
    depth = w_query.shape[0]
    chunks = slots // 2
    group = w_query.shape[1] // size // chunks
    rows = steps * batch
    wide = (group + 2) // 2 * size
    pieces = 2 * chunks
    share = w_query.shape[1] // 4
    lanes = np.arange(size, dtype=np.float32) % (size // 2)
    freq = np.float32(THETA) ** (-(lanes * np.float32(2.0) / np.float32(size)))
    anywhere = pl.BlockSpec(memory_space=pl.ANY)
    scalars = pl.BlockSpec(memory_space=pltpu.SMEM)
    dma = pltpu.SemaphoreType.DMA
    return pl.pallas_call(
        functools.partial(fused_kernel, group),
        out_shape=jax.ShapeDtypeStruct((steps, 4 * batch, share), jnp.bfloat16),
        in_specs=[pl.BlockSpec(memory_space=pltpu.VMEM), scalars, scalars] + [anywhere] * 5,
        out_specs=anywhere,
        scratch_shapes=[
            pltpu.VMEM((4, steps, batch, 2 * depth), jnp.bfloat16),
            pltpu.VMEM((pieces, 2 * depth, wide), jnp.bfloat16),
            pltpu.VMEM((pieces, 4, steps, batch, wide), jnp.float32),
            pltpu.VMEM((pieces, 3, steps, batch, wide), jnp.float32),
            pltpu.VMEM((chunks, batch, 2, half_len, size), jnp.bfloat16),
            pltpu.VMEM((chunks, batch, 2, half_len, size), jnp.bfloat16),
            pltpu.VMEM((steps, batch, size), jnp.float32),
            pltpu.VMEM((steps, batch, size), jnp.float32),
            pltpu.VMEM((group * rows, size), jnp.float32),
            pltpu.VMEM((group * rows, rows // 2), jnp.float32),
            pltpu.VMEM((group * rows, size), jnp.float32),
            pltpu.VMEM((chunks, steps, batch, group * size), jnp.bfloat16),
            dma, dma((2 * steps,)), dma((2 * steps,)),
            dma((chunks, 3)), dma((chunks, 3)), dma((chunks, 3)),
            dma((chunks, 2)),
            dma((pieces, 4)), dma((pieces, 4)),
            dma, dma((4,)), dma((4,)),
        ],
        compiler_params=pltpu.CompilerParams(
            collective_id=0, has_side_effects=True, vmem_limit_bytes=56 * 1024 * 1024
        ),
        cost_estimate=pl.CostEstimate(
            flops=2 * 4 * rows * 2 * depth * pieces * wide,
            bytes_accessed=2 * (w_query.size + w_keyval.size + 2 * key_cache.size),
            transcendentals=0,
        ),
    )(freq[None, :], cache_begin, cache_end, hidden_states, w_query, w_keyval, key_cache, value_cache)


def body(sizes, hidden_states, w_query, w_keyval, key_cache, value_cache, cache_begin, cache_end):
    arrays = (hidden_states, w_query, w_keyval, key_cache, value_cache, cache_begin, cache_end)
    slots = key_cache.shape[1]
    if sizes["dp"] == 2 and sizes["sec"] == 4 and sizes["tp"] % 2 == 0 and slots in (2, 4, 8):
        return fused_body(*arrays)
    return general_body(*arrays)


def solution(mesh):
    return jax.shard_map(
        functools.partial(body, mesh.shape),
        mesh=mesh,
        in_specs=(
            P(None, ("dp", "sec"), None),
            P(("dp", "sec"), "tp"),
            P(("dp", "sec"), "tp"),
            P(("dp", "sec"), "tp", None, None),
            P(("dp", "sec"), "tp", None, None),
            P(("dp", "sec")),
            P(("dp", "sec")),
        ),
        out_specs=P(None, "dp", ("tp", "sec")),
        check_vma=False,
    )
```

```python
import functools

import jax
import jax.numpy as jnp
import numpy as np
from jax import lax
from jax.experimental import pallas as pl
from jax.experimental.pallas import tpu as pltpu
from jax.sharding import PartitionSpec as P

THETA = 500000.0


def swapped(value, axis, stride):
    mask = 2**stride
    pairs = [(source, source ^ mask) for source in range(lax.axis_size(axis))]
    return lax.ppermute(value, axis, pairs)


def rotate(vector, positions):
    half = vector.shape[-1] // 2
    freq = THETA ** (-(jnp.arange(half, dtype=jnp.float32) * 2.0 / vector.shape[-1]))
    angle = positions[..., None] * freq
    angle = angle.reshape(positions.shape + (1,) * (vector.ndim - positions.ndim - 1) + (half,))
    cosine = jnp.cos(angle)
    sine = jnp.sin(angle)
    first = vector[..., :half]
    second = vector[..., half:]
    return jnp.concatenate(
        [first * cosine - second * sine, second * cosine + first * sine], axis=-1
    )


def make_accumulate(token_rows, pieces):
    return (
        jnp.dot(token_rows, pieces[0], preferred_element_type=jnp.float32),
        jnp.dot(token_rows, pieces[1], preferred_element_type=jnp.float32),
    )


def partial_attention(query, keys, values, live, score_scale):
    scores = (
        jnp.einsum("sbkgd,bkpd->sbkgp", query, keys, preferred_element_type=jnp.float32)
        * score_scale
    )
    live = jnp.broadcast_to(live, scores.shape)
    masked = jnp.where(live, scores, jnp.float32(-1e30))
    maxima = jnp.max(masked, axis=-1)
    expo = jnp.where(live, jnp.exp(masked - maxima[..., None]), jnp.float32(0.0))
    totals = jnp.sum(expo, axis=-1)
    weighted = jnp.einsum(
        "sbkgp,bkpd->sbkgd", expo.astype(jnp.bfloat16), values, preferred_element_type=jnp.float32
    )
    return (maxima, totals, weighted)


def merge_parts(parts):
    overall = parts[0][0]
    for entry in parts[1:]:
        overall = jnp.maximum(overall, entry[0])
    weighted = jnp.zeros_like(parts[0][2])
    totals = jnp.zeros_like(parts[0][1])
    for entry in parts:
        factor = jnp.exp(entry[0] - overall)
        weighted = weighted + entry[2] * factor[..., None]
        totals = totals + entry[1] * factor
    return weighted / totals[..., None]


def general_body(hidden_states, w_query, w_keyval, key_cache, value_cache, cache_begin, cache_end):
    num_steps, batch_rows, width = hidden_states.shape
    head_size = key_cache.shape[-1]
    query_cols = w_query.shape[1]
    keyval_cols = w_keyval.shape[1]
    local_heads = query_cols // head_size
    slot_count = key_cache.shape[1]
    half_len = key_cache.shape[2]
    score_scale = head_size ** (-0.5)
    sec_count = lax.axis_size("sec")
    sec_index = lax.axis_index("sec")
    sec_group = lax.all_gather(hidden_states, "sec", axis=1, tiled=True)
    shard_rows = w_query.shape[0]
    dp_count = width // (sec_count * shard_rows)
    group_rows = num_steps * batch_rows * sec_count
    grouped = sec_group.reshape(group_rows, dp_count, sec_count, shard_rows)
    chosen = lax.dynamic_slice_in_dim(grouped, sec_index, 1, 2).reshape(
        group_rows, dp_count * shard_rows
    )
    query_all, keyval_all = make_accumulate(
        chosen,
        (
            lax.all_gather(w_query, "dp", axis=0, tiled=True),
            lax.all_gather(w_keyval, "dp", axis=0, tiled=True),
        ),
    )
    query_acc, keyval_acc = (
        lax.psum_scatter(
            query_all.reshape(num_steps, sec_count * batch_rows, query_cols),
            "sec",
            scatter_dimension=1,
            tiled=True,
        ),
        lax.psum_scatter(
            keyval_all.reshape(num_steps, sec_count * batch_rows, keyval_cols),
            "sec",
            scatter_dimension=1,
            tiled=True,
        ),
    )
    query_acc = query_acc.reshape(num_steps * batch_rows, query_cols)
    keyval_acc = keyval_acc.reshape(num_steps * batch_rows, keyval_cols)
    positions = (
        cache_end.astype(jnp.float32)[None, :] + jnp.arange(num_steps, dtype=jnp.float32)[:, None]
    )
    query = rotate(
        query_acc.reshape(num_steps, batch_rows, local_heads, head_size), positions
    ).astype(jnp.bfloat16)
    step_ids = jnp.arange(num_steps, dtype=jnp.int32)
    causal = step_ids[None, :] <= step_ids[:, None]
    if slot_count == 1:
        parity = lax.axis_index("tp") % 2
        own_proj = keyval_acc.reshape(num_steps, batch_rows, head_size)
        own_proj = jnp.where(parity == 0, rotate(own_proj, positions), own_proj).astype(
            jnp.bfloat16
        )
        partner_query, partner_proj = swapped((query, own_proj), "tp", 0)
        new_keys = jnp.where(parity == 0, own_proj, partner_proj)
        new_values = jnp.where(parity == 0, partner_proj, own_proj)
        lower_heads = jnp.where(parity == 0, query, partner_query)
        upper_heads = jnp.where(parity == 0, partner_query, query)
        both_heads = jnp.concatenate([lower_heads, upper_heads], axis=2)[:, :, None]
        cache_pos = parity * half_len + jnp.arange(half_len, dtype=jnp.int32)
        cache_live = (cache_pos[None, :] >= cache_begin[:, None]) & (
            cache_pos[None, :] < cache_end[:, None]
        )
        cache_part = partial_attention(
            both_heads, key_cache, value_cache, cache_live[None, :, None, None, :], score_scale
        )
        mine_start = parity * local_heads
        theirs_start = (1 - parity) * local_heads

        def select_heads(array, start):
            return lax.dynamic_slice_in_dim(array, start, local_heads, 3)

        returned = (
            swapped(select_heads(cache_part[0], theirs_start).astype(jnp.bfloat16), "tp", 0).astype(
                jnp.float32
            ),
            swapped(select_heads(cache_part[1], theirs_start).astype(jnp.bfloat16), "tp", 0).astype(
                jnp.float32
            ),
            swapped(select_heads(cache_part[2], theirs_start).astype(jnp.bfloat16), "tp", 0).astype(
                jnp.float32
            ),
        )
        own_part = (
            select_heads(cache_part[0], mine_start),
            select_heads(cache_part[1], mine_start),
            select_heads(cache_part[2], mine_start),
        )
        fresh_part = partial_attention(
            query[:, :, None],
            jnp.transpose(new_keys, (1, 0, 2))[:, None],
            jnp.transpose(new_values, (1, 0, 2))[:, None],
            causal[:, None, None, None, :],
            score_scale,
        )
        parts = [own_part, returned, fresh_part]
    else:
        local_kv = keyval_cols // (2 * head_size)
        keyval = keyval_acc.reshape(num_steps, batch_rows, local_kv, 2, head_size)
        new_keys = rotate(keyval[:, :, :, 0], positions).astype(jnp.bfloat16)
        new_values = keyval[:, :, :, 1].astype(jnp.bfloat16)
        whole_keys = key_cache.reshape(batch_rows, local_kv, 2 * half_len, head_size)
        whole_values = value_cache.reshape(batch_rows, local_kv, 2 * half_len, head_size)
        grouped_query = query.reshape(
            num_steps, batch_rows, local_kv, local_heads // local_kv, head_size
        )
        cache_pos = jnp.arange(2 * half_len, dtype=jnp.int32)
        cache_live = (cache_pos[None, :] >= cache_begin[:, None]) & (
            cache_pos[None, :] < cache_end[:, None]
        )
        cache_part = partial_attention(
            grouped_query, whole_keys, whole_values, cache_live[None, :, None, None, :], score_scale
        )
        fresh_part = partial_attention(
            grouped_query,
            jnp.transpose(new_keys, (1, 2, 0, 3)),
            jnp.transpose(new_values, (1, 2, 0, 3)),
            causal[:, None, None, None, :],
            score_scale,
        )
        parts = [cache_part, fresh_part]
    attended = (
        merge_parts(parts)
        .astype(jnp.bfloat16)
        .reshape(num_steps, batch_rows, local_heads * head_size)
    )
    return lax.all_to_all(attended, "sec", split_axis=2, concat_axis=1, tiled=True)


def fused_kernel(
    group, freq_ref, begin_ref, end_ref, hidden_ref, wq_ref, wkv_ref, key_ref, value_ref, out_ref,
    xbuf, wbuf, pbuf, rbuf, kbuf, vbuf, cosine, sine, qbuf, fresh, obuf, abuf,
    x_local, x_send, x_recv, w_local, w_send, w_recv, kv_sem, r_send, r_recv, o_local, o_send, o_recv,
):
    chunks = wkv_ref.shape[1] // (2 * key_ref.shape[3])
    steps, batch, _ = hidden_ref.shape
    size = key_ref.shape[3]
    depth = wq_ref.shape[0]
    span = 2 * depth
    rows = steps * batch
    half_len = key_ref.shape[2]
    blocks = (group + 2) // 2
    wide = blocks * size
    dp, sec = lax.axis_index("dp"), lax.axis_index("sec")
    core = sec % 2
    dp_other = 1 - dp
    sec_far = (sec + 2) % 4
    sec_pair = sec + 1 - 2 * core
    near = ({"dp": dp, "sec": sec}, {"dp": dp_other, "sec": sec}, {"dp": dp, "sec": sec_far}, {"dp": dp_other, "sec": sec_far})
    pair = {"dp": dp, "sec": sec_pair}
    cross = {"dp": dp, "sec": (sec_pair + 2) % 4}
    odd = lax.axis_index("tp") % 2
    above = {"tp": lax.axis_index("tp") + 1 - 2 * odd}
    chips = (dp * 2 + sec // 2, dp_other * 2 + sec // 2, dp * 2 + sec_far // 2, dp_other * 2 + sec_far // 2)

    def weight_parts(chunk):
        first = chunk * group * size
        return (
            (2 * chunk, 0, wide, wq_ref, first),
            (2 * chunk + 1, 0, group * size - wide, wq_ref, first + wide),
            (2 * chunk + 1, group * size - wide, 2 * size, wkv_ref, chunk * 2 * size),
        )

    own_rows = pl.ds(pl.multiple_of(core * depth, depth), depth)

    def weight_refs(part):
        piece, start, width, source, column = part
        return (
            source.at[:, pl.ds(column, width)],
            wbuf.at[piece, own_rows, pl.ds(start, width)],
        )

    def hidden_slice(relation):
        return hidden_ref.at[:, :, pl.ds(pl.multiple_of(chips[relation] * span, span), span)]

    local_copies = {}
    x_own = pltpu.make_async_copy(hidden_slice(0), xbuf.at[0], x_local)
    x_own.start()
    for chunk in range(chunks):
        for index, part in enumerate(weight_parts(chunk)):
            source, target = weight_refs(part)
            copy = pltpu.make_async_copy(source, target, w_local.at[chunk, index])
            copy.start()
            local_copies[chunk, index] = copy

    barrier = pltpu.get_barrier_semaphore()
    for peer in near[1:] + (pair, cross, above):
        pl.semaphore_signal(barrier, inc=1, device_id=peer, device_id_type=pl.DeviceIdType.MESH)
    pl.semaphore_wait(barrier, 6)

    def deliver(source, target, index, device):
        return pltpu.make_async_remote_copy(
            src_ref=source, dst_ref=target, send_sem=x_send.at[index], recv_sem=x_recv.at[index],
            device_id=device, device_id_type=pl.DeviceIdType.MESH,
        )

    half_steps = steps // 2
    x_copies = []
    for step in range(half_steps):
        where = odd * half_steps + step
        x_copies.append(deliver(hidden_slice(3).at[where], xbuf.at[3, where], step, near[3]))
    for relation in (1, 2):
        x_copies.append(
            deliver(hidden_slice(relation), xbuf.at[relation], half_steps + relation - 1, near[relation])
        )
    for copy in x_copies:
        copy.start()
    w_copies = {}
    for chunk in range(chunks):
        for index, part in enumerate(weight_parts(chunk)):
            source, target = weight_refs(part)
            copy = pltpu.make_async_remote_copy(
                src_ref=source, dst_ref=target,
                send_sem=w_send.at[chunk, index], recv_sem=w_recv.at[chunk, index],
                device_id=pair, device_id_type=pl.DeviceIdType.MESH,
            )
            copy.start()
            w_copies[chunk, index] = copy
    kv_copies = []
    for chunk in range(chunks):
        slots = pl.ds(2 * chunk, 2)
        for index, (source, target) in enumerate(((key_ref, kbuf), (value_ref, vbuf))):
            copy = pltpu.make_async_copy(source.at[:, slots], target.at[chunk], kv_sem.at[chunk, index])
            copy.start()
            kv_copies.append(copy)

    row = lax.broadcasted_iota(jnp.int32, (rows, size), 0)
    lane = lax.broadcasted_iota(jnp.int32, (rows, size), 1)
    place = row // batch
    for index in range(batch):
        place = place + jnp.where(row % batch == index, end_ref[index], 0)
    angle = place.astype(jnp.float32) * freq_ref[...]
    cosine[...] = jnp.cos(angle)
    sine[...] = jnp.where(lane < size // 2, -jnp.sin(angle), jnp.sin(angle))

    def rotated(vector):
        return vector * cosine[...] + pltpu.roll(vector, size // 2, 1) * sine[...]

    def send(piece, message, source, target):
        copy = pltpu.make_async_remote_copy(
            src_ref=source, dst_ref=rbuf.at[piece, message],
            send_sem=r_send.at[piece, message], recv_sem=r_recv.at[piece, message],
            device_id=target, device_id_type=pl.DeviceIdType.MESH,
        )
        copy.start()
        return copy

    tile = 512 if span % 512 == 0 else span

    def multiply(piece, first, count):
        group_rows = pl.ds(first, count)
        for step in range(span // tile):
            deep = pl.ds(step * tile, tile)
            part = jnp.dot(
                xbuf[group_rows, :, :, deep].reshape(count * rows, tile), wbuf[piece, deep, :],
                preferred_element_type=jnp.float32,
            ).reshape(count, rows, wide)
            if step == 0:
                pbuf[piece, group_rows] = part
            else:
                pbuf[piece, group_rows] += part

    messages = {}

    def first_hop(piece, message):
        one = 1 if piece % 2 == 0 else 2
        source = pbuf.at[piece, 3 if message == 0 else one]
        messages[piece, message] = send(piece, message, source, near[one])

    def second_hop(piece):
        two = 2 if piece % 2 == 0 else 1
        messages[piece, 0].wait_recv()
        pbuf[piece, two] += rbuf[piece, 0]
        messages[piece, 2] = send(piece, 2, pbuf.at[piece, two], near[two])

    def await_weights(piece):
        for index in ((0,), (1, 2))[piece % 2]:
            local_copies[piece // 2, index].wait()
            w_copies[piece // 2, index].wait_recv()

    passed = []
    for step in range(half_steps):
        x_copies[step].wait_recv()
        here = xbuf.at[3, odd * half_steps + step]
        passed.append(deliver(here, here, half_steps + 2 + step, above))
        passed[-1].start()
    for step in range(half_steps):
        there = xbuf.at[3, (1 - odd) * half_steps + step]
        deliver(there, there, half_steps + 2 + step, above).wait_recv()
    for piece in range(2):
        await_weights(piece)
        multiply(piece, 3, 1)
        first_hop(piece, 0)
    x_own.wait()
    for copy in x_copies[half_steps:]:
        copy.wait_recv()
    for piece in range(2):
        multiply(piece, 0, 3)
        first_hop(piece, 1)
    def attend(chunk):
        new = [None, None]
        for half in range(2):
            piece = 2 * chunk + half
            messages[piece, 1].wait_recv()
            messages[piece, 2].wait_recv()
            for block in range(blocks):
                cols = pl.ds(block * size, size)
                total = pbuf[piece, 0, :, cols] + rbuf[piece, 1, :, cols] + rbuf[piece, 2, :, cols]
                head = half * blocks + block
                if head == group + 1:
                    new[1] = total.astype(jnp.bfloat16)
                elif head == group:
                    new[0] = rotated(total).astype(jnp.bfloat16)
                else:
                    turned = rotated(total).astype(jnp.bfloat16).astype(jnp.float32)
                    for step in range(steps):
                        qbuf[pl.ds(head * steps + step, batch, stride=group * steps), :] = turned[
                            step * batch : (step + 1) * batch
                        ]
        new_keys, new_values = new
        lines = group * steps
        scale = size ** (-0.5)
        query = qbuf[...].astype(jnp.bfloat16)
        contract = (((1,), (1,)), ((), ()))
        scores = lax.dot_general(query, new_keys, contract, preferred_element_type=jnp.float32) * scale
        line = lax.broadcasted_iota(jnp.int32, scores.shape, 0)
        other = lax.broadcasted_iota(jnp.int32, scores.shape, 1)
        live = (line // lines == other % batch) & (other // batch <= line % steps)
        fresh[...] = jnp.where(live, scores, jnp.float32(-1e30))
        kv_copies[2 * chunk].wait()
        kv_copies[2 * chunk + 1].wait()
        cache_len = 2 * half_len

        def one(index):
            here = pl.ds(pl.multiple_of(index * lines, lines), lines)
            keys = kbuf[chunk, index].reshape(cache_len, size)
            values = vbuf[chunk, index].reshape(cache_len, size)
            position = lax.broadcasted_iota(jnp.int32, (lines, cache_len), 1)
            cached = lax.dot_general(
                qbuf[here, :].astype(jnp.bfloat16), keys, contract, preferred_element_type=jnp.float32
            ) * scale
            cached = jnp.where(
                (position >= begin_ref[index]) & (position < end_ref[index]), cached, jnp.float32(-1e30)
            )
            extra = fresh[here, :]
            peak = jnp.maximum(
                jnp.max(cached, axis=1, keepdims=True), jnp.max(extra, axis=1, keepdims=True)
            )
            cached = jnp.exp(cached - peak)
            extra = jnp.exp(extra - peak)
            total = jnp.sum(cached, axis=1, keepdims=True) + jnp.sum(extra, axis=1, keepdims=True)
            weighted = jnp.dot(
                cached.astype(jnp.bfloat16), values, preferred_element_type=jnp.float32
            ) + jnp.dot(extra.astype(jnp.bfloat16), new_values, preferred_element_type=jnp.float32)
            obuf[here, :] = weighted / total

        unroll = 8 if batch % 8 == 0 else 1

        def several(outer, carry):
            for inner in range(unroll):
                one(outer * unroll + inner)
            return carry

        lax.fori_loop(0, batch // unroll, several, 0)
        for head in range(group):
            for step in range(steps):
                abuf[chunk, step, :, pl.ds(head * size, size)] = obuf[
                    pl.ds(head * steps + step, batch, stride=lines), :
                ].astype(jnp.bfloat16)

    share = out_ref.shape[2]
    per = 4 // chunks
    out_rows = pl.ds(pl.multiple_of(sec * batch, batch), batch)

    def handoff(target):
        chunk, place = target // per, target % per
        source = abuf.at[chunk, :, :, pl.ds(place * share, share)]
        keep = pltpu.make_async_copy(source, out_ref.at[:, out_rows, :], o_local)
        copy = pltpu.make_async_remote_copy(
            src_ref=source, dst_ref=out_ref.at[:, out_rows, :],
            send_sem=o_send.at[target], recv_sem=o_recv.at[sec],
            device_id={"dp": dp, "sec": target}, device_id_type=pl.DeviceIdType.MESH,
        )
        return keep, copy

    for piece in range(2):
        second_hop(piece)
    for chunk in range(chunks):
        if chunk + 1 < chunks:
            for piece in (2 * chunk + 2, 2 * chunk + 3):
                await_weights(piece)
                multiply(piece, 0, 4)
                first_hop(piece, 0)
                first_hop(piece, 1)
            second_hop(2 * chunk + 2)
            second_hop(2 * chunk + 3)
        attend(chunk)
        for target in range(chunk * per, (chunk + 1) * per):
            keep, copy = handoff(target)
            pl.when(sec == target)(keep.start)
            pl.when(sec != target)(copy.start)

    for target in range(4):
        keep, copy = handoff(target)
        pl.when(sec == target)(keep.wait)
        pl.when(sec != target)(copy.wait_send)
        arrived = pltpu.make_async_remote_copy(
            src_ref=abuf.at[0, :, :, pl.ds(0, share)],
            dst_ref=out_ref.at[:, pl.ds(target * batch, batch), :],
            send_sem=o_send.at[target], recv_sem=o_recv.at[target],
            device_id={"dp": dp, "sec": target}, device_id_type=pl.DeviceIdType.MESH,
        )
        pl.when(sec != target)(arrived.wait_recv)
    for copy in x_copies + passed + list(w_copies.values()) + list(messages.values()):
        copy.wait_send()


def fused_body(hidden_states, w_query, w_keyval, key_cache, value_cache, cache_begin, cache_end):
    steps, batch, _ = hidden_states.shape
    slots, half_len, size = key_cache.shape[1:]
    depth = w_query.shape[0]
    chunks = slots // 2
    group = w_query.shape[1] // size // chunks
    rows = steps * batch
    wide = (group + 2) // 2 * size
    pieces = 2 * chunks
    share = w_query.shape[1] // 4
    lanes = np.arange(size, dtype=np.float32) % (size // 2)
    freq = np.float32(THETA) ** (-(lanes * np.float32(2.0) / np.float32(size)))
    anywhere = pl.BlockSpec(memory_space=pl.ANY)
    scalars = pl.BlockSpec(memory_space=pltpu.SMEM)
    dma = pltpu.SemaphoreType.DMA
    return pl.pallas_call(
        functools.partial(fused_kernel, group),
        out_shape=jax.ShapeDtypeStruct((steps, 4 * batch, share), jnp.bfloat16),
        in_specs=[pl.BlockSpec(memory_space=pltpu.VMEM), scalars, scalars] + [anywhere] * 5,
        out_specs=anywhere,
        scratch_shapes=[
            pltpu.VMEM((4, steps, batch, 2 * depth), jnp.bfloat16),
            pltpu.VMEM((pieces, 2 * depth, wide), jnp.bfloat16),
            pltpu.VMEM((pieces, 4, rows, wide), jnp.float32),
            pltpu.VMEM((pieces, 3, rows, wide), jnp.float32),
            pltpu.VMEM((chunks, batch, 2, half_len, size), jnp.bfloat16),
            pltpu.VMEM((chunks, batch, 2, half_len, size), jnp.bfloat16),
            pltpu.VMEM((rows, size), jnp.float32),
            pltpu.VMEM((rows, size), jnp.float32),
            pltpu.VMEM((group * rows, size), jnp.float32),
            pltpu.VMEM((group * rows, rows), jnp.float32),
            pltpu.VMEM((group * rows, size), jnp.float32),
            pltpu.VMEM((chunks, steps, batch, group * size), jnp.bfloat16),
            dma, dma((steps + 2,)), dma((steps + 2,)),
            dma((chunks, 3)), dma((chunks, 3)), dma((chunks, 3)),
            dma((chunks, 2)),
            dma((pieces, 3)), dma((pieces, 3)),
            dma, dma((4,)), dma((4,)),
        ],
        compiler_params=pltpu.CompilerParams(
            collective_id=0, has_side_effects=True, vmem_limit_bytes=56 * 1024 * 1024
        ),
        cost_estimate=pl.CostEstimate(
            flops=2 * 4 * rows * 2 * depth * pieces * wide,
            bytes_accessed=2 * (w_query.size + w_keyval.size + 2 * key_cache.size),
            transcendentals=0,
        ),
    )(freq[None, :], cache_begin, cache_end, hidden_states, w_query, w_keyval, key_cache, value_cache)


def body(sizes, hidden_states, w_query, w_keyval, key_cache, value_cache, cache_begin, cache_end):
    arrays = (hidden_states, w_query, w_keyval, key_cache, value_cache, cache_begin, cache_end)
    slots = key_cache.shape[1]
    if sizes["dp"] == 2 and sizes["sec"] == 4 and sizes["tp"] % 2 == 0 and slots in (2, 4, 8):
        return fused_body(*arrays)
    return general_body(*arrays)


def solution(mesh):
    return jax.shard_map(
        functools.partial(body, mesh.shape),
        mesh=mesh,
        in_specs=(
            P(None, ("dp", "sec"), None),
            P(("dp", "sec"), "tp"),
            P(("dp", "sec"), "tp"),
            P(("dp", "sec"), "tp", None, None),
            P(("dp", "sec"), "tp", None, None),
            P(("dp", "sec")),
            P(("dp", "sec")),
        ),
        out_specs=P(None, "dp", ("tp", "sec")),
        check_vma=False,
    )
```

```python
import functools

import jax
import jax.numpy as jnp
import numpy as np
from jax import lax
from jax.experimental import pallas as pl
from jax.experimental.pallas import tpu as pltpu
from jax.sharding import PartitionSpec as P

THETA = 500000.0


def swapped(value, axis, stride):
    mask = 2**stride
    pairs = [(source, source ^ mask) for source in range(lax.axis_size(axis))]
    return lax.ppermute(value, axis, pairs)


def rotate(vector, positions):
    half = vector.shape[-1] // 2
    freq = THETA ** (-(jnp.arange(half, dtype=jnp.float32) * 2.0 / vector.shape[-1]))
    angle = positions[..., None] * freq
    angle = angle.reshape(positions.shape + (1,) * (vector.ndim - positions.ndim - 1) + (half,))
    cosine = jnp.cos(angle)
    sine = jnp.sin(angle)
    first = vector[..., :half]
    second = vector[..., half:]
    return jnp.concatenate(
        [first * cosine - second * sine, second * cosine + first * sine], axis=-1
    )


def make_accumulate(token_rows, pieces):
    return (
        jnp.dot(token_rows, pieces[0], preferred_element_type=jnp.float32),
        jnp.dot(token_rows, pieces[1], preferred_element_type=jnp.float32),
    )


def partial_attention(query, keys, values, live, score_scale):
    scores = (
        jnp.einsum("sbkgd,bkpd->sbkgp", query, keys, preferred_element_type=jnp.float32)
        * score_scale
    )
    live = jnp.broadcast_to(live, scores.shape)
    masked = jnp.where(live, scores, jnp.float32(-1e30))
    maxima = jnp.max(masked, axis=-1)
    expo = jnp.where(live, jnp.exp(masked - maxima[..., None]), jnp.float32(0.0))
    totals = jnp.sum(expo, axis=-1)
    weighted = jnp.einsum(
        "sbkgp,bkpd->sbkgd", expo.astype(jnp.bfloat16), values, preferred_element_type=jnp.float32
    )
    return (maxima, totals, weighted)


def merge_parts(parts):
    overall = parts[0][0]
    for entry in parts[1:]:
        overall = jnp.maximum(overall, entry[0])
    weighted = jnp.zeros_like(parts[0][2])
    totals = jnp.zeros_like(parts[0][1])
    for entry in parts:
        factor = jnp.exp(entry[0] - overall)
        weighted = weighted + entry[2] * factor[..., None]
        totals = totals + entry[1] * factor
    return weighted / totals[..., None]


def general_body(hidden_states, w_query, w_keyval, key_cache, value_cache, cache_begin, cache_end):
    num_steps, batch_rows, width = hidden_states.shape
    head_size = key_cache.shape[-1]
    query_cols = w_query.shape[1]
    keyval_cols = w_keyval.shape[1]
    local_heads = query_cols // head_size
    slot_count = key_cache.shape[1]
    half_len = key_cache.shape[2]
    score_scale = head_size ** (-0.5)
    sec_count = lax.axis_size("sec")
    sec_index = lax.axis_index("sec")
    sec_group = lax.all_gather(hidden_states, "sec", axis=1, tiled=True)
    shard_rows = w_query.shape[0]
    dp_count = width // (sec_count * shard_rows)
    group_rows = num_steps * batch_rows * sec_count
    grouped = sec_group.reshape(group_rows, dp_count, sec_count, shard_rows)
    chosen = lax.dynamic_slice_in_dim(grouped, sec_index, 1, 2).reshape(
        group_rows, dp_count * shard_rows
    )
    query_all, keyval_all = make_accumulate(
        chosen,
        (
            lax.all_gather(w_query, "dp", axis=0, tiled=True),
            lax.all_gather(w_keyval, "dp", axis=0, tiled=True),
        ),
    )
    query_acc, keyval_acc = (
        lax.psum_scatter(
            query_all.reshape(num_steps, sec_count * batch_rows, query_cols),
            "sec",
            scatter_dimension=1,
            tiled=True,
        ),
        lax.psum_scatter(
            keyval_all.reshape(num_steps, sec_count * batch_rows, keyval_cols),
            "sec",
            scatter_dimension=1,
            tiled=True,
        ),
    )
    query_acc = query_acc.reshape(num_steps * batch_rows, query_cols)
    keyval_acc = keyval_acc.reshape(num_steps * batch_rows, keyval_cols)
    positions = (
        cache_end.astype(jnp.float32)[None, :] + jnp.arange(num_steps, dtype=jnp.float32)[:, None]
    )
    query = rotate(
        query_acc.reshape(num_steps, batch_rows, local_heads, head_size), positions
    ).astype(jnp.bfloat16)
    step_ids = jnp.arange(num_steps, dtype=jnp.int32)
    causal = step_ids[None, :] <= step_ids[:, None]
    if slot_count == 1:
        parity = lax.axis_index("tp") % 2
        own_proj = keyval_acc.reshape(num_steps, batch_rows, head_size)
        own_proj = jnp.where(parity == 0, rotate(own_proj, positions), own_proj).astype(
            jnp.bfloat16
        )
        partner_query, partner_proj = swapped((query, own_proj), "tp", 0)
        new_keys = jnp.where(parity == 0, own_proj, partner_proj)
        new_values = jnp.where(parity == 0, partner_proj, own_proj)
        lower_heads = jnp.where(parity == 0, query, partner_query)
        upper_heads = jnp.where(parity == 0, partner_query, query)
        both_heads = jnp.concatenate([lower_heads, upper_heads], axis=2)[:, :, None]
        cache_pos = parity * half_len + jnp.arange(half_len, dtype=jnp.int32)
        cache_live = (cache_pos[None, :] >= cache_begin[:, None]) & (
            cache_pos[None, :] < cache_end[:, None]
        )
        cache_part = partial_attention(
            both_heads, key_cache, value_cache, cache_live[None, :, None, None, :], score_scale
        )
        mine_start = parity * local_heads
        theirs_start = (1 - parity) * local_heads

        def select_heads(array, start):
            return lax.dynamic_slice_in_dim(array, start, local_heads, 3)

        returned = (
            swapped(select_heads(cache_part[0], theirs_start).astype(jnp.bfloat16), "tp", 0).astype(
                jnp.float32
            ),
            swapped(select_heads(cache_part[1], theirs_start).astype(jnp.bfloat16), "tp", 0).astype(
                jnp.float32
            ),
            swapped(select_heads(cache_part[2], theirs_start).astype(jnp.bfloat16), "tp", 0).astype(
                jnp.float32
            ),
        )
        own_part = (
            select_heads(cache_part[0], mine_start),
            select_heads(cache_part[1], mine_start),
            select_heads(cache_part[2], mine_start),
        )
        fresh_part = partial_attention(
            query[:, :, None],
            jnp.transpose(new_keys, (1, 0, 2))[:, None],
            jnp.transpose(new_values, (1, 0, 2))[:, None],
            causal[:, None, None, None, :],
            score_scale,
        )
        parts = [own_part, returned, fresh_part]
    else:
        local_kv = keyval_cols // (2 * head_size)
        keyval = keyval_acc.reshape(num_steps, batch_rows, local_kv, 2, head_size)
        new_keys = rotate(keyval[:, :, :, 0], positions).astype(jnp.bfloat16)
        new_values = keyval[:, :, :, 1].astype(jnp.bfloat16)
        whole_keys = key_cache.reshape(batch_rows, local_kv, 2 * half_len, head_size)
        whole_values = value_cache.reshape(batch_rows, local_kv, 2 * half_len, head_size)
        grouped_query = query.reshape(
            num_steps, batch_rows, local_kv, local_heads // local_kv, head_size
        )
        cache_pos = jnp.arange(2 * half_len, dtype=jnp.int32)
        cache_live = (cache_pos[None, :] >= cache_begin[:, None]) & (
            cache_pos[None, :] < cache_end[:, None]
        )
        cache_part = partial_attention(
            grouped_query, whole_keys, whole_values, cache_live[None, :, None, None, :], score_scale
        )
        fresh_part = partial_attention(
            grouped_query,
            jnp.transpose(new_keys, (1, 2, 0, 3)),
            jnp.transpose(new_values, (1, 2, 0, 3)),
            causal[:, None, None, None, :],
            score_scale,
        )
        parts = [cache_part, fresh_part]
    attended = (
        merge_parts(parts)
        .astype(jnp.bfloat16)
        .reshape(num_steps, batch_rows, local_heads * head_size)
    )
    return lax.all_to_all(attended, "sec", split_axis=2, concat_axis=1, tiled=True)


def fused_kernel(
    group, freq_ref, begin_ref, end_ref, hidden_ref, wq_ref, wkv_ref, key_ref, value_ref, out_ref,
    xbuf, wbuf, pbuf, gbuf, sbuf, rbuf, kbuf, vbuf, cosine, sine, qbuf, fresh, obuf, abuf,
    x_local, x_send, x_recv, w_local, s_send, s_recv, kv_sem, r_send, r_recv, o_local, o_send, o_recv,
):
    chunks = wkv_ref.shape[1] // (2 * key_ref.shape[3])
    steps, batch, _ = hidden_ref.shape
    size = key_ref.shape[3]
    depth = wq_ref.shape[0]
    rows = steps * batch
    half_len = key_ref.shape[2]
    blocks = (group + 2) // 2
    wide = blocks * size
    dp, sec = lax.axis_index("dp"), lax.axis_index("sec")
    core = sec % 2
    dp_other = 1 - dp
    sec_far = (sec + 2) % 4
    sec_pair = sec + 1 - 2 * core
    near = ({"dp": dp, "sec": sec}, {"dp": dp_other, "sec": sec}, {"dp": dp, "sec": sec_far}, {"dp": dp_other, "sec": sec_far})
    dp_at = (dp, dp_other, dp, dp_other)
    sec_at = (sec, sec, sec_far, sec_far)
    sec_across = (sec_pair, sec_pair, (sec_pair + 2) % 4, (sec_pair + 2) % 4)
    places = tuple(zip(dp_at + dp_at, sec_at + sec_across))
    everyone = tuple({"dp": one, "sec": two} for one, two in places)
    pair = everyone[4]
    odd = lax.axis_index("tp") % 2
    above = {"tp": lax.axis_index("tp") + 1 - 2 * odd}

    def weight_parts(chunk):
        first = chunk * group * size
        return (
            (2 * chunk, 0, wide, wq_ref, first),
            (2 * chunk + 1, 0, group * size - wide, wq_ref, first + wide),
            (2 * chunk + 1, group * size - wide, 2 * size, wkv_ref, chunk * 2 * size),
        )

    def weight_refs(part):
        piece, start, width, source, column = part
        return (
            source.at[:, pl.ds(column, width)],
            wbuf.at[piece, :, pl.ds(start, width)],
        )

    def hidden_slice(relation):
        block = places[relation][0] * 4 + places[relation][1]
        return hidden_ref.at[:, :, pl.ds(pl.multiple_of(block * depth, depth), depth)]

    local_copies = {}
    x_own = pltpu.make_async_copy(hidden_slice(0), xbuf.at[0], x_local)
    x_own.start()
    for chunk in range(chunks):
        for index, part in enumerate(weight_parts(chunk)):
            source, target = weight_refs(part)
            copy = pltpu.make_async_copy(source, target, w_local.at[chunk, index])
            copy.start()
            local_copies[chunk, index] = copy

    barrier = pltpu.get_barrier_semaphore()
    for peer in everyone[1:] + (above,):
        pl.semaphore_signal(barrier, inc=1, device_id=peer, device_id_type=pl.DeviceIdType.MESH)
    pl.semaphore_wait(barrier, 8)

    def deliver(source, target, index, device):
        return pltpu.make_async_remote_copy(
            src_ref=source, dst_ref=target, send_sem=x_send.at[index], recv_sem=x_recv.at[index],
            device_id=device, device_id_type=pl.DeviceIdType.MESH,
        )

    def deliver(source, target, index, device):
        return pltpu.make_async_remote_copy(
            src_ref=source, dst_ref=target, send_sem=x_send.at[index], recv_sem=x_recv.at[index],
            device_id=device, device_id_type=pl.DeviceIdType.MESH,
        )

    half_steps = steps // 2
    mine = pl.ds(odd * half_steps, half_steps)
    theirs = pl.ds((1 - odd) * half_steps, half_steps)
    x_copies = {}
    for relation in (7, 3, 5, 6, 1, 2, 4):
        source, target = hidden_slice(relation), xbuf.at[relation]
        if relation % 4 == 3:
            source, target = source.at[mine], target.at[mine]
        x_copies[relation] = deliver(source, target, relation, everyone[relation])
        x_copies[relation].start()
    kv_copies = []
    for chunk in range(chunks):
        slots = pl.ds(2 * chunk, 2)
        for index, (source, target) in enumerate(((key_ref, kbuf), (value_ref, vbuf))):
            copy = pltpu.make_async_copy(source.at[:, slots], target.at[chunk], kv_sem.at[chunk, index])
            copy.start()
            kv_copies.append(copy)

    row = lax.broadcasted_iota(jnp.int32, (rows, size), 0)
    lane = lax.broadcasted_iota(jnp.int32, (rows, size), 1)
    place = row // batch
    for index in range(batch):
        place = place + jnp.where(row % batch == index, end_ref[index], 0)
    angle = place.astype(jnp.float32) * freq_ref[...]
    cosine[...] = jnp.cos(angle)
    sine[...] = jnp.where(lane < size // 2, -jnp.sin(angle), jnp.sin(angle))

    def rotated(vector):
        return vector * cosine[...] + pltpu.roll(vector, size // 2, 1) * sine[...]

    def send(piece, message, source, target):
        copy = pltpu.make_async_remote_copy(
            src_ref=source, dst_ref=rbuf.at[piece, message],
            send_sem=r_send.at[piece, message], recv_sem=r_recv.at[piece, message],
            device_id=target, device_id_type=pl.DeviceIdType.MESH,
        )
        copy.start()
        return copy

    tile = 512 if depth % 512 == 0 else depth

    def multiply(piece, first, target):
        group_rows = pl.ds(first, 4)
        for step in range(depth // tile):
            deep = pl.ds(step * tile, tile)
            part = jnp.dot(
                xbuf[group_rows, :, :, deep].reshape(4 * rows, tile), wbuf[piece, deep, :],
                preferred_element_type=jnp.float32,
            ).reshape(4, rows, wide)
            if step == 0:
                target[piece] = part
            else:
                target[piece] += part

    messages, swaps = {}, {}

    def swap(piece):
        for index, part in enumerate((pl.ds(3, 1), pl.ds(0, 3))):
            copy = pltpu.make_async_remote_copy(
                src_ref=gbuf.at[piece, part], dst_ref=sbuf.at[piece, part],
                send_sem=s_send.at[piece, index], recv_sem=s_recv.at[piece, index],
                device_id=pair, device_id_type=pl.DeviceIdType.MESH,
            )
            copy.start()
            swaps[piece, index] = copy

    def join(piece, message):
        swaps[piece, message].wait_recv()
        part = (pl.ds(3, 1), pl.ds(0, 3))[message]
        pbuf[piece, part] += sbuf[piece, part]
        first_hop(piece, message)

    def first_hop(piece, message):
        one = 1 if piece % 2 == 0 else 2
        source = pbuf.at[piece, 3 if message == 0 else one]
        messages[piece, message] = send(piece, message, source, near[one])

    def second_hop(piece):
        two = 2 if piece % 2 == 0 else 1
        messages[piece, 0].wait_recv()
        pbuf[piece, two] += rbuf[piece, 0]
        messages[piece, 2] = send(piece, 2, pbuf.at[piece, two], near[two])

    def await_weights(piece):
        for index in ((0,), (1, 2))[piece % 2]:
            local_copies[piece // 2, index].wait()

    passed = []
    for order, relation in enumerate((7, 3)):
        x_copies[relation].wait_recv()
        here = xbuf.at[relation, mine]
        passed.append(deliver(here, here, 8 + order, above))
        passed[-1].start()
    for relation in (4, 5, 6):
        x_copies[relation].wait_recv()
    x_copies[1].wait_recv()
    x_copies[2].wait_recv()
    x_own.wait()
    for order, relation in enumerate((7, 3)):
        there = xbuf.at[relation, theirs]
        deliver(there, there, 8 + order, above).wait_recv()
    for piece in range(2):
        await_weights(piece)
        multiply(piece, 4, gbuf)
        swap(piece)
    for piece in range(2):
        multiply(piece, 0, pbuf)
        join(piece, 0)
    for piece in range(2):
        join(piece, 1)
    for piece in range(2, 2 * chunks):
        await_weights(piece)
        multiply(piece, 4, gbuf)
        swap(piece)

    def attend(chunk):
        new = [None, None]
        for half in range(2):
            piece = 2 * chunk + half
            messages[piece, 1].wait_recv()
            messages[piece, 2].wait_recv()
            for block in range(blocks):
                cols = pl.ds(block * size, size)
                total = pbuf[piece, 0, :, cols] + rbuf[piece, 1, :, cols] + rbuf[piece, 2, :, cols]
                head = half * blocks + block
                if head == group + 1:
                    new[1] = total.astype(jnp.bfloat16)
                elif head == group:
                    new[0] = rotated(total).astype(jnp.bfloat16)
                else:
                    turned = rotated(total).astype(jnp.bfloat16).astype(jnp.float32)
                    for step in range(steps):
                        qbuf[pl.ds(head * steps + step, batch, stride=group * steps), :] = turned[
                            step * batch : (step + 1) * batch
                        ]
        new_keys, new_values = new
        lines = group * steps
        scale = size ** (-0.5)
        query = qbuf[...].astype(jnp.bfloat16)
        contract = (((1,), (1,)), ((), ()))
        scores = lax.dot_general(query, new_keys, contract, preferred_element_type=jnp.float32) * scale
        line = lax.broadcasted_iota(jnp.int32, scores.shape, 0)
        other = lax.broadcasted_iota(jnp.int32, scores.shape, 1)
        live = (line // lines == other % batch) & (other // batch <= line % steps)
        fresh[...] = jnp.where(live, scores, jnp.float32(-1e30))
        kv_copies[2 * chunk].wait()
        kv_copies[2 * chunk + 1].wait()
        cache_len = 2 * half_len

        def one(index):
            here = pl.ds(pl.multiple_of(index * lines, lines), lines)
            keys = kbuf[chunk, index].reshape(cache_len, size)
            values = vbuf[chunk, index].reshape(cache_len, size)
            position = lax.broadcasted_iota(jnp.int32, (1, cache_len), 1)
            cached = lax.dot_general(
                qbuf[here, :].astype(jnp.bfloat16), keys, contract, preferred_element_type=jnp.float32
            ) * scale
            cached = jnp.where(
                (position >= begin_ref[index]) & (position < end_ref[index]), cached, jnp.float32(-1e30)
            )
            extra = fresh[here, :]
            peak = jnp.maximum(
                jnp.max(cached, axis=1, keepdims=True), jnp.max(extra, axis=1, keepdims=True)
            )
            cached = jnp.exp(cached - peak)
            extra = jnp.exp(extra - peak)
            total = jnp.sum(cached, axis=1, keepdims=True) + jnp.sum(extra, axis=1, keepdims=True)
            weighted = jnp.dot(
                cached.astype(jnp.bfloat16), values, preferred_element_type=jnp.float32
            ) + jnp.dot(extra.astype(jnp.bfloat16), new_values, preferred_element_type=jnp.float32)
            obuf[here, :] = weighted / total

        unroll = 8 if batch % 8 == 0 else 1

        def several(outer, carry):
            for inner in range(unroll):
                one(outer * unroll + inner)
            return carry

        lax.fori_loop(0, batch // unroll, several, 0)
        for head in range(group):
            for step in range(steps):
                abuf[chunk, step, :, pl.ds(head * size, size)] = obuf[
                    pl.ds(head * steps + step, batch, stride=lines), :
                ].astype(jnp.bfloat16)

    share = out_ref.shape[2]
    per = 4 // chunks
    out_rows = pl.ds(pl.multiple_of(sec * batch, batch), batch)

    def handoff(target):
        chunk, place = target // per, target % per
        source = abuf.at[chunk, :, :, pl.ds(place * share, share)]
        keep = pltpu.make_async_copy(source, out_ref.at[:, out_rows, :], o_local)
        copy = pltpu.make_async_remote_copy(
            src_ref=source, dst_ref=out_ref.at[:, out_rows, :],
            send_sem=o_send.at[target], recv_sem=o_recv.at[sec],
            device_id={"dp": dp, "sec": target}, device_id_type=pl.DeviceIdType.MESH,
        )
        return keep, copy

    for piece in range(2):
        second_hop(piece)
    for chunk in range(chunks):
        if chunk + 1 < chunks:
            for piece in (2 * chunk + 2, 2 * chunk + 3):
                multiply(piece, 0, pbuf)
                join(piece, 0)
                join(piece, 1)
            second_hop(2 * chunk + 2)
            second_hop(2 * chunk + 3)
        attend(chunk)
        for target in range(chunk * per, (chunk + 1) * per):
            keep, copy = handoff(target)
            pl.when(sec == target)(keep.start)
            pl.when(sec != target)(copy.start)

    for target in range(4):
        keep, copy = handoff(target)
        pl.when(sec == target)(keep.wait)
        pl.when(sec != target)(copy.wait_send)
        arrived = pltpu.make_async_remote_copy(
            src_ref=abuf.at[0, :, :, pl.ds(0, share)],
            dst_ref=out_ref.at[:, pl.ds(target * batch, batch), :],
            send_sem=o_send.at[target], recv_sem=o_recv.at[target],
            device_id={"dp": dp, "sec": target}, device_id_type=pl.DeviceIdType.MESH,
        )
        pl.when(sec != target)(arrived.wait_recv)
    for copy in list(x_copies.values()) + passed + list(swaps.values()) + list(messages.values()):
        copy.wait_send()


def fused_body(hidden_states, w_query, w_keyval, key_cache, value_cache, cache_begin, cache_end):
    steps, batch, _ = hidden_states.shape
    slots, half_len, size = key_cache.shape[1:]
    depth = w_query.shape[0]
    chunks = slots // 2
    group = w_query.shape[1] // size // chunks
    rows = steps * batch
    wide = (group + 2) // 2 * size
    pieces = 2 * chunks
    share = w_query.shape[1] // 4
    lanes = np.arange(size, dtype=np.float32) % (size // 2)
    freq = np.float32(THETA) ** (-(lanes * np.float32(2.0) / np.float32(size)))
    anywhere = pl.BlockSpec(memory_space=pl.ANY)
    scalars = pl.BlockSpec(memory_space=pltpu.SMEM)
    dma = pltpu.SemaphoreType.DMA
    return pl.pallas_call(
        functools.partial(fused_kernel, group),
        out_shape=jax.ShapeDtypeStruct((steps, 4 * batch, share), jnp.bfloat16),
        in_specs=[pl.BlockSpec(memory_space=pltpu.VMEM), scalars, scalars] + [anywhere] * 5,
        out_specs=anywhere,
        scratch_shapes=[
            pltpu.VMEM((8, steps, batch, depth), jnp.bfloat16),
            pltpu.VMEM((pieces, depth, wide), jnp.bfloat16),
            pltpu.VMEM((pieces, 4, rows, wide), jnp.float32),
            pltpu.VMEM((pieces, 4, rows, wide), jnp.float32),
            pltpu.VMEM((pieces, 4, rows, wide), jnp.float32),
            pltpu.VMEM((pieces, 3, rows, wide), jnp.float32),
            pltpu.VMEM((chunks, batch, 2, half_len, size), jnp.bfloat16),
            pltpu.VMEM((chunks, batch, 2, half_len, size), jnp.bfloat16),
            pltpu.VMEM((rows, size), jnp.float32),
            pltpu.VMEM((rows, size), jnp.float32),
            pltpu.VMEM((group * rows, size), jnp.float32),
            pltpu.VMEM((group * rows, rows), jnp.float32),
            pltpu.VMEM((group * rows, size), jnp.float32),
            pltpu.VMEM((chunks, steps, batch, group * size), jnp.bfloat16),
            dma, dma((10,)), dma((10,)),
            dma((chunks, 3)), dma((pieces, 2)), dma((pieces, 2)),
            dma((chunks, 2)),
            dma((pieces, 3)), dma((pieces, 3)),
            dma, dma((4,)), dma((4,)),
        ],
        compiler_params=pltpu.CompilerParams(
            collective_id=0, has_side_effects=True, vmem_limit_bytes=56 * 1024 * 1024
        ),
        cost_estimate=pl.CostEstimate(
            flops=2 * 4 * rows * 2 * depth * pieces * wide,
            bytes_accessed=2 * (w_query.size + w_keyval.size + 2 * key_cache.size),
            transcendentals=0,
        ),
    )(freq[None, :], cache_begin, cache_end, hidden_states, w_query, w_keyval, key_cache, value_cache)


def body(sizes, hidden_states, w_query, w_keyval, key_cache, value_cache, cache_begin, cache_end):
    arrays = (hidden_states, w_query, w_keyval, key_cache, value_cache, cache_begin, cache_end)
    slots = key_cache.shape[1]
    if sizes["dp"] == 2 and sizes["sec"] == 4 and sizes["tp"] % 2 == 0 and slots in (2, 4, 8):
        return fused_body(*arrays)
    return general_body(*arrays)


def solution(mesh):
    return jax.shard_map(
        functools.partial(body, mesh.shape),
        mesh=mesh,
        in_specs=(
            P(None, ("dp", "sec"), None),
            P(("dp", "sec"), "tp"),
            P(("dp", "sec"), "tp"),
            P(("dp", "sec"), "tp", None, None),
            P(("dp", "sec"), "tp", None, None),
            P(("dp", "sec")),
            P(("dp", "sec")),
        ),
        out_specs=P(None, "dp", ("tp", "sec")),
        check_vma=False,
    )
```

```python
import functools

import jax
import jax.numpy as jnp
import numpy as np
from jax import lax
from jax.experimental import pallas as pl
from jax.experimental.pallas import tpu as pltpu
from jax.sharding import PartitionSpec as P

THETA = 500000.0


def swapped(value, axis, stride):
    mask = 2**stride
    pairs = [(source, source ^ mask) for source in range(lax.axis_size(axis))]
    return lax.ppermute(value, axis, pairs)


def rotate(vector, positions):
    half = vector.shape[-1] // 2
    freq = THETA ** (-(jnp.arange(half, dtype=jnp.float32) * 2.0 / vector.shape[-1]))
    angle = positions[..., None] * freq
    angle = angle.reshape(positions.shape + (1,) * (vector.ndim - positions.ndim - 1) + (half,))
    cosine = jnp.cos(angle)
    sine = jnp.sin(angle)
    first = vector[..., :half]
    second = vector[..., half:]
    return jnp.concatenate(
        [first * cosine - second * sine, second * cosine + first * sine], axis=-1
    )


def make_accumulate(token_rows, pieces):
    return (
        jnp.dot(token_rows, pieces[0], preferred_element_type=jnp.float32),
        jnp.dot(token_rows, pieces[1], preferred_element_type=jnp.float32),
    )


def partial_attention(query, keys, values, live, score_scale):
    scores = (
        jnp.einsum("sbkgd,bkpd->sbkgp", query, keys, preferred_element_type=jnp.float32)
        * score_scale
    )
    live = jnp.broadcast_to(live, scores.shape)
    masked = jnp.where(live, scores, jnp.float32(-1e30))
    maxima = jnp.max(masked, axis=-1)
    expo = jnp.where(live, jnp.exp(masked - maxima[..., None]), jnp.float32(0.0))
    totals = jnp.sum(expo, axis=-1)
    weighted = jnp.einsum(
        "sbkgp,bkpd->sbkgd", expo.astype(jnp.bfloat16), values, preferred_element_type=jnp.float32
    )
    return (maxima, totals, weighted)


def merge_parts(parts):
    overall = parts[0][0]
    for entry in parts[1:]:
        overall = jnp.maximum(overall, entry[0])
    weighted = jnp.zeros_like(parts[0][2])
    totals = jnp.zeros_like(parts[0][1])
    for entry in parts:
        factor = jnp.exp(entry[0] - overall)
        weighted = weighted + entry[2] * factor[..., None]
        totals = totals + entry[1] * factor
    return weighted / totals[..., None]


def general_body(hidden_states, w_query, w_keyval, key_cache, value_cache, cache_begin, cache_end):
    num_steps, batch_rows, width = hidden_states.shape
    head_size = key_cache.shape[-1]
    query_cols = w_query.shape[1]
    keyval_cols = w_keyval.shape[1]
    local_heads = query_cols // head_size
    slot_count = key_cache.shape[1]
    half_len = key_cache.shape[2]
    score_scale = head_size ** (-0.5)
    sec_count = lax.axis_size("sec")
    sec_index = lax.axis_index("sec")
    sec_group = lax.all_gather(hidden_states, "sec", axis=1, tiled=True)
    shard_rows = w_query.shape[0]
    dp_count = width // (sec_count * shard_rows)
    group_rows = num_steps * batch_rows * sec_count
    grouped = sec_group.reshape(group_rows, dp_count, sec_count, shard_rows)
    chosen = lax.dynamic_slice_in_dim(grouped, sec_index, 1, 2).reshape(
        group_rows, dp_count * shard_rows
    )
    query_all, keyval_all = make_accumulate(
        chosen,
        (
            lax.all_gather(w_query, "dp", axis=0, tiled=True),
            lax.all_gather(w_keyval, "dp", axis=0, tiled=True),
        ),
    )
    query_acc, keyval_acc = (
        lax.psum_scatter(
            query_all.reshape(num_steps, sec_count * batch_rows, query_cols),
            "sec",
            scatter_dimension=1,
            tiled=True,
        ),
        lax.psum_scatter(
            keyval_all.reshape(num_steps, sec_count * batch_rows, keyval_cols),
            "sec",
            scatter_dimension=1,
            tiled=True,
        ),
    )
    query_acc = query_acc.reshape(num_steps * batch_rows, query_cols)
    keyval_acc = keyval_acc.reshape(num_steps * batch_rows, keyval_cols)
    positions = (
        cache_end.astype(jnp.float32)[None, :] + jnp.arange(num_steps, dtype=jnp.float32)[:, None]
    )
    query = rotate(
        query_acc.reshape(num_steps, batch_rows, local_heads, head_size), positions
    ).astype(jnp.bfloat16)
    step_ids = jnp.arange(num_steps, dtype=jnp.int32)
    causal = step_ids[None, :] <= step_ids[:, None]
    if slot_count == 1:
        parity = lax.axis_index("tp") % 2
        own_proj = keyval_acc.reshape(num_steps, batch_rows, head_size)
        own_proj = jnp.where(parity == 0, rotate(own_proj, positions), own_proj).astype(
            jnp.bfloat16
        )
        partner_query, partner_proj = swapped((query, own_proj), "tp", 0)
        new_keys = jnp.where(parity == 0, own_proj, partner_proj)
        new_values = jnp.where(parity == 0, partner_proj, own_proj)
        lower_heads = jnp.where(parity == 0, query, partner_query)
        upper_heads = jnp.where(parity == 0, partner_query, query)
        both_heads = jnp.concatenate([lower_heads, upper_heads], axis=2)[:, :, None]
        cache_pos = parity * half_len + jnp.arange(half_len, dtype=jnp.int32)
        cache_live = (cache_pos[None, :] >= cache_begin[:, None]) & (
            cache_pos[None, :] < cache_end[:, None]
        )
        cache_part = partial_attention(
            both_heads, key_cache, value_cache, cache_live[None, :, None, None, :], score_scale
        )
        mine_start = parity * local_heads
        theirs_start = (1 - parity) * local_heads

        def select_heads(array, start):
            return lax.dynamic_slice_in_dim(array, start, local_heads, 3)

        returned = (
            swapped(select_heads(cache_part[0], theirs_start).astype(jnp.bfloat16), "tp", 0).astype(
                jnp.float32
            ),
            swapped(select_heads(cache_part[1], theirs_start).astype(jnp.bfloat16), "tp", 0).astype(
                jnp.float32
            ),
            swapped(select_heads(cache_part[2], theirs_start).astype(jnp.bfloat16), "tp", 0).astype(
                jnp.float32
            ),
        )
        own_part = (
            select_heads(cache_part[0], mine_start),
            select_heads(cache_part[1], mine_start),
            select_heads(cache_part[2], mine_start),
        )
        fresh_part = partial_attention(
            query[:, :, None],
            jnp.transpose(new_keys, (1, 0, 2))[:, None],
            jnp.transpose(new_values, (1, 0, 2))[:, None],
            causal[:, None, None, None, :],
            score_scale,
        )
        parts = [own_part, returned, fresh_part]
    else:
        local_kv = keyval_cols // (2 * head_size)
        keyval = keyval_acc.reshape(num_steps, batch_rows, local_kv, 2, head_size)
        new_keys = rotate(keyval[:, :, :, 0], positions).astype(jnp.bfloat16)
        new_values = keyval[:, :, :, 1].astype(jnp.bfloat16)
        whole_keys = key_cache.reshape(batch_rows, local_kv, 2 * half_len, head_size)
        whole_values = value_cache.reshape(batch_rows, local_kv, 2 * half_len, head_size)
        grouped_query = query.reshape(
            num_steps, batch_rows, local_kv, local_heads // local_kv, head_size
        )
        cache_pos = jnp.arange(2 * half_len, dtype=jnp.int32)
        cache_live = (cache_pos[None, :] >= cache_begin[:, None]) & (
            cache_pos[None, :] < cache_end[:, None]
        )
        cache_part = partial_attention(
            grouped_query, whole_keys, whole_values, cache_live[None, :, None, None, :], score_scale
        )
        fresh_part = partial_attention(
            grouped_query,
            jnp.transpose(new_keys, (1, 2, 0, 3)),
            jnp.transpose(new_values, (1, 2, 0, 3)),
            causal[:, None, None, None, :],
            score_scale,
        )
        parts = [cache_part, fresh_part]
    attended = (
        merge_parts(parts)
        .astype(jnp.bfloat16)
        .reshape(num_steps, batch_rows, local_heads * head_size)
    )
    return lax.all_to_all(attended, "sec", split_axis=2, concat_axis=1, tiled=True)


def fused_kernel(
    group, freq_ref, begin_ref, end_ref, hidden_ref, wq_ref, wkv_ref, key_ref, value_ref, out_ref,
    xbuf, wbuf, pbuf, rbuf, kbuf, vbuf, cosine, sine, qbuf, fresh, obuf, abuf,
    x_local, x_send, x_recv, w_local, w_send, w_recv, kv_sem, r_send, r_recv, o_local, o_send, o_recv,
):
    chunks = wkv_ref.shape[1] // (2 * key_ref.shape[3])
    steps, batch, _ = hidden_ref.shape
    size = key_ref.shape[3]
    depth = wq_ref.shape[0]
    span = 2 * depth
    rows = steps * batch
    half_len = key_ref.shape[2]
    blocks = (group + 2) // 2
    wide = blocks * size
    dp, sec = lax.axis_index("dp"), lax.axis_index("sec")
    core = sec % 2
    dp_other = 1 - dp
    sec_far = (sec + 2) % 4
    sec_pair = sec + 1 - 2 * core
    near = ({"dp": dp, "sec": sec}, {"dp": dp_other, "sec": sec}, {"dp": dp, "sec": sec_far}, {"dp": dp_other, "sec": sec_far})
    pair = {"dp": dp, "sec": sec_pair}
    cross = {"dp": dp, "sec": (sec_pair + 2) % 4}
    odd = lax.axis_index("tp") % 2
    above = {"tp": lax.axis_index("tp") + 1 - 2 * odd}
    chips = (dp * 2 + sec // 2, dp_other * 2 + sec // 2, dp * 2 + sec_far // 2, dp_other * 2 + sec_far // 2)

    def weight_parts(chunk):
        first = chunk * group * size
        return (
            (2 * chunk, 0, wide, wq_ref, first),
            (2 * chunk + 1, 0, group * size - wide, wq_ref, first + wide),
            (2 * chunk + 1, group * size - wide, 2 * size, wkv_ref, chunk * 2 * size),
        )

    own_rows = pl.ds(pl.multiple_of(core * depth, depth), depth)

    def weight_refs(part):
        piece, start, width, source, column = part
        return (
            source.at[:, pl.ds(column, width)],
            wbuf.at[piece, own_rows, pl.ds(start, width)],
        )

    def hidden_slice(relation):
        return hidden_ref.at[:, :, pl.ds(pl.multiple_of(chips[relation] * span, span), span)]

    local_copies = {}
    x_own = pltpu.make_async_copy(hidden_slice(0), xbuf.at[0], x_local)
    x_own.start()
    for chunk in range(chunks):
        for index, part in enumerate(weight_parts(chunk)):
            source, target = weight_refs(part)
            copy = pltpu.make_async_copy(source, target, w_local.at[chunk, index])
            copy.start()
            local_copies[chunk, index] = copy

    barrier = pltpu.get_barrier_semaphore()
    for peer in near[1:] + (pair, cross, above):
        pl.semaphore_signal(barrier, inc=1, device_id=peer, device_id_type=pl.DeviceIdType.MESH)
    pl.semaphore_wait(barrier, 6)

    def deliver(source, target, index, device):
        return pltpu.make_async_remote_copy(
            src_ref=source, dst_ref=target, send_sem=x_send.at[index], recv_sem=x_recv.at[index],
            device_id=device, device_id_type=pl.DeviceIdType.MESH,
        )

    half_steps = steps // 2
    x_copies = []
    for step in range(half_steps):
        where = odd * half_steps + step
        x_copies.append(deliver(hidden_slice(3).at[where], xbuf.at[3, where], step, near[3]))
    for relation in (1, 2):
        x_copies.append(
            deliver(hidden_slice(relation), xbuf.at[relation], half_steps + relation - 1, near[relation])
        )
    for copy in x_copies:
        copy.start()
    w_copies = {}
    for chunk in range(chunks):
        for index, part in enumerate(weight_parts(chunk)):
            source, target = weight_refs(part)
            copy = pltpu.make_async_remote_copy(
                src_ref=source, dst_ref=target,
                send_sem=w_send.at[chunk, index], recv_sem=w_recv.at[chunk, index],
                device_id=pair, device_id_type=pl.DeviceIdType.MESH,
            )
            copy.start()
            w_copies[chunk, index] = copy
    kv_copies = []
    for chunk in range(chunks):
        slots = pl.ds(2 * chunk, 2)
        for index, (source, target) in enumerate(((key_ref, kbuf), (value_ref, vbuf))):
            copy = pltpu.make_async_copy(source.at[:, slots], target.at[chunk], kv_sem.at[chunk, index])
            copy.start()
            kv_copies.append(copy)

    row = lax.broadcasted_iota(jnp.int32, (rows, size), 0)
    lane = lax.broadcasted_iota(jnp.int32, (rows, size), 1)
    place = row // batch
    for index in range(batch):
        place = place + jnp.where(row % batch == index, end_ref[index], 0)
    angle = place.astype(jnp.float32) * freq_ref[...]
    cosine[...] = jnp.cos(angle)
    sine[...] = jnp.where(lane < size // 2, -jnp.sin(angle), jnp.sin(angle))

    def rotated(vector):
        return vector * cosine[...] + pltpu.roll(vector, size // 2, 1) * sine[...]

    def send(piece, message, source, target):
        copy = pltpu.make_async_remote_copy(
            src_ref=source, dst_ref=rbuf.at[piece, message],
            send_sem=r_send.at[piece, message], recv_sem=r_recv.at[piece, message],
            device_id=target, device_id_type=pl.DeviceIdType.MESH,
        )
        copy.start()
        return copy

    tile = 512 if span % 512 == 0 else span

    def multiply(piece, first, count):
        group_rows = pl.ds(first, count)
        for step in range(span // tile):
            deep = pl.ds(step * tile, tile)
            part = jnp.dot(
                xbuf[group_rows, :, :, deep].reshape(count * rows, tile), wbuf[piece, deep, :],
                preferred_element_type=jnp.float32,
            ).reshape(count, rows, wide)
            if step == 0:
                pbuf[piece, group_rows] = part
            else:
                pbuf[piece, group_rows] += part

    messages = {}

    def first_hop(piece, message):
        one = 1 if piece % 2 == 0 else 2
        source = pbuf.at[piece, 3 if message == 0 else one]
        messages[piece, message] = send(piece, message, source, near[one])

    def second_hop(piece):
        two = 2 if piece % 2 == 0 else 1
        messages[piece, 0].wait_recv()
        pbuf[piece, two] += rbuf[piece, 0]
        messages[piece, 2] = send(piece, 2, pbuf.at[piece, two], near[two])

    def await_weights(piece):
        for index in ((0,), (1, 2))[piece % 2]:
            local_copies[piece // 2, index].wait()
            w_copies[piece // 2, index].wait_recv()

    passed = []
    for step in range(half_steps):
        x_copies[step].wait_recv()
        here = xbuf.at[3, odd * half_steps + step]
        passed.append(deliver(here, here, half_steps + 2 + step, above))
        passed[-1].start()
    for step in range(half_steps):
        there = xbuf.at[3, (1 - odd) * half_steps + step]
        deliver(there, there, half_steps + 2 + step, above).wait_recv()
    for piece in range(2):
        await_weights(piece)
        multiply(piece, 3, 1)
        first_hop(piece, 0)
    x_own.wait()
    for copy in x_copies[half_steps:]:
        copy.wait_recv()
    for piece in range(2):
        multiply(piece, 0, 3)
        first_hop(piece, 1)
    def attend(chunk):
        new = [None, None]
        for half in range(2):
            piece = 2 * chunk + half
            for block in range(blocks):
                cols = pl.ds(block * size, size)
                total = pbuf[piece, 0, :, cols] + rbuf[piece, 1, :, cols] + rbuf[piece, 2, :, cols]
                head = half * blocks + block
                if head == group + 1:
                    new[1] = total.astype(jnp.bfloat16)
                elif head == group:
                    new[0] = rotated(total).astype(jnp.bfloat16)
                else:
                    turned = rotated(total).astype(jnp.bfloat16).astype(jnp.float32)
                    for step in range(steps):
                        qbuf[pl.ds(head * steps + step, batch, stride=group * steps), :] = turned[
                            step * batch : (step + 1) * batch
                        ]
        spare = jnp.zeros((-rows % 128, size), jnp.bfloat16)
        new_keys, new_values = (jnp.concatenate([part, spare], axis=0) for part in new)
        lines = group * steps
        scale = size ** (-0.5)
        query = qbuf[...].astype(jnp.bfloat16)
        contract = (((1,), (1,)), ((), ()))
        scores = lax.dot_general(query, new_keys, contract, preferred_element_type=jnp.float32) * scale
        line = lax.broadcasted_iota(jnp.int32, scores.shape, 0)
        other = lax.broadcasted_iota(jnp.int32, scores.shape, 1)
        live = (line // lines == other % batch) & (other // batch <= line % steps) & (other < rows)
        fresh[...] = jnp.where(live, scores, jnp.float32(-1e30))
        kv_copies[2 * chunk].wait()
        kv_copies[2 * chunk + 1].wait()
        cache_len = 2 * half_len

        def one(index):
            here = pl.ds(pl.multiple_of(index * lines, lines), lines)
            keys = kbuf[chunk, index].reshape(cache_len, size)
            values = vbuf[chunk, index].reshape(cache_len, size)
            position = lax.broadcasted_iota(jnp.int32, (1, cache_len), 1)
            dead = jnp.where(
                (position >= begin_ref[index]) & (position < end_ref[index]), jnp.float32(0.0), jnp.float32(-1e30)
            )
            cached = lax.dot_general(
                qbuf[here, :].astype(jnp.bfloat16), keys, contract, preferred_element_type=jnp.float32
            ) * scale + dead
            extra = fresh[here, :]
            packs = range(0, cache_len, extra.shape[1])
            peak = extra
            for pack in packs:
                peak = jnp.maximum(peak, cached[:, pack : pack + extra.shape[1]])
            peak = jnp.max(peak, axis=1, keepdims=True)
            cached = jnp.exp(cached - peak)
            extra = jnp.exp(extra - peak)
            total = extra
            for pack in packs:
                total = total + cached[:, pack : pack + extra.shape[1]]
            total = jnp.sum(total, axis=1, keepdims=True)
            weighted = jnp.dot(
                cached.astype(jnp.bfloat16), values, preferred_element_type=jnp.float32
            ) + jnp.dot(extra.astype(jnp.bfloat16), new_values, preferred_element_type=jnp.float32)
            obuf[here, :] = weighted / total

        unroll = 8 if batch % 8 == 0 else 1

        def several(outer, carry):
            for inner in range(unroll):
                one(outer * unroll + inner)
            return carry

        lax.fori_loop(0, batch // unroll, several, 0)
        for head in range(group):
            for step in range(steps):
                abuf[chunk, step, :, pl.ds(head * size, size)] = obuf[
                    pl.ds(head * steps + step, batch, stride=lines), :
                ].astype(jnp.bfloat16)

    share = out_ref.shape[2]
    per = 4 // chunks
    out_rows = pl.ds(pl.multiple_of(sec * batch, batch), batch)

    def handoff(target):
        chunk, place = target // per, target % per
        source = abuf.at[chunk, :, :, pl.ds(place * share, share)]
        keep = pltpu.make_async_copy(source, out_ref.at[:, out_rows, :], o_local)
        copy = pltpu.make_async_remote_copy(
            src_ref=source, dst_ref=out_ref.at[:, out_rows, :],
            send_sem=o_send.at[target], recv_sem=o_recv.at[sec],
            device_id={"dp": dp, "sec": target}, device_id_type=pl.DeviceIdType.MESH,
        )
        return keep, copy

    def hand_over(chunk):
        for target in range(chunk * per, (chunk + 1) * per):
            keep, copy = handoff(target)
            pl.when(sec == target)(keep.start)
            pl.when(sec != target)(copy.start)

    for piece in range(2):
        second_hop(piece)
    for chunk in range(chunks):
        if chunk + 1 < chunks:
            for piece in (2 * chunk + 2, 2 * chunk + 3):
                await_weights(piece)
                multiply(piece, 0, 4)
                first_hop(piece, 0)
                first_hop(piece, 1)
            second_hop(2 * chunk + 2)
            second_hop(2 * chunk + 3)
        for piece in (2 * chunk, 2 * chunk + 1):
            messages[piece, 1].wait_recv()
            messages[piece, 2].wait_recv()
        if chunk > 0:
            hand_over(chunk - 1)
        attend(chunk)
    hand_over(chunks - 1)

    for target in range(4):
        keep, copy = handoff(target)
        pl.when(sec == target)(keep.wait)
        pl.when(sec != target)(copy.wait_send)
        arrived = pltpu.make_async_remote_copy(
            src_ref=abuf.at[0, :, :, pl.ds(0, share)],
            dst_ref=out_ref.at[:, pl.ds(target * batch, batch), :],
            send_sem=o_send.at[target], recv_sem=o_recv.at[target],
            device_id={"dp": dp, "sec": target}, device_id_type=pl.DeviceIdType.MESH,
        )
        pl.when(sec != target)(arrived.wait_recv)
    for copy in x_copies + passed + list(w_copies.values()) + list(messages.values()):
        copy.wait_send()


def fused_body(hidden_states, w_query, w_keyval, key_cache, value_cache, cache_begin, cache_end):
    steps, batch, _ = hidden_states.shape
    slots, half_len, size = key_cache.shape[1:]
    depth = w_query.shape[0]
    chunks = slots // 2
    group = w_query.shape[1] // size // chunks
    rows = steps * batch
    wide = (group + 2) // 2 * size
    pieces = 2 * chunks
    share = w_query.shape[1] // 4
    lanes = np.arange(size, dtype=np.float32) % (size // 2)
    freq = np.float32(THETA) ** (-(lanes * np.float32(2.0) / np.float32(size)))
    anywhere = pl.BlockSpec(memory_space=pl.ANY)
    scalars = pl.BlockSpec(memory_space=pltpu.SMEM)
    dma = pltpu.SemaphoreType.DMA
    return pl.pallas_call(
        functools.partial(fused_kernel, group),
        out_shape=jax.ShapeDtypeStruct((steps, 4 * batch, share), jnp.bfloat16),
        in_specs=[pl.BlockSpec(memory_space=pltpu.VMEM), scalars, scalars] + [anywhere] * 5,
        out_specs=anywhere,
        scratch_shapes=[
            pltpu.VMEM((4, steps, batch, 2 * depth), jnp.bfloat16),
            pltpu.VMEM((pieces, 2 * depth, wide), jnp.bfloat16),
            pltpu.VMEM((pieces, 4, rows, wide), jnp.float32),
            pltpu.VMEM((pieces, 3, rows, wide), jnp.float32),
            pltpu.VMEM((chunks, batch, 2, half_len, size), jnp.bfloat16),
            pltpu.VMEM((chunks, batch, 2, half_len, size), jnp.bfloat16),
            pltpu.VMEM((rows, size), jnp.float32),
            pltpu.VMEM((rows, size), jnp.float32),
            pltpu.VMEM((group * rows, size), jnp.float32),
            pltpu.VMEM((group * rows, rows + -rows % 128), jnp.float32),
            pltpu.VMEM((group * rows, size), jnp.float32),
            pltpu.VMEM((chunks, steps, batch, group * size), jnp.bfloat16),
            dma, dma((steps + 2,)), dma((steps + 2,)),
            dma((chunks, 3)), dma((chunks, 3)), dma((chunks, 3)),
            dma((chunks, 2)),
            dma((pieces, 3)), dma((pieces, 3)),
            dma, dma((4,)), dma((4,)),
        ],
        compiler_params=pltpu.CompilerParams(
            collective_id=0, has_side_effects=True, vmem_limit_bytes=56 * 1024 * 1024
        ),
        cost_estimate=pl.CostEstimate(
            flops=2 * 4 * rows * 2 * depth * pieces * wide,
            bytes_accessed=2 * (w_query.size + w_keyval.size + 2 * key_cache.size),
            transcendentals=0,
        ),
    )(freq[None, :], cache_begin, cache_end, hidden_states, w_query, w_keyval, key_cache, value_cache)


def body(sizes, hidden_states, w_query, w_keyval, key_cache, value_cache, cache_begin, cache_end):
    arrays = (hidden_states, w_query, w_keyval, key_cache, value_cache, cache_begin, cache_end)
    slots = key_cache.shape[1]
    if sizes["dp"] == 2 and sizes["sec"] == 4 and sizes["tp"] % 2 == 0 and slots in (2, 4, 8):
        return fused_body(*arrays)
    return general_body(*arrays)


def solution(mesh):
    return jax.shard_map(
        functools.partial(body, mesh.shape),
        mesh=mesh,
        in_specs=(
            P(None, ("dp", "sec"), None),
            P(("dp", "sec"), "tp"),
            P(("dp", "sec"), "tp"),
            P(("dp", "sec"), "tp", None, None),
            P(("dp", "sec"), "tp", None, None),
            P(("dp", "sec")),
            P(("dp", "sec")),
        ),
        out_specs=P(None, "dp", ("tp", "sec")),
        check_vma=False,
    )
```

```python
import functools

import jax
import jax.numpy as jnp
import numpy as np
from jax import lax
from jax.experimental import pallas as pl
from jax.experimental.pallas import tpu as pltpu
from jax.sharding import PartitionSpec as P

THETA = 500000.0


def swapped(value, axis, stride):
    mask = 2**stride
    pairs = [(source, source ^ mask) for source in range(lax.axis_size(axis))]
    return lax.ppermute(value, axis, pairs)


def rotate(vector, positions):
    half = vector.shape[-1] // 2
    freq = THETA ** (-(jnp.arange(half, dtype=jnp.float32) * 2.0 / vector.shape[-1]))
    angle = positions[..., None] * freq
    angle = angle.reshape(positions.shape + (1,) * (vector.ndim - positions.ndim - 1) + (half,))
    cosine = jnp.cos(angle)
    sine = jnp.sin(angle)
    first = vector[..., :half]
    second = vector[..., half:]
    return jnp.concatenate(
        [first * cosine - second * sine, second * cosine + first * sine], axis=-1
    )


def make_accumulate(token_rows, pieces):
    return (
        jnp.dot(token_rows, pieces[0], preferred_element_type=jnp.float32),
        jnp.dot(token_rows, pieces[1], preferred_element_type=jnp.float32),
    )


def partial_attention(query, keys, values, live, score_scale):
    scores = (
        jnp.einsum("sbkgd,bkpd->sbkgp", query, keys, preferred_element_type=jnp.float32)
        * score_scale
    )
    live = jnp.broadcast_to(live, scores.shape)
    masked = jnp.where(live, scores, jnp.float32(-1e30))
    maxima = jnp.max(masked, axis=-1)
    expo = jnp.where(live, jnp.exp(masked - maxima[..., None]), jnp.float32(0.0))
    totals = jnp.sum(expo, axis=-1)
    weighted = jnp.einsum(
        "sbkgp,bkpd->sbkgd", expo.astype(jnp.bfloat16), values, preferred_element_type=jnp.float32
    )
    return (maxima, totals, weighted)


def merge_parts(parts):
    overall = parts[0][0]
    for entry in parts[1:]:
        overall = jnp.maximum(overall, entry[0])
    weighted = jnp.zeros_like(parts[0][2])
    totals = jnp.zeros_like(parts[0][1])
    for entry in parts:
        factor = jnp.exp(entry[0] - overall)
        weighted = weighted + entry[2] * factor[..., None]
        totals = totals + entry[1] * factor
    return weighted / totals[..., None]


def general_body(hidden_states, w_query, w_keyval, key_cache, value_cache, cache_begin, cache_end):
    num_steps, batch_rows, width = hidden_states.shape
    head_size = key_cache.shape[-1]
    query_cols = w_query.shape[1]
    keyval_cols = w_keyval.shape[1]
    local_heads = query_cols // head_size
    slot_count = key_cache.shape[1]
    half_len = key_cache.shape[2]
    score_scale = head_size ** (-0.5)
    sec_count = lax.axis_size("sec")
    sec_index = lax.axis_index("sec")
    sec_group = lax.all_gather(hidden_states, "sec", axis=1, tiled=True)
    shard_rows = w_query.shape[0]
    dp_count = width // (sec_count * shard_rows)
    group_rows = num_steps * batch_rows * sec_count
    grouped = sec_group.reshape(group_rows, dp_count, sec_count, shard_rows)
    chosen = lax.dynamic_slice_in_dim(grouped, sec_index, 1, 2).reshape(
        group_rows, dp_count * shard_rows
    )
    query_all, keyval_all = make_accumulate(
        chosen,
        (
            lax.all_gather(w_query, "dp", axis=0, tiled=True),
            lax.all_gather(w_keyval, "dp", axis=0, tiled=True),
        ),
    )
    query_acc, keyval_acc = (
        lax.psum_scatter(
            query_all.reshape(num_steps, sec_count * batch_rows, query_cols),
            "sec",
            scatter_dimension=1,
            tiled=True,
        ),
        lax.psum_scatter(
            keyval_all.reshape(num_steps, sec_count * batch_rows, keyval_cols),
            "sec",
            scatter_dimension=1,
            tiled=True,
        ),
    )
    query_acc = query_acc.reshape(num_steps * batch_rows, query_cols)
    keyval_acc = keyval_acc.reshape(num_steps * batch_rows, keyval_cols)
    positions = (
        cache_end.astype(jnp.float32)[None, :] + jnp.arange(num_steps, dtype=jnp.float32)[:, None]
    )
    query = rotate(
        query_acc.reshape(num_steps, batch_rows, local_heads, head_size), positions
    ).astype(jnp.bfloat16)
    step_ids = jnp.arange(num_steps, dtype=jnp.int32)
    causal = step_ids[None, :] <= step_ids[:, None]
    if slot_count == 1:
        parity = lax.axis_index("tp") % 2
        own_proj = keyval_acc.reshape(num_steps, batch_rows, head_size)
        own_proj = jnp.where(parity == 0, rotate(own_proj, positions), own_proj).astype(
            jnp.bfloat16
        )
        partner_query, partner_proj = swapped((query, own_proj), "tp", 0)
        new_keys = jnp.where(parity == 0, own_proj, partner_proj)
        new_values = jnp.where(parity == 0, partner_proj, own_proj)
        lower_heads = jnp.where(parity == 0, query, partner_query)
        upper_heads = jnp.where(parity == 0, partner_query, query)
        both_heads = jnp.concatenate([lower_heads, upper_heads], axis=2)[:, :, None]
        cache_pos = parity * half_len + jnp.arange(half_len, dtype=jnp.int32)
        cache_live = (cache_pos[None, :] >= cache_begin[:, None]) & (
            cache_pos[None, :] < cache_end[:, None]
        )
        cache_part = partial_attention(
            both_heads, key_cache, value_cache, cache_live[None, :, None, None, :], score_scale
        )
        mine_start = parity * local_heads
        theirs_start = (1 - parity) * local_heads

        def select_heads(array, start):
            return lax.dynamic_slice_in_dim(array, start, local_heads, 3)

        returned = (
            swapped(select_heads(cache_part[0], theirs_start).astype(jnp.bfloat16), "tp", 0).astype(
                jnp.float32
            ),
            swapped(select_heads(cache_part[1], theirs_start).astype(jnp.bfloat16), "tp", 0).astype(
                jnp.float32
            ),
            swapped(select_heads(cache_part[2], theirs_start).astype(jnp.bfloat16), "tp", 0).astype(
                jnp.float32
            ),
        )
        own_part = (
            select_heads(cache_part[0], mine_start),
            select_heads(cache_part[1], mine_start),
            select_heads(cache_part[2], mine_start),
        )
        fresh_part = partial_attention(
            query[:, :, None],
            jnp.transpose(new_keys, (1, 0, 2))[:, None],
            jnp.transpose(new_values, (1, 0, 2))[:, None],
            causal[:, None, None, None, :],
            score_scale,
        )
        parts = [own_part, returned, fresh_part]
    else:
        local_kv = keyval_cols // (2 * head_size)
        keyval = keyval_acc.reshape(num_steps, batch_rows, local_kv, 2, head_size)
        new_keys = rotate(keyval[:, :, :, 0], positions).astype(jnp.bfloat16)
        new_values = keyval[:, :, :, 1].astype(jnp.bfloat16)
        whole_keys = key_cache.reshape(batch_rows, local_kv, 2 * half_len, head_size)
        whole_values = value_cache.reshape(batch_rows, local_kv, 2 * half_len, head_size)
        grouped_query = query.reshape(
            num_steps, batch_rows, local_kv, local_heads // local_kv, head_size
        )
        cache_pos = jnp.arange(2 * half_len, dtype=jnp.int32)
        cache_live = (cache_pos[None, :] >= cache_begin[:, None]) & (
            cache_pos[None, :] < cache_end[:, None]
        )
        cache_part = partial_attention(
            grouped_query, whole_keys, whole_values, cache_live[None, :, None, None, :], score_scale
        )
        fresh_part = partial_attention(
            grouped_query,
            jnp.transpose(new_keys, (1, 2, 0, 3)),
            jnp.transpose(new_values, (1, 2, 0, 3)),
            causal[:, None, None, None, :],
            score_scale,
        )
        parts = [cache_part, fresh_part]
    attended = (
        merge_parts(parts)
        .astype(jnp.bfloat16)
        .reshape(num_steps, batch_rows, local_heads * head_size)
    )
    return lax.all_to_all(attended, "sec", split_axis=2, concat_axis=1, tiled=True)


def fused_kernel(
    group, freq_ref, begin_ref, end_ref, hidden_ref, wq_ref, wkv_ref, key_ref, value_ref, out_ref,
    xbuf, wbuf, pbuf, rbuf, kbuf, vbuf, cosine, sine, qbuf, fresh, obuf, abuf,
    x_local, x_send, x_recv, w_local, w_send, w_recv, kv_sem, r_send, r_recv, o_local, o_send, o_recv,
):
    chunks = wkv_ref.shape[1] // (2 * key_ref.shape[3])
    steps, batch, _ = hidden_ref.shape
    size = key_ref.shape[3]
    depth = wq_ref.shape[0]
    span = 2 * depth
    rows = steps * batch
    half_len = key_ref.shape[2]
    blocks = (group + 2) // 2
    wide = blocks * size
    dp, sec = lax.axis_index("dp"), lax.axis_index("sec")
    core = sec % 2
    dp_other = 1 - dp
    sec_far = (sec + 2) % 4
    sec_pair = sec + 1 - 2 * core
    near = ({"dp": dp, "sec": sec}, {"dp": dp_other, "sec": sec}, {"dp": dp, "sec": sec_far}, {"dp": dp_other, "sec": sec_far})
    pair = {"dp": dp, "sec": sec_pair}
    cross = {"dp": dp, "sec": (sec_pair + 2) % 4}
    odd = lax.axis_index("tp") % 2
    above = {"tp": lax.axis_index("tp") + 1 - 2 * odd}
    chips = (dp * 2 + sec // 2, dp_other * 2 + sec // 2, dp * 2 + sec_far // 2, dp_other * 2 + sec_far // 2)

    def weight_parts(chunk):
        first = chunk * group * size
        return (
            (2 * chunk, 0, wide, wq_ref, first),
            (2 * chunk + 1, 0, group * size - wide, wq_ref, first + wide),
            (2 * chunk + 1, group * size - wide, 2 * size, wkv_ref, chunk * 2 * size),
        )

    own_rows = pl.ds(pl.multiple_of(core * depth, depth), depth)

    def weight_refs(part):
        piece, start, width, source, column = part
        return (
            source.at[:, pl.ds(column, width)],
            wbuf.at[piece, own_rows, pl.ds(start, width)],
        )

    def hidden_slice(relation):
        return hidden_ref.at[:, :, pl.ds(pl.multiple_of(chips[relation] * span, span), span)]

    local_copies = {}
    x_own = pltpu.make_async_copy(hidden_slice(0), xbuf.at[0], x_local)
    x_own.start()
    for chunk in range(chunks):
        for index, part in enumerate(weight_parts(chunk)):
            source, target = weight_refs(part)
            copy = pltpu.make_async_copy(source, target, w_local.at[chunk, index])
            copy.start()
            local_copies[chunk, index] = copy

    barrier = pltpu.get_barrier_semaphore()
    for peer in near[1:] + (pair, cross, above):
        pl.semaphore_signal(barrier, inc=1, device_id=peer, device_id_type=pl.DeviceIdType.MESH)
    pl.semaphore_wait(barrier, 6)

    def deliver(source, target, index, device):
        return pltpu.make_async_remote_copy(
            src_ref=source, dst_ref=target, send_sem=x_send.at[index], recv_sem=x_recv.at[index],
            device_id=device, device_id_type=pl.DeviceIdType.MESH,
        )

    half_steps = steps // 2
    most = pl.ds(odd, steps - 1)
    x_copies = []
    for step in range(half_steps):
        where = odd * half_steps + step
        x_copies.append(deliver(hidden_slice(3).at[where], xbuf.at[3, where], step, near[3]))
    for relation in (1, 2):
        x_copies.append(
            deliver(
                hidden_slice(relation).at[most], xbuf.at[relation, most], half_steps + relation - 1, near[relation]
            )
        )
    for copy in x_copies:
        copy.start()
    w_copies = {}
    for chunk in range(chunks):
        for index, part in enumerate(weight_parts(chunk)):
            source, target = weight_refs(part)
            copy = pltpu.make_async_remote_copy(
                src_ref=source, dst_ref=target,
                send_sem=w_send.at[chunk, index], recv_sem=w_recv.at[chunk, index],
                device_id=pair, device_id_type=pl.DeviceIdType.MESH,
            )
            copy.start()
            w_copies[chunk, index] = copy
    kv_copies = []
    for chunk in range(chunks):
        slots = pl.ds(2 * chunk, 2)
        for index, (source, target) in enumerate(((key_ref, kbuf), (value_ref, vbuf))):
            copy = pltpu.make_async_copy(source.at[:, slots], target.at[chunk], kv_sem.at[chunk, index])
            copy.start()
            kv_copies.append(copy)

    row = lax.broadcasted_iota(jnp.int32, (rows, size), 0)
    lane = lax.broadcasted_iota(jnp.int32, (rows, size), 1)
    place = row // batch
    for index in range(batch):
        place = place + jnp.where(row % batch == index, end_ref[index], 0)
    angle = place.astype(jnp.float32) * freq_ref[...]
    cosine[...] = jnp.cos(angle)
    sine[...] = jnp.where(lane < size // 2, -jnp.sin(angle), jnp.sin(angle))

    def rotated(vector):
        return vector * cosine[...] + pltpu.roll(vector, size // 2, 1) * sine[...]

    def send(piece, message, source, target):
        copy = pltpu.make_async_remote_copy(
            src_ref=source, dst_ref=rbuf.at[piece, message],
            send_sem=r_send.at[piece, message], recv_sem=r_recv.at[piece, message],
            device_id=target, device_id_type=pl.DeviceIdType.MESH,
        )
        copy.start()
        return copy

    tile = 512 if span % 512 == 0 else span

    def multiply(piece, first, count):
        group_rows = pl.ds(first, count)
        for step in range(span // tile):
            deep = pl.ds(step * tile, tile)
            part = jnp.dot(
                xbuf[group_rows, :, :, deep].reshape(count * rows, tile), wbuf[piece, deep, :],
                preferred_element_type=jnp.float32,
            ).reshape(count, rows, wide)
            if step == 0:
                pbuf[piece, group_rows] = part
            else:
                pbuf[piece, group_rows] += part

    messages = {}

    def first_hop(piece, message):
        one = 1 if piece % 2 == 0 else 2
        source = pbuf.at[piece, 3 if message == 0 else one]
        messages[piece, message] = send(piece, message, source, near[one])

    def second_hop(piece):
        two = 2 if piece % 2 == 0 else 1
        messages[piece, 0].wait_recv()
        pbuf[piece, two] += rbuf[piece, 0]
        messages[piece, 2] = send(piece, 2, pbuf.at[piece, two], near[two])

    def await_weights(piece):
        for index in ((0,), (1, 2))[piece % 2]:
            local_copies[piece // 2, index].wait()
            w_copies[piece // 2, index].wait_recv()

    passed = []
    for step in range(half_steps):
        x_copies[step].wait_recv()
        here = xbuf.at[3, odd * half_steps + step]
        passed.append(deliver(here, here, half_steps + 2 + step, above))
        passed[-1].start()
    for step in range(half_steps):
        there = xbuf.at[3, (1 - odd) * half_steps + step]
        deliver(there, there, half_steps + 2 + step, above).wait_recv()
    for piece in range(2):
        await_weights(piece)
        multiply(piece, 3, 1)
        first_hop(piece, 0)
    x_own.wait()
    for relation in (1, 2):
        x_copies[half_steps + relation - 1].wait_recv()
        here = xbuf.at[relation, odd * (steps - 1)]
        passed.append(deliver(here, here, 2 * half_steps + 1 + relation, above))
        passed[-1].start()
    for relation in (1, 2):
        there = xbuf.at[relation, (1 - odd) * (steps - 1)]
        deliver(there, there, 2 * half_steps + 1 + relation, above).wait_recv()
    for piece in range(2):
        multiply(piece, 0, 3)
        first_hop(piece, 1)
    def attend(chunk):
        new = [None, None]
        for half in range(2):
            piece = 2 * chunk + half
            for block in range(blocks):
                cols = pl.ds(block * size, size)
                total = pbuf[piece, 0, :, cols] + rbuf[piece, 1, :, cols] + rbuf[piece, 2, :, cols]
                head = half * blocks + block
                if head == group + 1:
                    new[1] = total.astype(jnp.bfloat16)
                elif head == group:
                    new[0] = rotated(total).astype(jnp.bfloat16)
                else:
                    turned = rotated(total).astype(jnp.bfloat16).astype(jnp.float32)
                    for step in range(steps):
                        qbuf[pl.ds(head * steps + step, batch, stride=group * steps), :] = turned[
                            step * batch : (step + 1) * batch
                        ]
        spare = jnp.zeros((-rows % 128, size), jnp.bfloat16)
        new_keys, new_values = (jnp.concatenate([part, spare], axis=0) for part in new)
        lines = group * steps
        scale = size ** (-0.5)
        query = qbuf[...].astype(jnp.bfloat16)
        contract = (((1,), (1,)), ((), ()))
        scores = lax.dot_general(query, new_keys, contract, preferred_element_type=jnp.float32) * scale
        line = lax.broadcasted_iota(jnp.int32, scores.shape, 0)
        other = lax.broadcasted_iota(jnp.int32, scores.shape, 1)
        live = (line // lines == other % batch) & (other // batch <= line % steps) & (other < rows)
        fresh[...] = jnp.where(live, scores, jnp.float32(-1e30))
        kv_copies[2 * chunk].wait()
        kv_copies[2 * chunk + 1].wait()
        cache_len = 2 * half_len

        def one(index):
            here = pl.ds(pl.multiple_of(index * lines, lines), lines)
            keys = kbuf[chunk, index].reshape(cache_len, size)
            values = vbuf[chunk, index].reshape(cache_len, size)
            position = lax.broadcasted_iota(jnp.int32, (1, cache_len), 1)
            dead = jnp.where(
                (position >= begin_ref[index]) & (position < end_ref[index]), jnp.float32(0.0), jnp.float32(-1e30)
            )
            cached = lax.dot_general(
                qbuf[here, :].astype(jnp.bfloat16), keys, contract, preferred_element_type=jnp.float32
            ) * scale + dead
            extra = fresh[here, :]
            packs = range(0, cache_len, extra.shape[1])
            peak = extra
            for pack in packs:
                peak = jnp.maximum(peak, cached[:, pack : pack + extra.shape[1]])
            peak = jnp.max(peak, axis=1, keepdims=True)
            cached = jnp.exp(cached - peak)
            extra = jnp.exp(extra - peak)
            total = extra
            for pack in packs:
                total = total + cached[:, pack : pack + extra.shape[1]]
            total = jnp.sum(total, axis=1, keepdims=True)
            weighted = jnp.dot(
                cached.astype(jnp.bfloat16), values, preferred_element_type=jnp.float32
            ) + jnp.dot(extra.astype(jnp.bfloat16), new_values, preferred_element_type=jnp.float32)
            obuf[here, :] = weighted / total

        unroll = 8 if batch % 8 == 0 else 1

        def several(outer, carry):
            for inner in range(unroll):
                one(outer * unroll + inner)
            return carry

        lax.fori_loop(0, batch // unroll, several, 0)
        for head in range(group):
            for step in range(steps):
                abuf[chunk, step, :, pl.ds(head * size, size)] = obuf[
                    pl.ds(head * steps + step, batch, stride=lines), :
                ].astype(jnp.bfloat16)

    share = out_ref.shape[2]
    per = 4 // chunks
    out_rows = pl.ds(pl.multiple_of(sec * batch, batch), batch)

    def handoff(target):
        chunk, place = target // per, target % per
        source = abuf.at[chunk, :, :, pl.ds(place * share, share)]
        keep = pltpu.make_async_copy(source, out_ref.at[:, out_rows, :], o_local)
        copy = pltpu.make_async_remote_copy(
            src_ref=source, dst_ref=out_ref.at[:, out_rows, :],
            send_sem=o_send.at[target], recv_sem=o_recv.at[sec],
            device_id={"dp": dp, "sec": target}, device_id_type=pl.DeviceIdType.MESH,
        )
        return keep, copy

    def hand_over(chunk):
        for target in range(chunk * per, (chunk + 1) * per):
            keep, copy = handoff(target)
            pl.when(sec == target)(keep.start)
            pl.when(sec != target)(copy.start)

    for piece in range(2):
        second_hop(piece)
    for chunk in range(chunks):
        if chunk + 1 < chunks:
            for piece in (2 * chunk + 2, 2 * chunk + 3):
                await_weights(piece)
                multiply(piece, 0, 4)
                first_hop(piece, 0)
                first_hop(piece, 1)
            second_hop(2 * chunk + 2)
            second_hop(2 * chunk + 3)
        for piece in (2 * chunk, 2 * chunk + 1):
            messages[piece, 1].wait_recv()
            messages[piece, 2].wait_recv()
        if chunk > 0:
            hand_over(chunk - 1)
        attend(chunk)
    hand_over(chunks - 1)

    for target in range(4):
        keep, copy = handoff(target)
        pl.when(sec == target)(keep.wait)
        pl.when(sec != target)(copy.wait_send)
        arrived = pltpu.make_async_remote_copy(
            src_ref=abuf.at[0, :, :, pl.ds(0, share)],
            dst_ref=out_ref.at[:, pl.ds(target * batch, batch), :],
            send_sem=o_send.at[target], recv_sem=o_recv.at[target],
            device_id={"dp": dp, "sec": target}, device_id_type=pl.DeviceIdType.MESH,
        )
        pl.when(sec != target)(arrived.wait_recv)
    for copy in x_copies + passed + list(w_copies.values()) + list(messages.values()):
        copy.wait_send()


def fused_body(hidden_states, w_query, w_keyval, key_cache, value_cache, cache_begin, cache_end):
    steps, batch, _ = hidden_states.shape
    slots, half_len, size = key_cache.shape[1:]
    depth = w_query.shape[0]
    chunks = slots // 2
    group = w_query.shape[1] // size // chunks
    rows = steps * batch
    wide = (group + 2) // 2 * size
    pieces = 2 * chunks
    share = w_query.shape[1] // 4
    lanes = np.arange(size, dtype=np.float32) % (size // 2)
    freq = np.float32(THETA) ** (-(lanes * np.float32(2.0) / np.float32(size)))
    anywhere = pl.BlockSpec(memory_space=pl.ANY)
    scalars = pl.BlockSpec(memory_space=pltpu.SMEM)
    dma = pltpu.SemaphoreType.DMA
    return pl.pallas_call(
        functools.partial(fused_kernel, group),
        out_shape=jax.ShapeDtypeStruct((steps, 4 * batch, share), jnp.bfloat16),
        in_specs=[pl.BlockSpec(memory_space=pltpu.VMEM), scalars, scalars] + [anywhere] * 5,
        out_specs=anywhere,
        scratch_shapes=[
            pltpu.VMEM((4, steps, batch, 2 * depth), jnp.bfloat16),
            pltpu.VMEM((pieces, 2 * depth, wide), jnp.bfloat16),
            pltpu.VMEM((pieces, 4, rows, wide), jnp.float32),
            pltpu.VMEM((pieces, 3, rows, wide), jnp.float32),
            pltpu.VMEM((chunks, batch, 2, half_len, size), jnp.bfloat16),
            pltpu.VMEM((chunks, batch, 2, half_len, size), jnp.bfloat16),
            pltpu.VMEM((rows, size), jnp.float32),
            pltpu.VMEM((rows, size), jnp.float32),
            pltpu.VMEM((group * rows, size), jnp.float32),
            pltpu.VMEM((group * rows, rows + -rows % 128), jnp.float32),
            pltpu.VMEM((group * rows, size), jnp.float32),
            pltpu.VMEM((chunks, steps, batch, group * size), jnp.bfloat16),
            dma, dma((steps + 4,)), dma((steps + 4,)),
            dma((chunks, 3)), dma((chunks, 3)), dma((chunks, 3)),
            dma((chunks, 2)),
            dma((pieces, 3)), dma((pieces, 3)),
            dma, dma((4,)), dma((4,)),
        ],
        compiler_params=pltpu.CompilerParams(
            collective_id=0, has_side_effects=True, vmem_limit_bytes=56 * 1024 * 1024
        ),
        cost_estimate=pl.CostEstimate(
            flops=2 * 4 * rows * 2 * depth * pieces * wide,
            bytes_accessed=2 * (w_query.size + w_keyval.size + 2 * key_cache.size),
            transcendentals=0,
        ),
    )(freq[None, :], cache_begin, cache_end, hidden_states, w_query, w_keyval, key_cache, value_cache)


def body(sizes, hidden_states, w_query, w_keyval, key_cache, value_cache, cache_begin, cache_end):
    arrays = (hidden_states, w_query, w_keyval, key_cache, value_cache, cache_begin, cache_end)
    slots = key_cache.shape[1]
    if sizes["dp"] == 2 and sizes["sec"] == 4 and sizes["tp"] % 2 == 0 and slots in (2, 4, 8):
        return fused_body(*arrays)
    return general_body(*arrays)


def solution(mesh):
    return jax.shard_map(
        functools.partial(body, mesh.shape),
        mesh=mesh,
        in_specs=(
            P(None, ("dp", "sec"), None),
            P(("dp", "sec"), "tp"),
            P(("dp", "sec"), "tp"),
            P(("dp", "sec"), "tp", None, None),
            P(("dp", "sec"), "tp", None, None),
            P(("dp", "sec")),
            P(("dp", "sec")),
        ),
        out_specs=P(None, "dp", ("tp", "sec")),
        check_vma=False,
    )
```

```python
import functools

import jax
import jax.numpy as jnp
import numpy as np
from jax import lax
from jax.experimental import pallas as pl
from jax.experimental.pallas import tpu as pltpu
from jax.sharding import PartitionSpec as P

THETA = 500000.0


def swapped(value, axis, stride):
    mask = 2**stride
    pairs = [(source, source ^ mask) for source in range(lax.axis_size(axis))]
    return lax.ppermute(value, axis, pairs)


def rotate(vector, positions):
    half = vector.shape[-1] // 2
    freq = THETA ** (-(jnp.arange(half, dtype=jnp.float32) * 2.0 / vector.shape[-1]))
    angle = positions[..., None] * freq
    angle = angle.reshape(positions.shape + (1,) * (vector.ndim - positions.ndim - 1) + (half,))
    cosine = jnp.cos(angle)
    sine = jnp.sin(angle)
    first = vector[..., :half]
    second = vector[..., half:]
    return jnp.concatenate(
        [first * cosine - second * sine, second * cosine + first * sine], axis=-1
    )


def make_accumulate(token_rows, pieces):
    return (
        jnp.dot(token_rows, pieces[0], preferred_element_type=jnp.float32),
        jnp.dot(token_rows, pieces[1], preferred_element_type=jnp.float32),
    )


def partial_attention(query, keys, values, live, score_scale):
    scores = (
        jnp.einsum("sbkgd,bkpd->sbkgp", query, keys, preferred_element_type=jnp.float32)
        * score_scale
    )
    live = jnp.broadcast_to(live, scores.shape)
    masked = jnp.where(live, scores, jnp.float32(-1e30))
    maxima = jnp.max(masked, axis=-1)
    expo = jnp.where(live, jnp.exp(masked - maxima[..., None]), jnp.float32(0.0))
    totals = jnp.sum(expo, axis=-1)
    weighted = jnp.einsum(
        "sbkgp,bkpd->sbkgd", expo.astype(jnp.bfloat16), values, preferred_element_type=jnp.float32
    )
    return (maxima, totals, weighted)


def merge_parts(parts):
    overall = parts[0][0]
    for entry in parts[1:]:
        overall = jnp.maximum(overall, entry[0])
    weighted = jnp.zeros_like(parts[0][2])
    totals = jnp.zeros_like(parts[0][1])
    for entry in parts:
        factor = jnp.exp(entry[0] - overall)
        weighted = weighted + entry[2] * factor[..., None]
        totals = totals + entry[1] * factor
    return weighted / totals[..., None]


def general_body(hidden_states, w_query, w_keyval, key_cache, value_cache, cache_begin, cache_end):
    num_steps, batch_rows, width = hidden_states.shape
    head_size = key_cache.shape[-1]
    query_cols = w_query.shape[1]
    keyval_cols = w_keyval.shape[1]
    local_heads = query_cols // head_size
    slot_count = key_cache.shape[1]
    half_len = key_cache.shape[2]
    score_scale = head_size ** (-0.5)
    sec_count = lax.axis_size("sec")
    sec_index = lax.axis_index("sec")
    sec_group = lax.all_gather(hidden_states, "sec", axis=1, tiled=True)
    shard_rows = w_query.shape[0]
    dp_count = width // (sec_count * shard_rows)
    group_rows = num_steps * batch_rows * sec_count
    grouped = sec_group.reshape(group_rows, dp_count, sec_count, shard_rows)
    chosen = lax.dynamic_slice_in_dim(grouped, sec_index, 1, 2).reshape(
        group_rows, dp_count * shard_rows
    )
    query_all, keyval_all = make_accumulate(
        chosen,
        (
            lax.all_gather(w_query, "dp", axis=0, tiled=True),
            lax.all_gather(w_keyval, "dp", axis=0, tiled=True),
        ),
    )
    query_acc, keyval_acc = (
        lax.psum_scatter(
            query_all.reshape(num_steps, sec_count * batch_rows, query_cols),
            "sec",
            scatter_dimension=1,
            tiled=True,
        ),
        lax.psum_scatter(
            keyval_all.reshape(num_steps, sec_count * batch_rows, keyval_cols),
            "sec",
            scatter_dimension=1,
            tiled=True,
        ),
    )
    query_acc = query_acc.reshape(num_steps * batch_rows, query_cols)
    keyval_acc = keyval_acc.reshape(num_steps * batch_rows, keyval_cols)
    positions = (
        cache_end.astype(jnp.float32)[None, :] + jnp.arange(num_steps, dtype=jnp.float32)[:, None]
    )
    query = rotate(
        query_acc.reshape(num_steps, batch_rows, local_heads, head_size), positions
    ).astype(jnp.bfloat16)
    step_ids = jnp.arange(num_steps, dtype=jnp.int32)
    causal = step_ids[None, :] <= step_ids[:, None]
    if slot_count == 1:
        parity = lax.axis_index("tp") % 2
        own_proj = keyval_acc.reshape(num_steps, batch_rows, head_size)
        own_proj = jnp.where(parity == 0, rotate(own_proj, positions), own_proj).astype(
            jnp.bfloat16
        )
        partner_query, partner_proj = swapped((query, own_proj), "tp", 0)
        new_keys = jnp.where(parity == 0, own_proj, partner_proj)
        new_values = jnp.where(parity == 0, partner_proj, own_proj)
        lower_heads = jnp.where(parity == 0, query, partner_query)
        upper_heads = jnp.where(parity == 0, partner_query, query)
        both_heads = jnp.concatenate([lower_heads, upper_heads], axis=2)[:, :, None]
        cache_pos = parity * half_len + jnp.arange(half_len, dtype=jnp.int32)
        cache_live = (cache_pos[None, :] >= cache_begin[:, None]) & (
            cache_pos[None, :] < cache_end[:, None]
        )
        cache_part = partial_attention(
            both_heads, key_cache, value_cache, cache_live[None, :, None, None, :], score_scale
        )
        mine_start = parity * local_heads
        theirs_start = (1 - parity) * local_heads

        def select_heads(array, start):
            return lax.dynamic_slice_in_dim(array, start, local_heads, 3)

        returned = (
            swapped(select_heads(cache_part[0], theirs_start).astype(jnp.bfloat16), "tp", 0).astype(
                jnp.float32
            ),
            swapped(select_heads(cache_part[1], theirs_start).astype(jnp.bfloat16), "tp", 0).astype(
                jnp.float32
            ),
            swapped(select_heads(cache_part[2], theirs_start).astype(jnp.bfloat16), "tp", 0).astype(
                jnp.float32
            ),
        )
        own_part = (
            select_heads(cache_part[0], mine_start),
            select_heads(cache_part[1], mine_start),
            select_heads(cache_part[2], mine_start),
        )
        fresh_part = partial_attention(
            query[:, :, None],
            jnp.transpose(new_keys, (1, 0, 2))[:, None],
            jnp.transpose(new_values, (1, 0, 2))[:, None],
            causal[:, None, None, None, :],
            score_scale,
        )
        parts = [own_part, returned, fresh_part]
    else:
        local_kv = keyval_cols // (2 * head_size)
        keyval = keyval_acc.reshape(num_steps, batch_rows, local_kv, 2, head_size)
        new_keys = rotate(keyval[:, :, :, 0], positions).astype(jnp.bfloat16)
        new_values = keyval[:, :, :, 1].astype(jnp.bfloat16)
        whole_keys = key_cache.reshape(batch_rows, local_kv, 2 * half_len, head_size)
        whole_values = value_cache.reshape(batch_rows, local_kv, 2 * half_len, head_size)
        grouped_query = query.reshape(
            num_steps, batch_rows, local_kv, local_heads // local_kv, head_size
        )
        cache_pos = jnp.arange(2 * half_len, dtype=jnp.int32)
        cache_live = (cache_pos[None, :] >= cache_begin[:, None]) & (
            cache_pos[None, :] < cache_end[:, None]
        )
        cache_part = partial_attention(
            grouped_query, whole_keys, whole_values, cache_live[None, :, None, None, :], score_scale
        )
        fresh_part = partial_attention(
            grouped_query,
            jnp.transpose(new_keys, (1, 2, 0, 3)),
            jnp.transpose(new_values, (1, 2, 0, 3)),
            causal[:, None, None, None, :],
            score_scale,
        )
        parts = [cache_part, fresh_part]
    attended = (
        merge_parts(parts)
        .astype(jnp.bfloat16)
        .reshape(num_steps, batch_rows, local_heads * head_size)
    )
    return lax.all_to_all(attended, "sec", split_axis=2, concat_axis=1, tiled=True)


def fused_kernel(
    group, freq_ref, begin_ref, end_ref, hidden_ref, wq_ref, wkv_ref, key_ref, value_ref, out_ref,
    xbuf, wbuf, pbuf, rbuf, kbuf, vbuf, cosine, sine, qbuf, fresh, obuf, abuf,
    x_local, x_send, x_recv, w_local, w_send, w_recv, kv_sem, r_send, r_recv, o_local, o_send, o_recv,
):
    chunks = wkv_ref.shape[1] // (2 * key_ref.shape[3])
    steps, batch, _ = hidden_ref.shape
    size = key_ref.shape[3]
    depth = wq_ref.shape[0]
    span = 2 * depth
    rows = steps * batch
    half_len = key_ref.shape[2]
    blocks = (group + 2) // 2
    wide = blocks * size
    dp, sec = lax.axis_index("dp"), lax.axis_index("sec")
    core = sec % 2
    dp_other = 1 - dp
    sec_far = (sec + 2) % 4
    sec_pair = sec + 1 - 2 * core
    near = ({"dp": dp, "sec": sec}, {"dp": dp_other, "sec": sec}, {"dp": dp, "sec": sec_far}, {"dp": dp_other, "sec": sec_far})
    pair = {"dp": dp, "sec": sec_pair}
    cross = {"dp": dp, "sec": (sec_pair + 2) % 4}
    chips = (dp * 2 + sec // 2, dp_other * 2 + sec // 2, dp * 2 + sec_far // 2, dp_other * 2 + sec_far // 2)

    def weight_parts(chunk):
        first = chunk * group * size
        return (
            (2 * chunk, 0, wide, wq_ref, first),
            (2 * chunk + 1, 0, group * size - wide, wq_ref, first + wide),
            (2 * chunk + 1, group * size - wide, 2 * size, wkv_ref, chunk * 2 * size),
        )

    own_rows = pl.ds(pl.multiple_of(core * depth, depth), depth)

    def weight_refs(part):
        piece, start, width, source, column = part
        return (
            source.at[:, pl.ds(column, width)],
            wbuf.at[piece, own_rows, pl.ds(start, width)],
        )

    def hidden_slice(relation):
        return hidden_ref.at[:, :, pl.ds(pl.multiple_of(chips[relation] * span, span), span)]

    local_copies = {}
    x_own = pltpu.make_async_copy(hidden_slice(0), xbuf.at[0], x_local)
    x_own.start()
    for chunk in range(chunks):
        for index, part in enumerate(weight_parts(chunk)):
            source, target = weight_refs(part)
            copy = pltpu.make_async_copy(source, target, w_local.at[chunk, index])
            copy.start()
            local_copies[chunk, index] = copy

    barrier = pltpu.get_barrier_semaphore()
    for peer in near[1:] + (pair, cross):
        pl.semaphore_signal(barrier, inc=1, device_id=peer, device_id_type=pl.DeviceIdType.MESH)
    pl.semaphore_wait(barrier, 5)

    def deliver(source, target, index, device):
        return pltpu.make_async_remote_copy(
            src_ref=source, dst_ref=target, send_sem=x_send.at[index], recv_sem=x_recv.at[index],
            device_id=device, device_id_type=pl.DeviceIdType.MESH,
        )

    x_copies = [
        deliver(hidden_slice(relation), xbuf.at[relation], relation, near[relation]) for relation in (3, 1, 2)
    ]
    for copy in x_copies:
        copy.start()
    w_copies = {}
    for chunk in range(chunks):
        for index, part in enumerate(weight_parts(chunk)):
            source, target = weight_refs(part)
            copy = pltpu.make_async_remote_copy(
                src_ref=source, dst_ref=target,
                send_sem=w_send.at[chunk, index], recv_sem=w_recv.at[chunk, index],
                device_id=pair, device_id_type=pl.DeviceIdType.MESH,
            )
            copy.start()
            w_copies[chunk, index] = copy
    kv_copies = []
    for chunk in range(chunks):
        slots = pl.ds(2 * chunk, 2)
        for index, (source, target) in enumerate(((key_ref, kbuf), (value_ref, vbuf))):
            copy = pltpu.make_async_copy(source.at[:, slots], target.at[chunk], kv_sem.at[chunk, index])
            copy.start()
            kv_copies.append(copy)

    row = lax.broadcasted_iota(jnp.int32, (rows, size), 0)
    lane = lax.broadcasted_iota(jnp.int32, (rows, size), 1)
    place = row // batch
    for index in range(batch):
        place = place + jnp.where(row % batch == index, end_ref[index], 0)
    angle = place.astype(jnp.float32) * freq_ref[...]
    cosine[...] = jnp.cos(angle)
    sine[...] = jnp.where(lane < size // 2, -jnp.sin(angle), jnp.sin(angle))

    def rotated(vector):
        return vector * cosine[...] + pltpu.roll(vector, size // 2, 1) * sine[...]

    def send(piece, message, source, target):
        copy = pltpu.make_async_remote_copy(
            src_ref=source, dst_ref=rbuf.at[piece, message],
            send_sem=r_send.at[piece, message], recv_sem=r_recv.at[piece, message],
            device_id=target, device_id_type=pl.DeviceIdType.MESH,
        )
        copy.start()
        return copy

    tile = 512 if span % 512 == 0 else span

    def multiply(piece, first, count):
        group_rows = pl.ds(first, count)
        for step in range(span // tile):
            deep = pl.ds(step * tile, tile)
            part = jnp.dot(
                xbuf[group_rows, :, :, deep].reshape(count * rows, tile), wbuf[piece, deep, :],
                preferred_element_type=jnp.float32,
            ).reshape(count, rows, wide)
            if step == 0:
                pbuf[piece, group_rows] = part
            else:
                pbuf[piece, group_rows] += part

    messages = {}

    def first_hop(piece, message):
        one = 1 if piece % 2 == 0 else 2
        source = pbuf.at[piece, 3 if message == 0 else one]
        messages[piece, message] = send(piece, message, source, near[one])

    def second_hop(piece):
        two = 2 if piece % 2 == 0 else 1
        messages[piece, 0].wait_recv()
        pbuf[piece, two] += rbuf[piece, 0]
        messages[piece, 2] = send(piece, 2, pbuf.at[piece, two], near[two])

    def await_weights(piece):
        for index in ((0,), (1, 2))[piece % 2]:
            local_copies[piece // 2, index].wait()
            w_copies[piece // 2, index].wait_recv()

    x_copies[0].wait_recv()
    for piece in range(2):
        await_weights(piece)
        multiply(piece, 3, 1)
        first_hop(piece, 0)
    x_own.wait()
    for copy in x_copies[1:]:
        copy.wait_recv()
    for piece in range(2):
        multiply(piece, 0, 3)
        first_hop(piece, 1)
    def attend(chunk):
        new = [None, None]
        for half in range(2):
            piece = 2 * chunk + half
            for block in range(blocks):
                cols = pl.ds(block * size, size)
                total = pbuf[piece, 0, :, cols] + rbuf[piece, 1, :, cols] + rbuf[piece, 2, :, cols]
                head = half * blocks + block
                if head == group + 1:
                    new[1] = total.astype(jnp.bfloat16)
                elif head == group:
                    new[0] = rotated(total).astype(jnp.bfloat16)
                else:
                    turned = rotated(total).astype(jnp.bfloat16).astype(jnp.float32)
                    for step in range(steps):
                        qbuf[pl.ds(head * steps + step, batch, stride=group * steps), :] = turned[
                            step * batch : (step + 1) * batch
                        ]
        spare = jnp.zeros((-rows % 128, size), jnp.bfloat16)
        new_keys, new_values = (jnp.concatenate([part, spare], axis=0) for part in new)
        lines = group * steps
        scale = size ** (-0.5)
        query = qbuf[...].astype(jnp.bfloat16)
        contract = (((1,), (1,)), ((), ()))
        scores = lax.dot_general(query, new_keys, contract, preferred_element_type=jnp.float32) * scale
        line = lax.broadcasted_iota(jnp.int32, scores.shape, 0)
        other = lax.broadcasted_iota(jnp.int32, scores.shape, 1)
        live = (line // lines == other % batch) & (other // batch <= line % steps) & (other < rows)
        fresh[...] = jnp.where(live, scores, jnp.float32(-1e30))
        kv_copies[2 * chunk].wait()
        kv_copies[2 * chunk + 1].wait()
        cache_len = 2 * half_len

        def one(index):
            here = pl.ds(pl.multiple_of(index * lines, lines), lines)
            keys = kbuf[chunk, index].reshape(cache_len, size)
            values = vbuf[chunk, index].reshape(cache_len, size)
            position = lax.broadcasted_iota(jnp.int32, (1, cache_len), 1)
            dead = jnp.where(
                (position >= begin_ref[index]) & (position < end_ref[index]), jnp.float32(0.0), jnp.float32(-1e30)
            )
            cached = lax.dot_general(
                qbuf[here, :].astype(jnp.bfloat16), keys, contract, preferred_element_type=jnp.float32
            ) * scale + dead
            extra = fresh[here, :]
            packs = range(0, cache_len, extra.shape[1])
            peak = extra
            for pack in packs:
                peak = jnp.maximum(peak, cached[:, pack : pack + extra.shape[1]])
            peak = jnp.max(peak, axis=1, keepdims=True)
            cached = jnp.exp(cached - peak)
            extra = jnp.exp(extra - peak)
            total = extra
            for pack in packs:
                total = total + cached[:, pack : pack + extra.shape[1]]
            total = jnp.sum(total, axis=1, keepdims=True)
            weighted = jnp.dot(
                cached.astype(jnp.bfloat16), values, preferred_element_type=jnp.float32
            ) + jnp.dot(extra.astype(jnp.bfloat16), new_values, preferred_element_type=jnp.float32)
            obuf[here, :] = weighted / total

        unroll = 8 if batch % 8 == 0 else 1

        def several(outer, carry):
            for inner in range(unroll):
                one(outer * unroll + inner)
            return carry

        lax.fori_loop(0, batch // unroll, several, 0)
        for head in range(group):
            for step in range(steps):
                abuf[chunk, step, :, pl.ds(head * size, size)] = obuf[
                    pl.ds(head * steps + step, batch, stride=lines), :
                ].astype(jnp.bfloat16)

    share = out_ref.shape[2]
    per = 4 // chunks
    out_rows = pl.ds(pl.multiple_of(sec * batch, batch), batch)

    def handoff(target):
        chunk, place = target // per, target % per
        source = abuf.at[chunk, :, :, pl.ds(place * share, share)]
        keep = pltpu.make_async_copy(source, out_ref.at[:, out_rows, :], o_local)
        copy = pltpu.make_async_remote_copy(
            src_ref=source, dst_ref=out_ref.at[:, out_rows, :],
            send_sem=o_send.at[target], recv_sem=o_recv.at[sec],
            device_id={"dp": dp, "sec": target}, device_id_type=pl.DeviceIdType.MESH,
        )
        return keep, copy

    def hand_over(chunk):
        for target in range(chunk * per, (chunk + 1) * per):
            keep, copy = handoff(target)
            pl.when(sec == target)(keep.start)
            pl.when(sec != target)(copy.start)

    for piece in range(2):
        second_hop(piece)
    for chunk in range(chunks):
        if chunk + 1 < chunks:
            for piece in (2 * chunk + 2, 2 * chunk + 3):
                await_weights(piece)
                multiply(piece, 0, 4)
                first_hop(piece, 0)
                first_hop(piece, 1)
            second_hop(2 * chunk + 2)
            second_hop(2 * chunk + 3)
        for piece in (2 * chunk, 2 * chunk + 1):
            messages[piece, 1].wait_recv()
            messages[piece, 2].wait_recv()
        if chunk > 0:
            hand_over(chunk - 1)
        attend(chunk)
    hand_over(chunks - 1)

    for target in range(4):
        keep, copy = handoff(target)
        pl.when(sec == target)(keep.wait)
        pl.when(sec != target)(copy.wait_send)
        arrived = pltpu.make_async_remote_copy(
            src_ref=abuf.at[0, :, :, pl.ds(0, share)],
            dst_ref=out_ref.at[:, pl.ds(target * batch, batch), :],
            send_sem=o_send.at[target], recv_sem=o_recv.at[target],
            device_id={"dp": dp, "sec": target}, device_id_type=pl.DeviceIdType.MESH,
        )
        pl.when(sec != target)(arrived.wait_recv)
    for copy in x_copies + list(w_copies.values()) + list(messages.values()):
        copy.wait_send()


def fused_body(hidden_states, w_query, w_keyval, key_cache, value_cache, cache_begin, cache_end):
    steps, batch, _ = hidden_states.shape
    slots, half_len, size = key_cache.shape[1:]
    depth = w_query.shape[0]
    chunks = slots // 2
    group = w_query.shape[1] // size // chunks
    rows = steps * batch
    wide = (group + 2) // 2 * size
    pieces = 2 * chunks
    share = w_query.shape[1] // 4
    lanes = np.arange(size, dtype=np.float32) % (size // 2)
    freq = np.float32(THETA) ** (-(lanes * np.float32(2.0) / np.float32(size)))
    anywhere = pl.BlockSpec(memory_space=pl.ANY)
    scalars = pl.BlockSpec(memory_space=pltpu.SMEM)
    dma = pltpu.SemaphoreType.DMA
    return pl.pallas_call(
        functools.partial(fused_kernel, group),
        out_shape=jax.ShapeDtypeStruct((steps, 4 * batch, share), jnp.bfloat16),
        in_specs=[pl.BlockSpec(memory_space=pltpu.VMEM), scalars, scalars] + [anywhere] * 5,
        out_specs=anywhere,
        scratch_shapes=[
            pltpu.VMEM((4, steps, batch, 2 * depth), jnp.bfloat16),
            pltpu.VMEM((pieces, 2 * depth, wide), jnp.bfloat16),
            pltpu.VMEM((pieces, 4, rows, wide), jnp.float32),
            pltpu.VMEM((pieces, 3, rows, wide), jnp.float32),
            pltpu.VMEM((chunks, batch, 2, half_len, size), jnp.bfloat16),
            pltpu.VMEM((chunks, batch, 2, half_len, size), jnp.bfloat16),
            pltpu.VMEM((rows, size), jnp.float32),
            pltpu.VMEM((rows, size), jnp.float32),
            pltpu.VMEM((group * rows, size), jnp.float32),
            pltpu.VMEM((group * rows, rows + -rows % 128), jnp.float32),
            pltpu.VMEM((group * rows, size), jnp.float32),
            pltpu.VMEM((chunks, steps, batch, group * size), jnp.bfloat16),
            dma, dma((4,)), dma((4,)),
            dma((chunks, 3)), dma((chunks, 3)), dma((chunks, 3)),
            dma((chunks, 2)),
            dma((pieces, 3)), dma((pieces, 3)),
            dma, dma((4,)), dma((4,)),
        ],
        compiler_params=pltpu.CompilerParams(
            collective_id=0, has_side_effects=True, vmem_limit_bytes=56 * 1024 * 1024
        ),
        cost_estimate=pl.CostEstimate(
            flops=2 * 4 * rows * 2 * depth * pieces * wide,
            bytes_accessed=2 * (w_query.size + w_keyval.size + 2 * key_cache.size),
            transcendentals=0,
        ),
    )(freq[None, :], cache_begin, cache_end, hidden_states, w_query, w_keyval, key_cache, value_cache)


def body(sizes, hidden_states, w_query, w_keyval, key_cache, value_cache, cache_begin, cache_end):
    arrays = (hidden_states, w_query, w_keyval, key_cache, value_cache, cache_begin, cache_end)
    slots = key_cache.shape[1]
    if sizes["dp"] == 2 and sizes["sec"] == 4 and sizes["tp"] % 2 == 0 and slots in (2, 4, 8):
        return fused_body(*arrays)
    return general_body(*arrays)


def solution(mesh):
    return jax.shard_map(
        functools.partial(body, mesh.shape),
        mesh=mesh,
        in_specs=(
            P(None, ("dp", "sec"), None),
            P(("dp", "sec"), "tp"),
            P(("dp", "sec"), "tp"),
            P(("dp", "sec"), "tp", None, None),
            P(("dp", "sec"), "tp", None, None),
            P(("dp", "sec")),
            P(("dp", "sec")),
        ),
        out_specs=P(None, "dp", ("tp", "sec")),
        check_vma=False,
    )
```
